256 devices in a mesh: row: 8 (over x, core), col: 8 (over z), depth: 4 (over y).
Axes of the slice: x: 4, y: 4, z: 8, core: 2. Of those that a mesh axis runs over, the one named last changes fastest.
Arguments:
- x_blocks: bfloat16 [8, 8, 4, 1, 2, 128, 128], P('row', 'col', 'depth'), may hold values from -6 to 6
- y_blocks: bfloat16 [8, 8, 4, 1, 4, 128, 128], P('row', 'col', 'depth'), may hold values from -0.03125 to 0.03125
- task_left: int32 [8, 8, 4, 8, 8, 16], P('row', 'col', 'depth'), may hold values from 0 to 1
- task_right: int32 [8, 8, 4, 8, 8, 16], P('row', 'col', 'depth'), may hold values from 0 to 3
- colloc_block: int32 [8, 8, 4, 64, 1], P('row', 'col', 'depth'), may hold values from 0 to 3
- live: int32 [8, 8, 4, 64], P('row', 'col', 'depth'), may hold values from 0 to 1
- factors: bfloat16 [8, 8, 4, 64, 1, 2, 3, 8, 128], P('row', 'col', 'depth'), may hold values from 0.099609375 to 1
- cube_anchor: int32 [8, 8, 4, 64, 1, 3], P('row', 'col', 'depth'), may hold values from 0 to 256, as said below
Outputs:
- density: bfloat16 [8, 8, 16, 128, 128], P('row', 'col', 'depth')
- charge: float32 [64, 2048, 2048], P('depth', 'row', 'col')
The draws below stay inside these ranges and needn't reach their ends.
Inputs may be any that keep to these rules, and one draw needn't show every extreme that they name: `cube_anchor`: component 0 of each corner is at most 16; components 1 and 2 are at most 256.
All inputs are finite; a program needn't handle non-finite values.
Results may differ from the reference program's by a relative error of at most 0.0059.
Values may be sent and summed in bfloat16 or wider, within the bound.
A program may use at most 128 MiB of HBM per device.

```python
import jax
import jax.numpy as jnp
from jax import lax

BLK = 128
NA = 2
NB = 4
NC = 16
GROUP = 8
SLOT = 1
CUBE = 8
HALO = 4
BZ = 16
BXY = 256
L = 8
CBLK = 4
PEERS = 64
NZ = 64
NX = 2048
NY = 2048
N_ROW = 8
N_COL = 8
N_DEPTH = 4


def draw_cube_anchor(key, part):
    subkeys = jax.random.split(jax.random.fold_in(key, 17), 3)
    out_shape = (N_ROW, N_COL, N_DEPTH, PEERS, SLOT)
    depth_part = jax.random.randint(subkeys[0], out_shape, 0, BZ + 2 * HALO - CUBE + 1)
    across = jax.random.randint(subkeys[1], out_shape, 0, BXY + 2 * HALO - CUBE + 1)
    along_part = jax.random.randint(subkeys[2], out_shape, 0, BXY + 2 * HALO - CUBE + 1)
    return jnp.stack([depth_part, across, along_part], axis=-1).astype(jnp.int32)


def with_ends(array, stream_key, smallest, largest):
    longest = array.shape.index(max(array.shape))
    spots = []
    for shift in (0, 1):
        where = [jax.random.randint(jax.random.fold_in(stream_key, axis), (), 0, length) for axis, length in enumerate(array.shape)]
        where[longest] = (where[longest] + shift) % array.shape[longest]
        spots.append(tuple(where))
    return array.at[spots[0]].set(smallest).at[spots[1]].set(largest)


def levels(own_key, shape, cuts, smallest, high):
    loudness, own = 1.0, jax.random.fold_in(own_key, 6)
    for position, parts in cuts:
        draws = jnp.exp(jax.random.uniform(jax.random.fold_in(own, position), (parts,), jnp.float32, smallest / len(cuts), high / len(cuts)))
        loudness = loudness * jnp.repeat(draws, shape[position] // parts).reshape([-1 if axis == position else 1 for axis in range(len(shape))])
    return loudness


def normal_values(stream_key, extent, deviation, bound, shards=(), kind=jnp.bfloat16):
    gain = levels(stream_key, extent, shards, -0.22, 0.18) if shards else 1.0
    values = jax.random.normal(stream_key, extent, jnp.float32) * deviation * gain
    return jnp.minimum(jnp.maximum(values, -bound), bound).astype(kind)


def setup_inputs(seed: int = 0) -> dict:
    keys = jax.random.split(jax.random.key(seed), 9)
    x_blocks = normal_values(keys[0], (N_ROW, N_COL, N_DEPTH, L // N_COL, NA, BLK, BLK), 1.0, 6.0, ((0, 8), (1, 8), (2, 4)))
    y_blocks = normal_values(keys[1], (N_ROW, N_COL, N_DEPTH, L // N_ROW, NB, BLK, BLK), (BLK * GROUP * L * N_DEPTH) ** -0.5, 0.03125, ((0, 8), (1, 8), (2, 4)))
    task_left = with_ends(jax.random.randint(keys[2], (N_ROW, N_COL, N_DEPTH, L, GROUP, NC), 0, NA), jax.random.fold_in(keys[2], 1), 0, NA - 1).astype(jnp.int32)
    task_right = with_ends(jax.random.randint(keys[3], (N_ROW, N_COL, N_DEPTH, L, GROUP, NC), 0, NB), jax.random.fold_in(keys[3], 1), 0, NB - 1).astype(jnp.int32)
    colloc_block = with_ends(jax.random.randint(keys[4], (N_ROW, N_COL, N_DEPTH, PEERS, SLOT), 0, CBLK), jax.random.fold_in(keys[4], 1), 0, CBLK - 1).astype(jnp.int32)
    live = with_ends(jax.random.randint(keys[5], (N_ROW, N_COL, N_DEPTH, PEERS), 0, SLOT + 1), jax.random.fold_in(keys[5], 1), 0, SLOT).astype(jnp.int32)
    factors = jnp.clip(0.099609375 + 0.9003906 * jax.random.uniform(keys[6], (N_ROW, N_COL, N_DEPTH, PEERS, SLOT, 2, 3, CUBE, BLK), jnp.float32) ** levels(keys[6], (N_ROW, N_COL, N_DEPTH, PEERS, SLOT, 2, 3, CUBE, BLK), ((0, 8), (1, 8), (2, 4)), -0.2, 0.2), 0.099609375, 1.0).astype(jnp.bfloat16)
    cube_anchor = draw_cube_anchor(jax.random.fold_in(keys[8], 71), 0)
    return {"x_blocks": x_blocks, "y_blocks": y_blocks, "task_left": task_left, "task_right": task_right, "colloc_block": colloc_block, "live": live, "factors": factors, "cube_anchor": cube_anchor}


SCALE = 0.0625


def cube_basis(factor_set):
    depth_part = factor_set[..., 0, :, None, None, :].astype(jnp.float32)
    across = factor_set[..., 1, None, :, None, :].astype(jnp.float32)
    along_part = factor_set[..., 2, None, None, :, :].astype(jnp.float32)
    product = depth_part * across * along_part
    out_shape = product.shape[:-4] + (CUBE * CUBE * CUBE, product.shape[-1])
    return product.reshape(out_shape).astype(jnp.bfloat16)


def reference(x_blocks, y_blocks, task_left, task_right, colloc_block, live, factors, cube_anchor):
    def tile_sum(item_index):
        row_at = item_index // N_COL
        col_at = item_index % N_COL

        def layer_term(running, term_index):
            layer_id = term_index // L
            panel_id = term_index % L
            x_panel = x_blocks[row_at, (panel_id - row_at) % N_COL, layer_id, panel_id // N_COL]
            y_panel = y_blocks[(panel_id - col_at) % N_ROW, col_at, layer_id, panel_id // N_ROW]
            left_blocks = jnp.take(x_panel, task_left[row_at, col_at, layer_id, panel_id], axis=0).astype(jnp.float32)
            right_blocks = jnp.take(y_panel, task_right[row_at, col_at, layer_id, panel_id], axis=0).astype(jnp.float32)
            return running + jnp.einsum('goij,gojk->oik', left_blocks, right_blocks), None

        running, _ = lax.scan(layer_term, jnp.zeros((NC, BLK, BLK), jnp.float32), jnp.arange(N_DEPTH * L, dtype=jnp.int32))
        return running

    sums = lax.map(tile_sum, jnp.arange(N_ROW * N_COL, dtype=jnp.int32))
    density = sums.reshape((N_ROW, N_COL, NC, BLK, BLK)).astype(jnp.bfloat16)

    def device_cubes(item_index):
        row_at = item_index // (N_COL * N_DEPTH)
        col_at = (item_index // N_DEPTH) % N_COL
        layer_id = item_index % N_DEPTH
        own_blocks = lax.dynamic_slice_in_dim(density[row_at, col_at], layer_id * CBLK, CBLK, 0)
        blocks = jnp.take(own_blocks, colloc_block[row_at, col_at, layer_id], axis=0).astype(jnp.float32)
        basis_values = cube_basis(factors[row_at, col_at, layer_id])
        left_basis = basis_values[:, :, 0].astype(jnp.float32)
        right_basis = basis_values[:, :, 1].astype(jnp.float32)
        weighted = jnp.einsum('pqcn,pqmn->pqcm', right_basis, blocks)
        cube_values = SCALE * jnp.sum(left_basis * weighted, axis=-1)
        slot_ids = jnp.arange(SLOT, dtype=jnp.int32)
        is_live = slot_ids[None, :] < live[row_at, col_at, layer_id][:, None]
        return jnp.where(is_live[:, :, None], cube_values, jnp.float32(0.0))

    cube_batch = lax.map(device_cubes, jnp.arange(N_ROW * N_COL * N_DEPTH, dtype=jnp.int32))
    cube_batch = cube_batch.reshape((N_ROW, N_COL, N_DEPTH, PEERS, SLOT, CUBE, CUBE, CUBE))
    source_rows = jnp.arange(N_ROW, dtype=jnp.int32)[:, None, None, None, None]
    source_cols = jnp.arange(N_COL, dtype=jnp.int32)[None, :, None, None, None]
    layer_ids = jnp.arange(N_DEPTH, dtype=jnp.int32)[None, None, :, None, None]
    target = jnp.arange(PEERS, dtype=jnp.int32)[None, None, None, :, None]
    slot_ids = jnp.arange(SLOT, dtype=jnp.int32)[None, None, None, None, :]
    anchor = cube_anchor[target // N_COL, target % N_COL, layer_ids, source_rows * N_COL + source_cols, slot_ids]
    z_start = layer_ids * BZ + anchor[..., 0] - HALO
    x_start = (target // N_COL) * BXY + anchor[..., 1] - HALO
    y_start = (target % N_COL) * BXY + anchor[..., 2] - HALO
    offsets = jnp.arange(CUBE, dtype=jnp.int32)
    z_cells = (z_start[..., None, None, None] + offsets[:, None, None]) % NZ
    x_cells = (x_start[..., None, None, None] + offsets[None, :, None]) % NX
    y_cells = (y_start[..., None, None, None] + offsets[None, None, :]) % NY
    charge_grid = jnp.zeros((NZ, NX, NY), jnp.float32).at[z_cells, x_cells, y_cells].add(cube_batch)
    return density, charge_grid
```

```python
import functools

import jax
import jax.numpy as jnp
from jax import lax
from jax.experimental import pallas as pl
from jax.experimental.pallas import tpu as pltpu
from jax.sharding import PartitionSpec as P

BLK = 128
NA = 2
NB = 4
NC = 16
CUBE = 8
HALO = 4
BZ = 16
BXY = 256
CELLS = CUBE * CUBE * CUBE
SCALE = 0.0625
F32 = jnp.float32
BF16 = jnp.bfloat16
MESH = pl.DeviceIdType.MESH
NT = (((1,), (1,)), ((), ()))


def product_kernel(
    x_ref, y_ref, left_ref, right_ref, block_ref, live_ref, factor_ref, anchor_ref,
    density_ref, own_ref, below_ref, above_ref, near_anchor_ref,
    xg, yg, kmat, rhs, total, part_out, part_in, b0, b1, pairs, cubes, first_in, second_out,
    own_in, below_in, above_in,
    xr_send, xr_recv, xl_send, xl_recv, yr_send, yr_recv, yl_send, yl_recv, ys_send, ys_recv,
    part_send, part_recv, first_send, first_recv, second_send, second_recv, anchor_send, anchor_recv,
):
    nr, nc, nd = lax.axis_size("row"), lax.axis_size("col"), lax.axis_size("depth")
    chips = nr // 2
    r, c, d = lax.axis_index("row"), lax.axis_index("col"), lax.axis_index("depth")
    core = lax.rem(r, 2)
    chip = r // 2
    sibling = r + 1 - 2 * core

    def up(i, j, n):
        return lax.rem(i + j, n)

    def send(src, dst, s, t, row, col, depth):
        copy = pltpu.make_async_remote_copy(
            src_ref=src, dst_ref=dst, send_sem=s, recv_sem=t, device_id=(row, col, depth), device_id_type=MESH
        )
        copy.start()
        return copy

    barrier = pltpu.get_barrier_semaphore()
    greeted = 0
    for j in range(1, nr):
        pl.semaphore_signal(barrier, inc=1, device_id=(up(r, j, nr), c, d), device_id_type=MESH)
        greeted += 1
    for j in range(nc):
        for k in (0, 1, nd - 1):
            if j or k:
                pl.semaphore_signal(barrier, inc=1, device_id=(r, up(c, j, nc), up(d, k, nd)), device_id_type=MESH)
                greeted += 1
    for k in range(2, nd - 1):
        pl.semaphore_signal(barrier, inc=1, device_id=(r, c, up(d, k, nd)), device_id_type=MESH)
        greeted += 1
    pl.semaphore_wait(barrier, greeted)

    copies = []
    right, left = up(c, 1, nc), up(c, nc - 1, nc)
    chip_r, chip_l = up(chip, 1, chips) * 2 + core, up(chip, chips - 1, chips) * 2 + core
    half = nc // 2

    def x_step(h):
        rows_r = pl.ds(0, 256) if h < half else pl.ds(0, 128)
        rows_l = pl.ds(0, 256) if h < half else pl.ds(128, 128)
        src_r, src_l = up(c, nc - (h - 1), nc), up(c, h - 1, nc)
        copies.append(
            send((x_ref if h == 1 else xg.at[src_r]).at[rows_r], xg.at[src_r, rows_r], xr_send.at[h - 1], xr_recv.at[h - 1], r, right, d)
        )
        copies.append(
            send((x_ref if h == 1 else xg.at[src_l]).at[rows_l], xg.at[src_l, rows_l], xl_send.at[h - 1], xl_recv.at[h - 1], r, left, d)
        )

    def x_wait(h):
        rows_r = pl.ds(0, 256) if h < half else pl.ds(0, 128)
        rows_l = pl.ds(0, 256) if h < half else pl.ds(128, 128)
        src_r, src_l = up(c, nc - h, nc), up(c, h, nc)
        pltpu.make_async_copy(xg.at[src_r, rows_r], xg.at[src_r, rows_r], xr_recv.at[h - 1]).wait()
        pltpu.make_async_copy(xg.at[src_l, rows_l], xg.at[src_l, rows_l], xl_recv.at[h - 1]).wait()

    def y_wait(slot, rows, sem):
        pltpu.make_async_copy(yg.at[slot, rows], yg.at[slot, rows], sem).wait()

    def y_share(q):
        slot = up(r, 2 * q, nr)
        copies.append(send(y_ref if q == 0 else yg.at[slot], yg.at[slot], ys_send.at[q], ys_recv.at[q], sibling, c, d))

    whole, lower, upper = pl.ds(0, 512), pl.ds(0, 256), pl.ds(256, 256)
    x_step(1)
    y_share(0)
    copies.append(send(y_ref, yg.at[r], yr_send.at[0], yr_recv.at[0], chip_r, c, d))
    copies.append(send(y_ref, yg.at[r], yl_send.at[0], yl_recv.at[0], chip_l, c, d))
    for i, k in enumerate((1, nd - 1)):
        copies.append(send(anchor_ref, near_anchor_ref.at[i], anchor_send.at[i], anchor_recv.at[i], r, c, up(d, k, nd)))

    npair = NA * NB
    task = left_ref[...] * NB + right_ref[...]
    counts = jnp.concatenate(
        [jnp.sum(jnp.where(task == p, 1.0, 0.0).astype(F32), axis=1) for p in range(npair)], axis=0
    )
    pick_out = (lax.broadcasted_iota(jnp.int32, (256, NC), 0) // 16 == lax.broadcasted_iota(jnp.int32, (256, NC), 1))
    spread = lax.dot_general(pick_out.astype(F32), counts, NT, preferred_element_type=F32)
    npanel = left_ref.shape[0]
    row64 = lax.broadcasted_iota(jnp.int32, (npair * npanel, npair * 16), 0)
    lane64 = lax.broadcasted_iota(jnp.int32, (npair * npanel, npair * 16), 1)
    same = lax.rem(lax.broadcasted_iota(jnp.int32, (256, 128), 0), 16) == lax.rem(
        lax.broadcasted_iota(jnp.int32, (256, 128), 1), 16
    )
    for k in range(npanel):
        pick_in = (row64 == (lane64 // 16) * npanel + k).astype(BF16)
        m = jnp.dot(spread.astype(BF16), pick_in, preferred_element_type=F32)
        m = jnp.where(same, m, 0.0).astype(BF16)
        kmat[k, :, 0:128] = m
        kmat[k, :, 128:256] = m

    pairs[...] = jnp.zeros_like(pairs)

    def basis(lo, hi):
        @pl.loop(lo, hi)
        def _(t):
            for w in range(2):
                k = t * 2 + w
                f = factor_ref[pl.ds(pl.multiple_of(k * 48, 16), 48), :].astype(F32)
                for e, out in ((0, b0), (1, b1)):
                    f0, f1, f2 = (f[24 * e + 8 * i : 24 * e + 8 * i + 8] for i in range(3))
                    for a in range(CUBE):
                        g = f0[a : a + 1] * f1
                        for b in range(0, CUBE, 2):
                            two = jnp.concatenate([g[b : b + 1] * f2, g[b + 1 : b + 2] * f2], axis=0)
                            out[t, a * 64 + b * 8 : a * 64 + b * 8 + 16, w * 128 : w * 128 + 128] = two.astype(BF16)

    def stage_panel(delta):
        for b in range(NB):
            xs = x_ref if delta == 0 else xg.at[up(c, delta, nc)]
            ys = y_ref if delta == 0 else yg.at[up(r, delta, nr)]
            p = jnp.dot(xs[...], ys[b * 128 : b * 128 + 128, :], preferred_element_type=F32)
            high = p.astype(BF16)
            low = (p - high.astype(F32)).astype(BF16)
            for a in range(NA):
                at = (a * NB + b) * 16
                for ch in range(8):
                    rows = slice(a * 128 + ch * 16, a * 128 + ch * 16 + 16)
                    rhs[at : at + 16, ch * 128 : ch * 128 + 128] = high[rows]
                    rhs[128 + at : 128 + at + 16, ch * 128 : ch * 128 + 128] = low[rows]

    def panel(delta):
        stage_panel(delta)
        k = lax.rem(r + c + delta, npanel)
        got = jnp.dot(kmat[k], rhs[...], preferred_element_type=F32)
        if delta == 0:
            total[...] = got
        else:
            total[...] += got

    nslot = factor_ref.shape[0] // 48
    quarter = nslot // 8

    panel(0)
    x_wait(1)
    x_step(2)
    y_wait(up(r, nr - 2, nr), whole, yr_recv.at[0])
    copies.append(
        send(yg.at[up(r, nr - 2, nr), lower], yg.at[up(r, nr - 2, nr), lower], yr_send.at[1], yr_recv.at[1], chip_r, c, d)
    )
    y_wait(up(r, 2, nr), whole, yl_recv.at[0])
    copies.append(send(yg.at[up(r, 2, nr), upper], yg.at[up(r, 2, nr), upper], yl_send.at[1], yl_recv.at[1], chip_l, c, d))
    y_share(chips - 1)
    y_share(1)
    basis(0, quarter)
    x_wait(2)
    x_step(3)
    y_wait(up(r, 4, nr), lower, yr_recv.at[1])
    y_wait(up(r, 4, nr), upper, yl_recv.at[1])
    y_share(2)
    panel(2)
    panel(nr - 2)
    basis(quarter, 2 * quarter)
    x_wait(3)
    x_step(4)
    for q in range(chips):
        y_wait(lax.rem(sibling + 2 * q, nr), whole, ys_recv.at[q])
    for delta in (1, nr - 1, 3, nr - 3):
        panel(delta)
    basis(2 * quarter, 3 * quarter)
    x_wait(4)
    stage_panel(half)
    k = lax.rem(r + c + half, npanel)

    def last(dest):
        rows = pl.ds(pl.multiple_of(dest * 64, 64), 64)
        return total[rows, :] + jnp.dot(kmat[k, rows, :], rhs[...], preferred_element_type=F32)

    for j in (2, 1, 3):
        dest = up(d, j, nd)
        part_out[j - 1] = last(dest).astype(BF16)
        copies.append(send(part_out.at[j - 1], part_in.at[j - 1], part_send.at[j - 1], part_recv.at[j - 1], r, c, dest))
    summed = last(d)
    basis(3 * quarter, 4 * quarter)
    for j in (1, 3, 2):
        pltpu.make_async_copy(part_in.at[j - 1], part_in.at[j - 1], part_recv.at[j - 1]).wait()
        summed = summed + part_in[j - 1].astype(F32)
    density = summed.astype(BF16)
    for o in range(NC // 4):
        for ch in range(8):
            density_ref[o, ch * 16 : ch * 16 + 16, :] = density[o * 16 : o * 16 + 16, ch * 128 : ch * 128 + 128]
    for i in range(4):
        for j in range(4):
            pairs[i * 4 + j, 0:128, 0:128] = density_ref[i]
            pairs[i * 4 + j, 128:256, 128:256] = density_ref[j]

    row16 = lax.broadcasted_iota(jnp.int32, (16, 256), 0)
    side = lax.broadcasted_iota(jnp.int32, (16, 256), 1) // 128
    for j in (2, 1, 3, 0):
        group = up(chip, j, chips)
        base = group * 8

        def two(i, acc):
            t = base + i
            which = block_ref[t * 2] * 4 + block_ref[t * 2 + 1]
            ones = jnp.where(
                row16 == i * 2 + side,
                jnp.where(side == 0, jnp.minimum(live_ref[t * 2], 1), jnp.minimum(live_ref[t * 2 + 1], 1)).astype(F32) * SCALE,
                0.0,
            ).astype(BF16)
            weight = pairs[which]
            new = []
            for q in range(4):
                rows = pl.ds(q * 128, 128)
                v = jnp.dot(b0[t, rows, :], weight, preferred_element_type=F32)
                v = (v * b1[t, rows, :].astype(F32)).astype(BF16)
                new.append(acc[q] + lax.dot_general(ones, v, NT, preferred_element_type=F32))
            return tuple(new)

        acc = lax.fori_loop(0, 8, two, tuple(jnp.zeros((16, 128), F32) for _ in range(4)))
        for q in range(4):
            cubes[j, q] = acc[q]
        for w in range(2):
            owner = group * 2 + w
            if j:
                copies.append(
                    send(cubes.at[j, :, pl.ds(8 * w, 8)], first_in.at[:, pl.ds(pl.multiple_of(r * 8, 8), 8)], first_send.at[2 * j + w], first_recv.at[r], owner, c, d)
                )
    mine = pl.ds(pl.multiple_of(core * 8, 8), 8)
    theirs = pl.ds(pl.multiple_of(8 - core * 8, 8), 8)
    here = pl.ds(pl.multiple_of(r * 8, 8), 8)
    copies.append(send(cubes.at[0, :, theirs], first_in.at[:, here], first_send.at[0], first_recv.at[r], sibling, c, d))
    first_in[:, here, :] = cubes[0, :, mine, :]
    for j in range(1, nr):
        src = up(r, j, nr)
        rows = first_in.at[:, pl.ds(pl.multiple_of(src * 8, 8), 8)]
        pltpu.make_async_copy(rows, rows, first_recv.at[src]).wait()

    for s in range(nc):
        got = [first_in[q, pl.ds(s, 8, stride=8), :] for q in range(4)]
        for h in range(2):
            second_out[s, h] = jnp.concatenate(got[2 * h : 2 * h + 2], axis=0).astype(BF16)
    for j in [*range(1, nc), 0]:
        s = up(c, j, nc)
        copies.append(send(second_out.at[s, 1], below_in.at[c], second_send.at[1, j], second_recv.at[1, c], r, s, up(d, 1, nd)))
        copies.append(send(second_out.at[s, 0], above_in.at[c], second_send.at[2, j], second_recv.at[2, c], r, s, up(d, nd - 1, nd)))
        if j:
            copies.append(send(second_out.at[s], own_in.at[c], second_send.at[0, j], second_recv.at[0, c], r, s, d))
    own_ref[c] = second_out[c]
    for j in range(nc):
        s = up(c, j, nc)
        if j:
            pltpu.make_async_copy(own_in.at[s], own_in.at[s], second_recv.at[0, s]).wait()
            own_ref[s] = own_in[s]
        pltpu.make_async_copy(below_in.at[s], below_in.at[s], second_recv.at[1, s]).wait()
        below_ref[s] = below_in[s]
        pltpu.make_async_copy(above_in.at[s], above_in.at[s], second_recv.at[2, s]).wait()
        above_ref[s] = above_in[s]
    for i in range(2):
        pltpu.make_async_copy(near_anchor_ref.at[i], near_anchor_ref.at[i], anchor_recv.at[i]).wait()
    for copy in copies:
        copy.wait_send()


def product(x, y, left, right, block, live, factor, anchor, nr, nc):
    vmem = pl.BlockSpec(memory_space=pltpu.VMEM)
    smem = pl.BlockSpec(memory_space=pltpu.SMEM)
    hbm = pl.BlockSpec(memory_space=pl.ANY)
    dma = pltpu.SemaphoreType.DMA
    slots = block.shape[0]
    return pl.pallas_call(
        product_kernel,
        out_shape=(
            jax.ShapeDtypeStruct((NC // 4, BLK, BLK), BF16),
            jax.ShapeDtypeStruct((nc, 2, 16, 128), BF16),
            jax.ShapeDtypeStruct((nc, 16, 128), BF16),
            jax.ShapeDtypeStruct((nc, 16, 128), BF16),
            jax.ShapeDtypeStruct((2, *anchor.shape), jnp.int32),
        ),
        in_specs=[vmem, vmem, vmem, vmem, smem, smem, vmem, hbm],
        out_specs=(vmem, vmem, vmem, vmem, hbm),
        scratch_shapes=[
            pltpu.VMEM((nc, 256, 128), BF16),
            pltpu.VMEM((nr, 512, 128), BF16),
            pltpu.VMEM((8, 256, 256), BF16),
            pltpu.VMEM((256, 1024), BF16),
            pltpu.VMEM((256, 1024), F32),
            pltpu.VMEM((3, 64, 1024), BF16),
            pltpu.VMEM((3, 64, 1024), BF16),
            pltpu.VMEM((slots // 2, CELLS, 256), BF16),
            pltpu.VMEM((slots // 2, CELLS, 256), BF16),
            pltpu.VMEM((16, 256, 256), BF16),
            pltpu.VMEM((4, 4, 16, 128), F32),
            pltpu.VMEM((4, nr * 8, 128), F32),
            pltpu.VMEM((nc, 2, 16, 128), BF16),
            pltpu.VMEM((nc, 2, 16, 128), BF16),
            pltpu.VMEM((nc, 16, 128), BF16),
            pltpu.VMEM((nc, 16, 128), BF16),
            dma((4,)), dma((4,)), dma((4,)), dma((4,)),
            dma((2,)), dma((2,)), dma((2,)), dma((2,)), dma((4,)), dma((4,)),
            dma((3,)), dma((3,)), dma((8,)), dma((8,)), dma((3, 8)), dma((3, 8)), dma((2,)), dma((2,)),
        ],
        compiler_params=pltpu.CompilerParams(collective_id=0, has_side_effects=True, vmem_limit_bytes=56 * 1024 * 1024),
        name="product_and_cubes",
    )(x, y, left, right, block, live, factor, anchor)


def extended(x, sides, width):
    for axis, dim in sides:
        peers, length = (lax.axis_size(axis), x.shape[dim])
        up = [(i, (i + 1) % peers) for i in range(peers)]
        down = [(j, i) for i, j in up]
        last = lax.slice_in_dim(x, length - width, length, axis=dim)
        first = lax.slice_in_dim(x, 0, width, axis=dim)
        before = lax.ppermute(last, axis, up)
        after = lax.ppermute(first, axis, down)
        x = jnp.concatenate([before, x, after], axis=dim)
    return x


def fold_rims(grown_brick, along_dim, inner_len, rim_width):
    extent = grown_brick.shape[along_dim]
    centre = lax.slice_in_dim(grown_brick, 2 * rim_width, 2 * rim_width + inner_len, axis=along_dim)
    lower_rim = lax.slice_in_dim(grown_brick, 0, rim_width, axis=along_dim)
    upper_rim = lax.slice_in_dim(grown_brick, extent - rim_width, extent, axis=along_dim)
    pad_shape = list(lower_rim.shape)
    pad_shape[along_dim] = inner_len - rim_width
    filler = jnp.zeros(tuple(pad_shape), jnp.float32)
    return (
        centre
        + jnp.concatenate([lower_rim, filler], axis=along_dim)
        + jnp.concatenate([filler, upper_rim], axis=along_dim)
    )


def place_cubes(cube_values, corner, nz, nxy):
    offsets = jnp.arange(CUBE, dtype=jnp.int32)
    z_cells = jnp.arange(nz, dtype=jnp.int32)
    xy_cells = jnp.arange(nxy, dtype=jnp.int32)
    pick_z, pick_x, pick_y = (
        (cells[None, :, None] == corner[:, i][:, None, None] + offsets[None, None, :]).astype(jnp.float32)
        for i, cells in enumerate((z_cells, xy_cells, xy_cells))
    )
    along_y = jnp.einsum("kabt,kyt->kaby", cube_values, pick_y, precision=lax.Precision.HIGHEST)
    along_z = jnp.einsum("kza,kaby->zkby", pick_z, along_y, precision=lax.Precision.HIGHEST)
    return jnp.einsum("zkby,kxb->zxy", along_z, pick_x, precision=lax.Precision.HIGHEST)


def local(x_blocks, y_blocks, task_left, task_right, colloc_block, live, factors, cube_anchor):
    nr, nc = lax.axis_size("row"), lax.axis_size("col")
    density, own, below, above, near = product(
        x_blocks.reshape(NA * BLK, BLK),
        y_blocks.reshape(NB * BLK, BLK),
        task_left[0, 0, 0],
        task_right[0, 0, 0],
        colloc_block.reshape(-1),
        live.reshape(-1),
        factors.reshape(-1, BLK),
        cube_anchor[0, 0, 0],
        nr, nc,
    )
    zero = jnp.zeros((64, 256), F32)
    own = own.astype(F32).reshape(nc, 2, 2, 8, 128).transpose(3, 0, 1, 2, 4).reshape(64, 512)
    below = below.astype(F32).reshape(nc, 2, 8, 128).transpose(2, 0, 1, 3).reshape(64, 256)
    above = above.astype(F32).reshape(nc, 2, 8, 128).transpose(2, 0, 1, 3).reshape(64, 256)
    values = jnp.concatenate([own, jnp.concatenate([zero, below], 1), jnp.concatenate([above, zero], 1)], 0)
    corner = jnp.concatenate([cube_anchor.reshape(-1, 3), near[0].reshape(-1, 3), near[1].reshape(-1, 3)], 0)
    shift = jnp.concatenate([jnp.full((64,), -4), jnp.full((64,), -20), jnp.full((64,), 12)]).astype(jnp.int32)
    corner = corner.at[:, 0].add(shift)
    brick = place_cubes(values.reshape(-1, CUBE, CUBE, CUBE), corner, BZ, BXY + 2 * HALO)
    grown_brick = extended(brick, (("row", 1), ("col", 2)), HALO)
    charge = fold_rims(grown_brick, 1, BXY, HALO)
    charge = fold_rims(charge, 2, BXY, HALO)
    return (density[None, None], charge)


def solution(mesh):
    placed = tuple(P("row", "col", "depth", *(None,) * n) for n in (4, 4, 3, 3, 2, 1, 6, 3))
    return jax.shard_map(
        local,
        mesh=mesh,
        in_specs=placed,
        out_specs=(P("row", "col", "depth", None, None), P("depth", "row", "col")),
        check_vma=False,
    )
```

```python
import functools

import jax
import jax.numpy as jnp
from jax import lax
from jax.experimental import pallas as pl
from jax.experimental.pallas import tpu as pltpu
from jax.sharding import PartitionSpec as P

BLK = 128
NA = 2
NB = 4
NC = 16
CUBE = 8
HALO = 4
BZ = 16
BXY = 256
CELLS = CUBE * CUBE * CUBE
SCALE = 0.0625
F32 = jnp.float32
BF16 = jnp.bfloat16
MESH = pl.DeviceIdType.MESH
NT = (((1,), (1,)), ((), ()))


def product_kernel(
    x_ref, y_ref, left_ref, right_ref, block_ref, live_ref, factor_ref, anchor_ref,
    density_ref, own_ref, below_ref, above_ref, near_anchor_ref,
    xg, yg, kmat, rhs, total, part_out, part_in, b0, b1, pairs, cubes, first_in, second_out,
    own_in, below_in, above_in,
    xr_send, xr_recv, xl_send, xl_recv, yr_send, yr_recv, yl_send, yl_recv, ys_send, ys_recv,
    part_send, part_recv, first_send, first_recv, second_send, second_recv, anchor_send, anchor_recv,
):
    nr, nc, nd = lax.axis_size("row"), lax.axis_size("col"), lax.axis_size("depth")
    chips = nr // 2
    r, c, d = lax.axis_index("row"), lax.axis_index("col"), lax.axis_index("depth")
    core = lax.rem(r, 2)
    chip = r // 2
    sibling = r + 1 - 2 * core

    def up(i, j, n):
        return lax.rem(i + j, n)

    def send(src, dst, s, t, row, col, depth):
        copy = pltpu.make_async_remote_copy(
            src_ref=src, dst_ref=dst, send_sem=s, recv_sem=t, device_id=(row, col, depth), device_id_type=MESH
        )
        copy.start()
        return copy

    barrier = pltpu.get_barrier_semaphore()
    greeted = 0
    for j in range(1, nr):
        pl.semaphore_signal(barrier, inc=1, device_id=(up(r, j, nr), c, d), device_id_type=MESH)
        greeted += 1
    for j in range(nc):
        for k in (0, 1, nd - 1):
            if j or k:
                pl.semaphore_signal(barrier, inc=1, device_id=(r, up(c, j, nc), up(d, k, nd)), device_id_type=MESH)
                greeted += 1
    for k in range(2, nd - 1):
        pl.semaphore_signal(barrier, inc=1, device_id=(r, c, up(d, k, nd)), device_id_type=MESH)
        greeted += 1
    pl.semaphore_wait(barrier, greeted)

    copies = []
    right, left = up(c, 1, nc), up(c, nc - 1, nc)
    chip_r, chip_l = up(chip, 1, chips) * 2 + core, up(chip, chips - 1, chips) * 2 + core
    half = nc // 2

    def x_step(h):
        rows_r = pl.ds(0, 256) if h < half else pl.ds(0, 128)
        rows_l = pl.ds(0, 256) if h < half else pl.ds(128, 128)
        src_r, src_l = up(c, nc - (h - 1), nc), up(c, h - 1, nc)
        copies.append(
            send((x_ref if h == 1 else xg.at[src_r]).at[rows_r], xg.at[src_r, rows_r], xr_send.at[h - 1], xr_recv.at[h - 1], r, right, d)
        )
        copies.append(
            send((x_ref if h == 1 else xg.at[src_l]).at[rows_l], xg.at[src_l, rows_l], xl_send.at[h - 1], xl_recv.at[h - 1], r, left, d)
        )

    def x_wait(h):
        rows_r = pl.ds(0, 256) if h < half else pl.ds(0, 128)
        rows_l = pl.ds(0, 256) if h < half else pl.ds(128, 128)
        src_r, src_l = up(c, nc - h, nc), up(c, h, nc)
        pltpu.make_async_copy(xg.at[src_r, rows_r], xg.at[src_r, rows_r], xr_recv.at[h - 1]).wait()
        pltpu.make_async_copy(xg.at[src_l, rows_l], xg.at[src_l, rows_l], xl_recv.at[h - 1]).wait()

    def y_wait(slot, rows, sem):
        pltpu.make_async_copy(yg.at[slot, rows], yg.at[slot, rows], sem).wait()

    def y_share(q):
        slot = up(r, 2 * q, nr)
        copies.append(send(y_ref if q == 0 else yg.at[slot], yg.at[slot], ys_send.at[q], ys_recv.at[q], sibling, c, d))

    whole, lower, upper = pl.ds(0, 512), pl.ds(0, 256), pl.ds(256, 256)
    x_step(1)
    y_share(0)
    copies.append(send(y_ref, yg.at[r], yr_send.at[0], yr_recv.at[0], chip_r, c, d))
    copies.append(send(y_ref, yg.at[r], yl_send.at[0], yl_recv.at[0], chip_l, c, d))
    for i, k in enumerate((1, nd - 1)):
        copies.append(send(anchor_ref, near_anchor_ref.at[i], anchor_send.at[i], anchor_recv.at[i], r, c, up(d, k, nd)))

    npair = NA * NB
    task = left_ref[...] * NB + right_ref[...]
    counts = jnp.concatenate(
        [jnp.sum(jnp.where(task == p, 1.0, 0.0).astype(F32), axis=1) for p in range(npair)], axis=0
    )
    pick_out = (lax.broadcasted_iota(jnp.int32, (256, NC), 0) // 16 == lax.broadcasted_iota(jnp.int32, (256, NC), 1))
    spread = lax.dot_general(pick_out.astype(F32), counts, NT, preferred_element_type=F32)
    npanel = left_ref.shape[0]
    row64 = lax.broadcasted_iota(jnp.int32, (npair * npanel, npair * 16), 0)
    lane64 = lax.broadcasted_iota(jnp.int32, (npair * npanel, npair * 16), 1)
    same = lax.rem(lax.broadcasted_iota(jnp.int32, (256, 128), 0), 16) == lax.rem(
        lax.broadcasted_iota(jnp.int32, (256, 128), 1), 16
    )
    for k in range(npanel):
        pick_in = (row64 == (lane64 // 16) * npanel + k).astype(BF16)
        m = jnp.dot(spread.astype(BF16), pick_in, preferred_element_type=F32)
        m = jnp.where(same, m, 0.0).astype(BF16)
        kmat[k, :, 0:128] = m
        kmat[k, :, 128:256] = m

    pairs[...] = jnp.zeros_like(pairs)

    def basis(lo, hi):
        @pl.loop(lo, hi)
        def _(t):
            for w in range(2):
                k = t * 2 + w
                f = factor_ref[pl.ds(pl.multiple_of(k * 48, 16), 48), :].astype(F32)
                for e, out in ((0, b0), (1, b1)):
                    f0, f1, f2 = (f[24 * e + 8 * i : 24 * e + 8 * i + 8] for i in range(3))
                    for a in range(CUBE):
                        g = f0[a : a + 1] * f1
                        for b in range(0, CUBE, 2):
                            two = jnp.concatenate([g[b : b + 1] * f2, g[b + 1 : b + 2] * f2], axis=0)
                            out[t, a * 64 + b * 8 : a * 64 + b * 8 + 16, w * 128 : w * 128 + 128] = two.astype(BF16)

    def stage_panel(delta):
        for b in range(NB):
            xs = x_ref if delta == 0 else xg.at[up(c, delta, nc)]
            ys = y_ref if delta == 0 else yg.at[up(r, delta, nr)]
            p = jnp.dot(xs[...], ys[b * 128 : b * 128 + 128, :], preferred_element_type=F32)
            high = p.astype(BF16)
            low = (p - high.astype(F32)).astype(BF16)
            for a in range(NA):
                at = (a * NB + b) * 16
                for ch in range(8):
                    rows = slice(a * 128 + ch * 16, a * 128 + ch * 16 + 16)
                    rhs[at : at + 16, ch * 128 : ch * 128 + 128] = high[rows]
                    rhs[128 + at : 128 + at + 16, ch * 128 : ch * 128 + 128] = low[rows]

    def panel(delta):
        stage_panel(delta)
        k = lax.rem(r + c + delta, npanel)
        got = jnp.dot(kmat[k], rhs[...], preferred_element_type=F32)
        if delta == 0:
            total[...] = got
        else:
            total[...] += got

    nslot = factor_ref.shape[0] // 48
    quarter = nslot // 8

    panel(0)
    x_wait(1)
    x_step(2)
    y_wait(up(r, nr - 2, nr), whole, yr_recv.at[0])
    copies.append(
        send(yg.at[up(r, nr - 2, nr), lower], yg.at[up(r, nr - 2, nr), lower], yr_send.at[1], yr_recv.at[1], chip_r, c, d)
    )
    y_wait(up(r, 2, nr), whole, yl_recv.at[0])
    copies.append(send(yg.at[up(r, 2, nr), upper], yg.at[up(r, 2, nr), upper], yl_send.at[1], yl_recv.at[1], chip_l, c, d))
    y_share(chips - 1)
    y_share(1)
    basis(0, quarter)
    x_wait(2)
    x_step(3)
    y_wait(up(r, 4, nr), lower, yr_recv.at[1])
    y_wait(up(r, 4, nr), upper, yl_recv.at[1])
    y_share(2)
    panel(2)
    panel(nr - 2)
    basis(quarter, 2 * quarter)
    x_wait(3)
    x_step(4)
    for q in range(chips):
        y_wait(lax.rem(sibling + 2 * q, nr), whole, ys_recv.at[q])
    for delta in (1, nr - 1, 3, nr - 3):
        panel(delta)
    basis(2 * quarter, 3 * quarter)
    x_wait(4)
    stage_panel(half)
    k = lax.rem(r + c + half, npanel)

    def last(dest):
        rows = pl.ds(pl.multiple_of(dest * 64, 64), 64)
        return total[rows, :] + jnp.dot(kmat[k, rows, :], rhs[...], preferred_element_type=F32)

    for j in (2, 1, 3):
        dest = up(d, j, nd)
        part_out[j - 1] = last(dest).astype(BF16)
        copies.append(send(part_out.at[j - 1], part_in.at[j - 1], part_send.at[j - 1], part_recv.at[j - 1], r, c, dest))
    summed = last(d)
    basis(3 * quarter, 4 * quarter)
    for j in (1, 3, 2):
        pltpu.make_async_copy(part_in.at[j - 1], part_in.at[j - 1], part_recv.at[j - 1]).wait()
        summed = summed + part_in[j - 1].astype(F32)
    density = summed.astype(BF16)
    for o in range(NC // 4):
        for ch in range(8):
            density_ref[o, ch * 16 : ch * 16 + 16, :] = density[o * 16 : o * 16 + 16, ch * 128 : ch * 128 + 128]
    for i in range(4):
        for j in range(4):
            pairs[i * 4 + j, 0:128, 0:128] = density_ref[i]
            pairs[i * 4 + j, 128:256, 128:256] = density_ref[j]

    row16 = lax.broadcasted_iota(jnp.int32, (16, 256), 0)
    side = lax.broadcasted_iota(jnp.int32, (16, 256), 1) // 128
    for j in (2, 1, 3, 0):
        group = up(chip, j, chips)
        base = group * 8

        def two(i, acc):
            t = base + i
            which = block_ref[t * 2] * 4 + block_ref[t * 2 + 1]
            ones = jnp.where(
                row16 == i * 2 + side,
                jnp.where(side == 0, jnp.minimum(live_ref[t * 2], 1), jnp.minimum(live_ref[t * 2 + 1], 1)).astype(F32) * SCALE,
                0.0,
            ).astype(BF16)
            weight = pairs[which]
            new = []
            for q in range(4):
                rows = pl.ds(q * 128, 128)
                v = jnp.dot(b0[t, rows, :], weight, preferred_element_type=F32)
                v = (v * b1[t, rows, :].astype(F32)).astype(BF16)
                new.append(acc[q] + lax.dot_general(ones, v, NT, preferred_element_type=F32))
            return tuple(new)

        acc = lax.fori_loop(0, 8, two, tuple(jnp.zeros((16, 128), F32) for _ in range(4)))
        for q in range(4):
            cubes[j, q] = acc[q]
        for w in range(2):
            owner = group * 2 + w
            if j:
                copies.append(
                    send(cubes.at[j, :, pl.ds(8 * w, 8)], first_in.at[:, pl.ds(pl.multiple_of(r * 8, 8), 8)], first_send.at[2 * j + w], first_recv.at[r], owner, c, d)
                )
    mine = pl.ds(pl.multiple_of(core * 8, 8), 8)
    theirs = pl.ds(pl.multiple_of(8 - core * 8, 8), 8)
    here = pl.ds(pl.multiple_of(r * 8, 8), 8)
    copies.append(send(cubes.at[0, :, theirs], first_in.at[:, here], first_send.at[0], first_recv.at[r], sibling, c, d))
    first_in[:, here, :] = cubes[0, :, mine, :]
    for j in range(1, nr):
        src = up(r, j, nr)
        rows = first_in.at[:, pl.ds(pl.multiple_of(src * 8, 8), 8)]
        pltpu.make_async_copy(rows, rows, first_recv.at[src]).wait()

    for s in range(nc):
        got = [first_in[q, pl.ds(s, 8, stride=8), :] for q in range(4)]
        for h in range(2):
            second_out[s, h] = jnp.concatenate(got[2 * h : 2 * h + 2], axis=0).astype(BF16)
    for j in [*range(1, nc), 0]:
        s = up(c, j, nc)
        copies.append(send(second_out.at[s, 1], below_in.at[c], second_send.at[1, j], second_recv.at[1, c], r, s, up(d, 1, nd)))
        copies.append(send(second_out.at[s, 0], above_in.at[c], second_send.at[2, j], second_recv.at[2, c], r, s, up(d, nd - 1, nd)))
        if j:
            copies.append(send(second_out.at[s], own_in.at[c], second_send.at[0, j], second_recv.at[0, c], r, s, d))
    own_ref[c] = second_out[c]
    for j in range(nc):
        s = up(c, j, nc)
        if j:
            pltpu.make_async_copy(own_in.at[s], own_in.at[s], second_recv.at[0, s]).wait()
            own_ref[s] = own_in[s]
        pltpu.make_async_copy(below_in.at[s], below_in.at[s], second_recv.at[1, s]).wait()
        below_ref[s] = below_in[s]
        pltpu.make_async_copy(above_in.at[s], above_in.at[s], second_recv.at[2, s]).wait()
        above_ref[s] = above_in[s]
    for i in range(2):
        pltpu.make_async_copy(near_anchor_ref.at[i], near_anchor_ref.at[i], anchor_recv.at[i]).wait()
    for copy in copies:
        copy.wait_send()


def product(x, y, left, right, block, live, factor, anchor, nr, nc):
    vmem = pl.BlockSpec(memory_space=pltpu.VMEM)
    smem = pl.BlockSpec(memory_space=pltpu.SMEM)
    hbm = pl.BlockSpec(memory_space=pl.ANY)
    dma = pltpu.SemaphoreType.DMA
    slots = block.shape[0]
    return pl.pallas_call(
        product_kernel,
        out_shape=(
            jax.ShapeDtypeStruct((NC // 4, BLK, BLK), BF16),
            jax.ShapeDtypeStruct((nc, 2, 16, 128), BF16),
            jax.ShapeDtypeStruct((nc, 16, 128), BF16),
            jax.ShapeDtypeStruct((nc, 16, 128), BF16),
            jax.ShapeDtypeStruct((2, *anchor.shape), jnp.int32),
        ),
        in_specs=[vmem, vmem, vmem, vmem, smem, smem, vmem, hbm],
        out_specs=(vmem, vmem, vmem, vmem, hbm),
        scratch_shapes=[
            pltpu.VMEM((nc, 256, 128), BF16),
            pltpu.VMEM((nr, 512, 128), BF16),
            pltpu.VMEM((8, 256, 256), BF16),
            pltpu.VMEM((256, 1024), BF16),
            pltpu.VMEM((256, 1024), F32),
            pltpu.VMEM((3, 64, 1024), BF16),
            pltpu.VMEM((3, 64, 1024), BF16),
            pltpu.VMEM((slots // 2, CELLS, 256), BF16),
            pltpu.VMEM((slots // 2, CELLS, 256), BF16),
            pltpu.VMEM((16, 256, 256), BF16),
            pltpu.VMEM((4, 4, 16, 128), F32),
            pltpu.VMEM((4, nr * 8, 128), F32),
            pltpu.VMEM((nc, 2, 16, 128), BF16),
            pltpu.VMEM((nc, 2, 16, 128), BF16),
            pltpu.VMEM((nc, 16, 128), BF16),
            pltpu.VMEM((nc, 16, 128), BF16),
            dma((4,)), dma((4,)), dma((4,)), dma((4,)),
            dma((2,)), dma((2,)), dma((2,)), dma((2,)), dma((4,)), dma((4,)),
            dma((3,)), dma((3,)), dma((8,)), dma((8,)), dma((3, 8)), dma((3, 8)), dma((2,)), dma((2,)),
        ],
        compiler_params=pltpu.CompilerParams(collective_id=0, has_side_effects=True, vmem_limit_bytes=56 * 1024 * 1024),
        name="product_and_cubes",
    )(x, y, left, right, block, live, factor, anchor)


ROWS = BXY + 32


def spread_tiles(own_ref, below_ref, above_ref, tiles):
    lane = lax.broadcasted_iota(jnp.int32, (8, 128), 1)
    here = lax.rem(lane // 8, 8) == lax.broadcasted_iota(jnp.int32, (8, 128), 0)
    src = lax.broadcasted_iota(jnp.int32, (128, 256), 0)
    dst = lax.broadcasted_iota(jnp.int32, (128, 256), 1)
    fold = ((src // 64 == dst // 128) & (lax.rem(src, 8) == lax.rem(dst, 8))).astype(BF16)

    @pl.loop(0, own_ref.shape[0])
    def _(s):
        for i in range(4):
            got = (own_ref[s, i] if i < 2 else (below_ref, above_ref)[i - 2][s]).astype(F32)
            wide = jnp.concatenate([jnp.where(here, got[j : j + 1], 0.0) for j in range(16)], axis=0)
            out = jnp.dot(wide.astype(BF16), fold, preferred_element_type=F32)
            for q in range(2):
                for r in range(8):
                    for w in range(2):
                        tiles[i, q * 2 + w, r, s] = out[(q * 8 + r) * 8 : (q * 8 + r) * 8 + 8, w * 128 : w * 128 + 128]


def each_cube(anchor_ref, near_ref, visit):
    @pl.loop(0, anchor_ref.shape[2])
    def _(k):
        visit([(a // 4, a % 4, a - 4) for a in range(8)], k, anchor_ref[0, 0, k], anchor_ref[1, 0, k], anchor_ref[2, 0, k])

        @pl.when(near_ref[0, 0, 0, k] > BZ - HALO)
        def _():
            visit([(2, w, w - BZ) for w in range(4)], k, near_ref[0, 0, 0, k], near_ref[0, 1, 0, k], near_ref[0, 2, 0, k])

        @pl.when(near_ref[1, 0, 0, k] < HALO)
        def _():
            visit([(3, w, w - HALO + BZ) for w in range(4)], k, near_ref[1, 0, 0, k], near_ref[1, 1, 0, k], near_ref[1, 2, 0, k])


def plane(z):
    return jnp.where((z >= 0) & (z < BZ), z, BZ)


def add_cube(out, tiles, parts, k, oz, oy, row):
    y = oy - HALO
    lane = lax.broadcasted_iota(jnp.int32, (8, 128), 1)
    shift = lax.rem(y + 8, 8)
    turned = [pltpu.roll(tiles[i, w, k // 8, lax.rem(k, 8)], shift, 1) for i, w, _ in parts]

    def into(h):
        t = lane + h * 128 - y
        inside = (t >= 0) & (t < 8)
        at = [(h, plane(oz + dz), pl.ds(row, 8)) for _, _, dz in parts]
        old = [out[i] for i in at]
        new = [o + jnp.where(inside, u, 0.0) for o, u in zip(old, turned)]
        for i, v in zip(at, new):
            out[i] = v

    first = jnp.maximum(y, 0) // 128
    last = jnp.minimum(y + 7, BXY - 1) // 128
    into(first)

    @pl.when(first != last)
    def _():
        into(last)


def rim_kernel(anchor_ref, near_ref, own_ref, below_ref, above_ref, low_ref, high_ref, sides_ref, tiles, low, high, sides):
    low[...] = jnp.zeros_like(low)
    high[...] = jnp.zeros_like(high)
    sides[...] = jnp.zeros_like(sides)
    spread_tiles(own_ref, below_ref, above_ref, tiles)
    lane = lax.broadcasted_iota(jnp.int32, (8, 128), 1)

    def visit(parts, k, oz, ox, oy):
        @pl.when(ox < HALO)
        def _():
            add_cube(low, tiles, parts, k, oz, oy, ox + 4)

        @pl.when(ox > BXY - HALO)
        def _():
            add_cube(high, tiles, parts, k, oz, oy, ox - HALO - (BXY - 8))

        @pl.when((oy < HALO) | (oy > BXY - HALO))
        def _():
            for i, w, dz in parts:
                z = oz + dz
                start = jnp.where(oy < HALO, z * 4, 64 + z * 4)
                base = start + jnp.where(oy < HALO, oy, oy - (BXY + HALO))
                u = pltpu.roll(tiles[i, w, k // 8, lax.rem(k, 8)], lax.rem(base + 128, 8), 1)
                t = lane - base
                inside = (t >= 0) & (t < 8) & (lane >= start) & (lane < start + 4) & (z >= 0) & (z < BZ)
                rows = pl.ds(ox + 12, 8)
                sides[rows, :] += jnp.where(inside, u, 0.0)

    each_cube(anchor_ref, near_ref, visit)
    for z in range(BZ):
        low_ref[z] = jnp.concatenate([low[0, z, 0:8], low[1, z, 0:8]], axis=0).astype(BF16)
        high_ref[z] = jnp.concatenate([high[0, z, 8:16], high[1, z, 8:16]], axis=0).astype(BF16)
    sides_ref[...] = sides[...].astype(BF16)


def exchange_kernel(low_ref, high_ref, sides_ref, low_out, high_out, sides_out, low_in, high_in, sides_in, send_sem, recv_sem):
    nr, nc = lax.axis_size("row"), lax.axis_size("col")
    r, c, d = lax.axis_index("row"), lax.axis_index("col"), lax.axis_index("depth")
    barrier = pltpu.get_barrier_semaphore()
    for i in (nr - 1, 0, 1):
        for j in (nc - 1, 0, 1):
            if i or j:
                to = (lax.rem(r + i, nr), lax.rem(c + j, nc), d)
                pl.semaphore_signal(barrier, inc=1, device_id=to, device_id_type=MESH)
    pl.semaphore_wait(barrier, 8)
    first, middle, last = pl.ds(0, 16), pl.ds(16, BXY), pl.ds(16 + BXY, 16)
    plan = [
        (0, nc - 1, sides_ref.at[middle], sides_in.at[1, middle]),
        (0, 1, sides_ref.at[middle], sides_in.at[0, middle]),
        (nr - 1, 0, low_ref, low_in),
        (1, 0, high_ref, high_in),
        (nr - 1, nc - 1, sides_ref.at[first], sides_in.at[1, last]),
        (nr - 1, 1, sides_ref.at[first], sides_in.at[0, last]),
        (1, nc - 1, sides_ref.at[last], sides_in.at[1, first]),
        (1, 1, sides_ref.at[last], sides_in.at[0, first]),
    ]
    copies = []
    for n, (i, j, src, dst) in enumerate(plan):
        copy = pltpu.make_async_remote_copy(
            src_ref=src, dst_ref=dst, send_sem=send_sem.at[n], recv_sem=recv_sem.at[n],
            device_id=(lax.rem(r + i, nr), lax.rem(c + j, nc), d), device_id_type=MESH,
        )
        copy.start()
        copies.append(copy)
    for copy in copies:
        copy.wait()
    low_out[...] = low_in[...]
    high_out[...] = high_in[...]
    lane = lax.broadcasted_iota(jnp.int32, (BXY, 128), 1)
    sides = jnp.where(lane < 64, sides_in[1, middle, :].astype(F32), sides_in[0, middle, :].astype(F32))
    sides_out[...] = sides
    for at, rows in ((first, pl.ds(0, 8)), (last, pl.ds(BXY - 8, 8))):
        got = jnp.where(
            lax.broadcasted_iota(jnp.int32, (16, 128), 1) < 64, sides_in[1, at, :].astype(F32), sides_in[0, at, :].astype(F32)
        )
        sides_out[rows, :] += got[0:8] if at is first else got[8:16]


def brick_kernel(anchor_ref, near_ref, own_ref, below_ref, above_ref, low_ref, high_ref, sides_ref, density_ref, density_out, charge_ref, tiles, brick, sems):
    copy = pltpu.make_async_copy(density_ref, density_out, sems.at[2])
    copy.start()
    src = lax.broadcasted_iota(jnp.int32, (128, 256), 0)
    dst = lax.broadcasted_iota(jnp.int32, (128, 256), 1)
    sides = sides_ref[...].astype(BF16)

    @pl.loop(0, BZ)
    def _(z):
        unfold = (((dst < 4) & (src == 64 + z * 4 + dst)) | ((dst >= BXY - 4) & (src == z * 4 + dst - (BXY - 4)))).astype(BF16)
        out = jnp.dot(sides, unfold, preferred_element_type=F32)
        for h in range(2):
            brick[h, z, 16 : 16 + BXY, :] = out[:, h * 128 : h * 128 + 128]
            brick[h, z, 16:24, :] += high_ref[z].astype(F32)[8 * h : 8 * h + 8]
            brick[h, z, 8 + BXY : 16 + BXY, :] += low_ref[z].astype(F32)[8 * h : 8 * h + 8]

    spread_tiles(own_ref, below_ref, above_ref, tiles)
    each_cube(anchor_ref, near_ref, lambda parts, k, oz, ox, oy: add_cube(brick, tiles, parts, k, oz, oy, ox + 12))
    copies = [
        pltpu.make_async_copy(brick.at[h, pl.ds(0, BZ), pl.ds(16, BXY)], charge_ref.at[:, :, pl.ds(h * 128, 128)], sems.at[h])
        for h in range(2)
    ]
    for x in copies:
        x.start()
    for x in copies:
        x.wait()
    copy.wait()


def local(x_blocks, y_blocks, task_left, task_right, colloc_block, live, factors, cube_anchor):
    nr, nc = lax.axis_size("row"), lax.axis_size("col")
    anchor = cube_anchor[0, 0, 0, :, 0, :].T.reshape(3, 1, -1)
    density, own, below, above, near = product(
        x_blocks.reshape(NA * BLK, BLK),
        y_blocks.reshape(NB * BLK, BLK),
        task_left[0, 0, 0],
        task_right[0, 0, 0],
        colloc_block.reshape(-1),
        live.reshape(-1),
        factors.reshape(-1, BLK),
        anchor,
        nr, nc,
    )
    vmem = pl.BlockSpec(memory_space=pltpu.VMEM)
    smem = pl.BlockSpec(memory_space=pltpu.SMEM)
    hbm = pl.BlockSpec(memory_space=pl.ANY)
    dma = pltpu.SemaphoreType.DMA
    tiles = pltpu.VMEM((4, 4, 8, nc, 8, 128), F32)
    params = functools.partial(pltpu.CompilerParams, vmem_limit_bytes=48 * 1024 * 1024)
    faces = (jax.ShapeDtypeStruct((BZ, 16, 128), BF16),) * 2
    low, high, sides = pl.pallas_call(
        rim_kernel,
        out_shape=(*faces, jax.ShapeDtypeStruct((ROWS, 128), BF16)),
        in_specs=[smem, smem, vmem, vmem, vmem],
        out_specs=(vmem, vmem, vmem),
        scratch_shapes=[
            tiles,
            pltpu.VMEM((2, BZ + 1, 16, 128), F32),
            pltpu.VMEM((2, BZ + 1, 16, 128), F32),
            pltpu.VMEM((ROWS, 128), F32),
        ],
        compiler_params=params(),
        name="rims",
    )(anchor, near, own, below, above)
    low, high, sides = pl.pallas_call(
        exchange_kernel,
        out_shape=(*faces, jax.ShapeDtypeStruct((BXY, 128), F32)),
        in_specs=[vmem, vmem, vmem],
        out_specs=(vmem, vmem, vmem),
        scratch_shapes=[
            pltpu.VMEM((BZ, 16, 128), BF16),
            pltpu.VMEM((BZ, 16, 128), BF16),
            pltpu.VMEM((2, ROWS, 128), BF16),
            dma((8,)),
            dma((8,)),
        ],
        compiler_params=params(collective_id=1, has_side_effects=True),
        name="rim_exchange",
    )(low, high, sides)
    density, charge = pl.pallas_call(
        brick_kernel,
        out_shape=(
            jax.ShapeDtypeStruct(density.shape, BF16),
            jax.ShapeDtypeStruct((BZ, BXY, BXY), F32),
        ),
        in_specs=[smem, smem, vmem, vmem, vmem, vmem, vmem, vmem, hbm],
        out_specs=(hbm, hbm),
        scratch_shapes=[tiles, pltpu.VMEM((2, BZ + 1, ROWS, 128), F32), dma((3,))],
        compiler_params=params(),
        name="brick",
    )(anchor, near, own, below, above, low, high, sides, density)
    return (density[None, None], charge)


def solution(mesh):
    placed = tuple(P("row", "col", "depth", *(None,) * n) for n in (4, 4, 3, 3, 2, 1, 6, 3))
    return jax.shard_map(
        local,
        mesh=mesh,
        in_specs=placed,
        out_specs=(P("row", "col", "depth", None, None), P("depth", "row", "col")),
        check_vma=False,
    )
```

```python
import functools

import jax
import jax.numpy as jnp
from jax import lax
from jax.experimental import pallas as pl
from jax.experimental.pallas import tpu as pltpu
from jax.sharding import PartitionSpec as P

BLK = 128
NA = 2
NB = 4
NC = 16
CUBE = 8
HALO = 4
BZ = 16
BXY = 256
CELLS = CUBE * CUBE * CUBE
SCALE = 0.0625
F32 = jnp.float32
BF16 = jnp.bfloat16
MESH = pl.DeviceIdType.MESH
NT = (((1,), (1,)), ((), ()))


def product_kernel(
    x_hbm, y_hbm, left_hbm, right_hbm, block_ref, live_ref, factor_hbm, anchor_ref,
    density_ref, own_ref, below_ref, above_ref, near_ref,
    x_ref, y_ref, left_ref, right_ref, factor_ref, near_anchor_ref,
    xg, yg, kmat, rhs, total, part_out, part_in, b0, b1, pairs, cubes, first_in, second_out,
    own_in, below_in, above_in,
    xr_send, xr_recv, xl_send, xl_recv, yr_send, yr_recv, yl_send, yl_recv, ys_send, ys_recv,
    part_send, part_recv, first_send, first_recv, second_send, second_recv, anchor_send, anchor_recv, load_sem,
):
    nr, nc, nd = lax.axis_size("row"), lax.axis_size("col"), lax.axis_size("depth")
    chips = nr // 2
    r, c, d = lax.axis_index("row"), lax.axis_index("col"), lax.axis_index("depth")
    core = lax.rem(r, 2)
    chip = r // 2
    sibling = r + 1 - 2 * core

    def up(i, j, n):
        return lax.rem(i + j, n)

    def send(src, dst, s, t, row, col, depth):
        copy = pltpu.make_async_remote_copy(
            src_ref=src, dst_ref=dst, send_sem=s, recv_sem=t, device_id=(row, col, depth), device_id_type=MESH
        )
        copy.start()
        return copy

    barrier = pltpu.get_barrier_semaphore()
    greeted = 0
    for j in range(1, nr):
        pl.semaphore_signal(barrier, inc=1, device_id=(up(r, j, nr), c, d), device_id_type=MESH)
        greeted += 1
    for j in range(nc):
        for k in (0, 1, nd - 1):
            if j or k:
                pl.semaphore_signal(barrier, inc=1, device_id=(r, up(c, j, nc), up(d, k, nd)), device_id_type=MESH)
                greeted += 1
    for k in range(2, nd - 1):
        pl.semaphore_signal(barrier, inc=1, device_id=(r, c, up(d, k, nd)), device_id_type=MESH)
        greeted += 1
    loads = [pltpu.make_async_copy(a, b, load_sem.at[i]) for i, (a, b) in enumerate(((x_hbm, x_ref), (y_hbm, y_ref), (left_hbm, left_ref), (right_hbm, right_ref), (factor_hbm, factor_ref)))]
    for load in loads:
        load.start()
    loads[0].wait()
    loads[1].wait()
    pl.semaphore_wait(barrier, greeted)

    copies = []
    right, left = up(c, 1, nc), up(c, nc - 1, nc)
    chip_r, chip_l = up(chip, 1, chips) * 2 + core, up(chip, chips - 1, chips) * 2 + core
    half = nc // 2

    def x_step(h):
        rows_r = pl.ds(0, 256) if h < half else pl.ds(0, 128)
        rows_l = pl.ds(0, 256) if h < half else pl.ds(128, 128)
        src_r, src_l = up(c, nc - (h - 1), nc), up(c, h - 1, nc)
        copies.append(
            send((x_ref if h == 1 else xg.at[src_r]).at[rows_r], xg.at[src_r, rows_r], xr_send.at[h - 1], xr_recv.at[h - 1], r, right, d)
        )
        copies.append(
            send((x_ref if h == 1 else xg.at[src_l]).at[rows_l], xg.at[src_l, rows_l], xl_send.at[h - 1], xl_recv.at[h - 1], r, left, d)
        )

    def x_wait(h):
        rows_r = pl.ds(0, 256) if h < half else pl.ds(0, 128)
        rows_l = pl.ds(0, 256) if h < half else pl.ds(128, 128)
        src_r, src_l = up(c, nc - h, nc), up(c, h, nc)
        pltpu.make_async_copy(xg.at[src_r, rows_r], xg.at[src_r, rows_r], xr_recv.at[h - 1]).wait()
        pltpu.make_async_copy(xg.at[src_l, rows_l], xg.at[src_l, rows_l], xl_recv.at[h - 1]).wait()

    def y_wait(slot, rows, sem):
        pltpu.make_async_copy(yg.at[slot, rows], yg.at[slot, rows], sem).wait()

    def y_share(q):
        slot = up(r, 2 * q, nr)
        copies.append(send(y_ref if q == 0 else yg.at[slot], yg.at[slot], ys_send.at[q], ys_recv.at[q], sibling, c, d))

    whole, lower, upper = pl.ds(0, 512), pl.ds(0, 256), pl.ds(256, 256)
    x_step(1)
    y_share(0)
    copies.append(send(y_ref, yg.at[r], yr_send.at[0], yr_recv.at[0], chip_r, c, d))
    copies.append(send(y_ref, yg.at[r], yl_send.at[0], yl_recv.at[0], chip_l, c, d))
    for i, k in enumerate((1, nd - 1)):
        copies.append(send(anchor_ref, near_anchor_ref.at[i], anchor_send.at[i], anchor_recv.at[i], r, c, up(d, k, nd)))

    loads[2].wait()
    loads[3].wait()
    npair = NA * NB
    task = left_ref[...] * NB + right_ref[...]
    counts = jnp.concatenate(
        [jnp.sum(jnp.where(task == p, 1.0, 0.0).astype(F32), axis=1) for p in range(npair)], axis=0
    )
    pick_out = (lax.broadcasted_iota(jnp.int32, (256, NC), 0) // 16 == lax.broadcasted_iota(jnp.int32, (256, NC), 1))
    spread = lax.dot_general(pick_out.astype(F32), counts, NT, preferred_element_type=F32)
    npanel = left_ref.shape[0]
    row64 = lax.broadcasted_iota(jnp.int32, (npair * npanel, npair * 16), 0)
    lane64 = lax.broadcasted_iota(jnp.int32, (npair * npanel, npair * 16), 1)
    same = lax.rem(lax.broadcasted_iota(jnp.int32, (256, 128), 0), 16) == lax.rem(
        lax.broadcasted_iota(jnp.int32, (256, 128), 1), 16
    )
    for k in range(npanel):
        pick_in = (row64 == (lane64 // 16) * npanel + k).astype(BF16)
        m = jnp.dot(spread.astype(BF16), pick_in, preferred_element_type=F32)
        m = jnp.where(same, m, 0.0).astype(BF16)
        kmat[k, :, 0:128] = m
        kmat[k, :, 128:256] = m

    pairs[...] = jnp.zeros_like(pairs)

    def basis(lo, hi):
        @pl.loop(lo, hi)
        def _(t):
            for w in range(2):
                k = t * 2 + w
                f = factor_ref[pl.ds(pl.multiple_of(k * 48, 16), 48), :].astype(F32)
                for e, out in ((0, b0), (1, b1)):
                    f0, f1, f2 = (f[24 * e + 8 * i : 24 * e + 8 * i + 8] for i in range(3))
                    for a in range(CUBE):
                        g = f0[a : a + 1] * f1
                        for b in range(0, CUBE, 2):
                            two = jnp.concatenate([g[b : b + 1] * f2, g[b + 1 : b + 2] * f2], axis=0)
                            out[t, a * 64 + b * 8 : a * 64 + b * 8 + 16, w * 128 : w * 128 + 128] = two.astype(BF16)

    def stage_panel(delta):
        for b in range(NB):
            xs = x_ref if delta == 0 else xg.at[up(c, delta, nc)]
            ys = y_ref if delta == 0 else yg.at[up(r, delta, nr)]
            p = jnp.dot(xs[...], ys[b * 128 : b * 128 + 128, :], preferred_element_type=F32)
            high = p.astype(BF16)
            low = (p - high.astype(F32)).astype(BF16)
            for a in range(NA):
                at = (a * NB + b) * 16
                for ch in range(8):
                    rows = slice(a * 128 + ch * 16, a * 128 + ch * 16 + 16)
                    rhs[at : at + 16, ch * 128 : ch * 128 + 128] = high[rows]
                    rhs[128 + at : 128 + at + 16, ch * 128 : ch * 128 + 128] = low[rows]

    def panel(delta):
        stage_panel(delta)
        k = lax.rem(r + c + delta, npanel)
        got = jnp.dot(kmat[k], rhs[...], preferred_element_type=F32)
        if delta == 0:
            total[...] = got
        else:
            total[...] += got

    nslot = factor_ref.shape[0] // 48
    quarter = nslot // 8

    panel(0)
    loads[4].wait()
    x_wait(1)
    x_step(2)
    y_wait(up(r, nr - 2, nr), whole, yr_recv.at[0])
    copies.append(
        send(yg.at[up(r, nr - 2, nr), lower], yg.at[up(r, nr - 2, nr), lower], yr_send.at[1], yr_recv.at[1], chip_r, c, d)
    )
    y_wait(up(r, 2, nr), whole, yl_recv.at[0])
    copies.append(send(yg.at[up(r, 2, nr), upper], yg.at[up(r, 2, nr), upper], yl_send.at[1], yl_recv.at[1], chip_l, c, d))
    y_share(chips - 1)
    y_share(1)
    basis(0, quarter)
    x_wait(2)
    x_step(3)
    y_wait(up(r, 4, nr), lower, yr_recv.at[1])
    y_wait(up(r, 4, nr), upper, yl_recv.at[1])
    y_share(2)
    panel(2)
    panel(nr - 2)
    x_wait(3)
    x_step(4)
    for q in range(chips):
        y_wait(lax.rem(sibling + 2 * q, nr), whole, ys_recv.at[q])
    for delta in (1, nr - 1, 3, nr - 3):
        panel(delta)
    x_wait(4)
    stage_panel(half)
    k = lax.rem(r + c + half, npanel)

    def last(dest):
        rows = pl.ds(pl.multiple_of(dest * 64, 64), 64)
        return total[rows, :] + jnp.dot(kmat[k, rows, :], rhs[...], preferred_element_type=F32)

    for j in (2, 1, 3):
        dest = up(d, j, nd)
        part_out[j - 1] = last(dest).astype(BF16)
        copies.append(send(part_out.at[j - 1], part_in.at[j - 1], part_send.at[j - 1], part_recv.at[j - 1], r, c, dest))
    summed = last(d)
    basis(quarter, 4 * quarter)
    for j in (1, 3, 2):
        pltpu.make_async_copy(part_in.at[j - 1], part_in.at[j - 1], part_recv.at[j - 1]).wait()
        summed = summed + part_in[j - 1].astype(F32)
    density = summed.astype(BF16)
    for o in range(NC // 4):
        for ch in range(8):
            density_ref[o, ch * 16 : ch * 16 + 16, :] = density[o * 16 : o * 16 + 16, ch * 128 : ch * 128 + 128]
    for i in range(4):
        for j in range(4):
            pairs[i * 4 + j, 0:128, 0:128] = density_ref[i]
            pairs[i * 4 + j, 128:256, 128:256] = density_ref[j]

    row16 = lax.broadcasted_iota(jnp.int32, (16, 256), 0)
    side = lax.broadcasted_iota(jnp.int32, (16, 256), 1) // 128
    for j in (2, 1, 3, 0):
        group = up(chip, j, chips)
        base = group * 8

        def two(i, acc):
            t = base + i
            which = block_ref[t * 2] * 4 + block_ref[t * 2 + 1]
            ones = jnp.where(
                row16 == i * 2 + side,
                jnp.where(side == 0, jnp.minimum(live_ref[t * 2], 1), jnp.minimum(live_ref[t * 2 + 1], 1)).astype(F32) * SCALE,
                0.0,
            ).astype(BF16)
            weight = pairs[which]
            new = []
            for q in range(4):
                rows = pl.ds(q * 128, 128)
                v = jnp.dot(b0[t, rows, :], weight, preferred_element_type=F32)
                v = (v * b1[t, rows, :].astype(F32)).astype(BF16)
                new.append(acc[q] + lax.dot_general(ones, v, NT, preferred_element_type=F32))
            return tuple(new)

        acc = lax.fori_loop(0, 8, two, tuple(jnp.zeros((16, 128), F32) for _ in range(4)), unroll=4)
        for q in range(4):
            cubes[j, q] = acc[q]
        for w in range(2):
            owner = group * 2 + w
            if j:
                copies.append(
                    send(cubes.at[j, :, pl.ds(8 * w, 8)], first_in.at[:, pl.ds(pl.multiple_of(r * 8, 8), 8)], first_send.at[2 * j + w], first_recv.at[r], owner, c, d)
                )
    mine = pl.ds(pl.multiple_of(core * 8, 8), 8)
    theirs = pl.ds(pl.multiple_of(8 - core * 8, 8), 8)
    here = pl.ds(pl.multiple_of(r * 8, 8), 8)
    copies.append(send(cubes.at[0, :, theirs], first_in.at[:, here], first_send.at[0], first_recv.at[r], sibling, c, d))
    first_in[:, here, :] = cubes[0, :, mine, :]
    for j in range(1, nr):
        src = up(r, j, nr)
        rows = first_in.at[:, pl.ds(pl.multiple_of(src * 8, 8), 8)]
        pltpu.make_async_copy(rows, rows, first_recv.at[src]).wait()

    for s in range(nc):
        got = [first_in[q, pl.ds(s, 8, stride=8), :] for q in range(4)]
        for h in range(2):
            second_out[s, h] = jnp.concatenate(got[2 * h : 2 * h + 2], axis=0).astype(BF16)
    for j in [*range(1, nc), 0]:
        s = up(c, j, nc)
        copies.append(send(second_out.at[s, 1], below_in.at[c], second_send.at[1, j], second_recv.at[1, c], r, s, up(d, 1, nd)))
        copies.append(send(second_out.at[s, 0], above_in.at[c], second_send.at[2, j], second_recv.at[2, c], r, s, up(d, nd - 1, nd)))
        if j:
            copies.append(send(second_out.at[s], own_in.at[c], second_send.at[0, j], second_recv.at[0, c], r, s, d))
    own_ref[c] = second_out[c]
    for j in range(nc):
        s = up(c, j, nc)
        if j:
            pltpu.make_async_copy(own_in.at[s], own_in.at[s], second_recv.at[0, s]).wait()
            own_ref[s] = own_in[s]
        pltpu.make_async_copy(below_in.at[s], below_in.at[s], second_recv.at[1, s]).wait()
        below_ref[s] = below_in[s]
        pltpu.make_async_copy(above_in.at[s], above_in.at[s], second_recv.at[2, s]).wait()
        above_ref[s] = above_in[s]
    for i in range(2):
        pltpu.make_async_copy(near_anchor_ref.at[i], near_anchor_ref.at[i], anchor_recv.at[i]).wait()
        near_ref[i + 1] = near_anchor_ref[i]
    near_ref[0] = anchor_ref[...]
    for copy in copies:
        copy.wait_send()


def product(x, y, left, right, block, live, factor, anchor, nr, nc):
    vmem = pl.BlockSpec(memory_space=pltpu.VMEM)
    smem = pl.BlockSpec(memory_space=pltpu.SMEM)
    hbm = pl.BlockSpec(memory_space=pl.ANY)
    dma = pltpu.SemaphoreType.DMA
    slots = block.shape[0]
    return pl.pallas_call(
        product_kernel,
        out_shape=(
            pltpu.VMEM((NC // 4, BLK, BLK), BF16),
            pltpu.VMEM((nc, 2, 16, 128), BF16),
            pltpu.VMEM((nc, 16, 128), BF16),
            pltpu.VMEM((nc, 16, 128), BF16),
            pltpu.VMEM((3, *anchor.shape), jnp.int32),
        ),
        in_specs=[hbm, hbm, hbm, hbm, smem, smem, hbm, vmem],
        out_specs=(vmem,) * 5,
        scratch_shapes=[
            pltpu.VMEM(x.shape, BF16),
            pltpu.VMEM(y.shape, BF16),
            pltpu.VMEM(left.shape, jnp.int32),
            pltpu.VMEM(right.shape, jnp.int32),
            pltpu.VMEM(factor.shape, BF16),
            pltpu.VMEM((2, *anchor.shape), jnp.int32),
            pltpu.VMEM((nc, 256, 128), BF16),
            pltpu.VMEM((nr, 512, 128), BF16),
            pltpu.VMEM((8, 256, 256), BF16),
            pltpu.VMEM((256, 1024), BF16),
            pltpu.VMEM((256, 1024), F32),
            pltpu.VMEM((3, 64, 1024), BF16),
            pltpu.VMEM((3, 64, 1024), BF16),
            pltpu.VMEM((slots // 2, CELLS, 256), BF16),
            pltpu.VMEM((slots // 2, CELLS, 256), BF16),
            pltpu.VMEM((16, 256, 256), BF16),
            pltpu.VMEM((4, 4, 16, 128), F32),
            pltpu.VMEM((4, nr * 8, 128), F32),
            pltpu.VMEM((nc, 2, 16, 128), BF16),
            pltpu.VMEM((nc, 2, 16, 128), BF16),
            pltpu.VMEM((nc, 16, 128), BF16),
            pltpu.VMEM((nc, 16, 128), BF16),
            dma((4,)), dma((4,)), dma((4,)), dma((4,)),
            dma((2,)), dma((2,)), dma((2,)), dma((2,)), dma((4,)), dma((4,)),
            dma((3,)), dma((3,)), dma((8,)), dma((8,)), dma((3, 8)), dma((3, 8)), dma((2,)), dma((2,)), dma((5,)),
        ],
        compiler_params=pltpu.CompilerParams(collective_id=0, has_side_effects=True, vmem_limit_bytes=56 * 1024 * 1024),
        name="product_and_cubes",
    )(x, y, left, right, block, live, factor, anchor)


ROWS = BXY + 32


def spread_tiles(anchor_ref, near_ref, own_ref, below_ref, above_ref, tiles):
    row16 = lax.broadcasted_iota(jnp.int32, (16, 128), 0)
    lane16 = lax.broadcasted_iota(jnp.int32, (16, 128), 1)
    lane = lax.broadcasted_iota(jnp.int32, (8, 128), 1)
    here = lax.rem(lane // 8, 8) == lax.broadcasted_iota(jnp.int32, (8, 128), 0)
    src = lax.broadcasted_iota(jnp.int32, (128, 256), 0)
    dst = lax.broadcasted_iota(jnp.int32, (128, 256), 1)
    fold = ((src // 64 == dst // 128) & (lax.rem(src, 8) == lax.rem(dst, 8))).astype(BF16)

    def turn(corner, s):
        y = jnp.zeros((16, 128), jnp.int32)
        for r in range(8):
            y = jnp.where(lax.rem(row16, 8) == r, corner(r * 8 + s) - HALO, y)
        return lane16 - lax.rem(lane16, 8) + lax.rem(lane16 - y + BXY * 2, 8)

    @pl.loop(0, own_ref.shape[0])
    def _(s):
        index = turn(lambda k: anchor_ref[2, 0, k], s)
        parts = [(own_ref[s, 0], index), (own_ref[s, 1], index)]
        parts.append((below_ref[s], turn(lambda k: near_ref[0, 2, 0, k], s)))
        parts.append((above_ref[s], turn(lambda k: near_ref[1, 2, 0, k], s)))
        for i, (got, index) in enumerate(parts):
            got = got.astype(F32)
            got = jnp.concatenate(
                [jnp.take_along_axis(got[j : j + 8], index[j : j + 8], axis=1) for j in (0, 8)], axis=0
            )
            wide = jnp.concatenate([jnp.where(here, got[j : j + 1], 0.0) for j in range(16)], axis=0)
            out = jnp.dot(wide.astype(BF16), fold, preferred_element_type=F32)
            for q in range(2):
                for r in range(8):
                    for w in range(2):
                        tiles[i, q * 2 + w, r * 8 + s] = out[(q * 8 + r) * 8 : (q * 8 + r) * 8 + 8, w * 128 : w * 128 + 128]


def place_kernel(corner_ref, own_ref, below_ref, above_ref, brick, low_ref, high_ref, sides_ref, tiles, sides):
    anchor_ref, near_ref = corner_ref.at[0], corner_ref.at[pl.ds(1, 2)]
    for h in range(2):

        @pl.loop(0, BZ)
        def _(z):
            brick[h, z, 8 : 24 + BXY, :] = jnp.zeros((16 + BXY, 128), F32)

    sides[...] = jnp.zeros_like(sides)
    spread_tiles(anchor_ref, near_ref, own_ref, below_ref, above_ref, tiles)
    lane = lax.broadcasted_iota(jnp.int32, (8, 128), 1)

    def add(parts, k, oz, ox, oy):
        first = jnp.maximum(oy - HALO, 0) // 128
        rows = pl.ds(ox + 16 - HALO, 8)
        for h in (first, first + 1):
            t = lane + (h * 128 - oy + HALO)
            inside = (t >= 0) & (t < 8)
            at = []
            for _, _, dz in parts:
                z = oz + dz
                at.append((h, jnp.where((z >= 0) & (z < BZ), z, BZ), rows))
            new = [brick[x] + jnp.where(inside, tiles[i, w, k], 0.0) for x, (i, w, _) in zip(at, parts)]
            for x, v in zip(at, new):
                brick[x] = v

        @pl.when((oy < HALO) | (oy > BXY - HALO))
        def _():
            for i, w, dz in parts:
                z = oz + dz
                start = jnp.where(oy < HALO, z * 4, 64 + z * 4)
                base = start + jnp.where(oy < HALO, oy, oy - (BXY + HALO))
                u = pltpu.roll(tiles[i, w, k], lax.rem(base - oy + HALO + 512, 8), 1)
                t = lane - base
                inside = (t >= 0) & (t < 8) & (lane >= start) & (lane < start + 4) & (z >= 0) & (z < BZ)
                sides[rows, :] += jnp.where(inside, u, 0.0)

    @pl.loop(0, anchor_ref.shape[2])
    def _(k):
        add([(a // 4, a % 4, a - 4) for a in range(8)], k, anchor_ref[0, 0, k], anchor_ref[1, 0, k], anchor_ref[2, 0, k])

    @pl.loop(0, anchor_ref.shape[2])
    def _(k):
        @pl.when(near_ref[0, 0, 0, k] > BZ - HALO)
        def _():
            add([(2, w, w - BZ) for w in range(4)], k, near_ref[0, 0, 0, k], near_ref[0, 1, 0, k], near_ref[0, 2, 0, k])

        @pl.when(near_ref[1, 0, 0, k] < HALO)
        def _():
            add([(3, w, w - HALO + BZ) for w in range(4)], k, near_ref[1, 0, 0, k], near_ref[1, 1, 0, k], near_ref[1, 2, 0, k])

    for z in range(BZ):
        low_ref[z] = jnp.concatenate([brick[h, z, 8:16] for h in range(2)], axis=0).astype(BF16)
        high_ref[z] = jnp.concatenate([brick[h, z, 16 + BXY : 24 + BXY] for h in range(2)], axis=0).astype(BF16)
    sides_ref[...] = sides[...].astype(BF16)


def exchange_kernel(low_ref, high_ref, sides_ref, low_out, high_out, sides_out, low_in, high_in, sides_in, send_sem, recv_sem):
    nr, nc = lax.axis_size("row"), lax.axis_size("col")
    r, c, d = lax.axis_index("row"), lax.axis_index("col"), lax.axis_index("depth")
    barrier = pltpu.get_barrier_semaphore()
    for i in (nr - 1, 0, 1):
        for j in (nc - 1, 0, 1):
            if i or j:
                to = (lax.rem(r + i, nr), lax.rem(c + j, nc), d)
                pl.semaphore_signal(barrier, inc=1, device_id=to, device_id_type=MESH)
    pl.semaphore_wait(barrier, 8)
    first, middle, last = pl.ds(0, 16), pl.ds(16, BXY), pl.ds(16 + BXY, 16)
    plan = [
        (0, nc - 1, sides_ref.at[middle], sides_in.at[1, middle]),
        (0, 1, sides_ref.at[middle], sides_in.at[0, middle]),
        (nr - 1, 0, low_ref, low_in),
        (1, 0, high_ref, high_in),
        (nr - 1, nc - 1, sides_ref.at[first], sides_in.at[1, last]),
        (nr - 1, 1, sides_ref.at[first], sides_in.at[0, last]),
        (1, nc - 1, sides_ref.at[last], sides_in.at[1, first]),
        (1, 1, sides_ref.at[last], sides_in.at[0, first]),
    ]
    copies = []
    for n, (i, j, src, dst) in enumerate(plan):
        copy = pltpu.make_async_remote_copy(
            src_ref=src, dst_ref=dst, send_sem=send_sem.at[n], recv_sem=recv_sem.at[n],
            device_id=(lax.rem(r + i, nr), lax.rem(c + j, nc), d), device_id_type=MESH,
        )
        copy.start()
        copies.append(copy)
    for copy in copies:
        copy.wait()
    low_out[...] = low_in[...]
    high_out[...] = high_in[...]
    lane = lax.broadcasted_iota(jnp.int32, (BXY, 128), 1)
    sides = jnp.where(lane < 64, sides_in[1, middle, :].astype(F32), sides_in[0, middle, :].astype(F32))
    sides_out[...] = sides
    for at, rows in ((first, pl.ds(0, 8)), (last, pl.ds(BXY - 8, 8))):
        got = jnp.where(
            lax.broadcasted_iota(jnp.int32, (16, 128), 1) < 64, sides_in[1, at, :].astype(F32), sides_in[0, at, :].astype(F32)
        )
        sides_out[rows, :] += got[0:8] if at is first else got[8:16]


def charge_kernel(brick, low_ref, high_ref, sides_ref, density_ref, density_out, charge_ref, full, sems):
    copies = [pltpu.make_async_copy(density_ref, density_out, sems.at[BZ])]
    copies[0].start()
    src = lax.broadcasted_iota(jnp.int32, (128, 256), 0)
    dst = lax.broadcasted_iota(jnp.int32, (128, 256), 1)
    sides = sides_ref[...].astype(BF16)
    at = jnp.where(dst < 4, 64 + dst, jnp.where(dst >= BXY - 4, dst - (BXY - 4), -BXY))
    for z in range(BZ):
        unfold = (src == at + z * 4).astype(BF16)
        out = jnp.dot(sides, unfold, preferred_element_type=F32)
        for h in range(2):
            lanes = slice(h * 128, h * 128 + 128)
            full[z, :, lanes] = out[:, lanes] + brick[h, z, 16 : 16 + BXY, :]
            full[z, 0:8, lanes] += high_ref[z].astype(F32)[8 * h : 8 * h + 8]
            full[z, BXY - 8 : BXY, lanes] += low_ref[z].astype(F32)[8 * h : 8 * h + 8]
        copies.append(pltpu.make_async_copy(full.at[z], charge_ref.at[z], sems.at[z]))
        copies[-1].start()
    for copy in copies:
        copy.wait()


def place(corner, own, below, above):
    vmem = pl.BlockSpec(memory_space=pltpu.VMEM)
    smem = pl.BlockSpec(memory_space=pltpu.SMEM)
    nk = corner.shape[3]
    faces = (jax.ShapeDtypeStruct((BZ, 16, 128), BF16),) * 2
    return pl.pallas_call(
        place_kernel,
        out_shape=(pltpu.VMEM((3, BZ + 1, ROWS, 128), F32), *faces, jax.ShapeDtypeStruct((ROWS, 128), BF16)),
        in_specs=[smem, vmem, vmem, vmem],
        out_specs=(vmem, vmem, vmem, vmem),
        scratch_shapes=[pltpu.VMEM((4, 4, nk, 8, 128), F32), pltpu.VMEM((ROWS, 128), F32)],
        compiler_params=pltpu.CompilerParams(vmem_limit_bytes=24 * 1024 * 1024),
        name="place",
    )(corner, own, below, above)


def finish(brick, low, high, sides, density):
    vmem = pl.BlockSpec(memory_space=pltpu.VMEM)
    hbm = pl.BlockSpec(memory_space=pl.ANY)
    return pl.pallas_call(
        charge_kernel,
        out_shape=(
            jax.ShapeDtypeStruct(density.shape, BF16),
            jax.ShapeDtypeStruct((BZ, BXY, BXY), F32),
        ),
        in_specs=[vmem, vmem, vmem, vmem, vmem],
        out_specs=(hbm, hbm),
        scratch_shapes=[pltpu.VMEM((BZ, BXY, BXY), F32), pltpu.SemaphoreType.DMA((BZ + 1,))],
        compiler_params=pltpu.CompilerParams(vmem_limit_bytes=24 * 1024 * 1024),
        name="charge",
    )(brick, low, high, sides, density)


def local(x_blocks, y_blocks, task_left, task_right, colloc_block, live, factors, cube_anchor):
    nr, nc = lax.axis_size("row"), lax.axis_size("col")
    anchor = cube_anchor[0, 0, 0].transpose(2, 1, 0)
    density, own, below, above, corner = product(
        x_blocks.reshape(NA * BLK, BLK),
        y_blocks.reshape(NB * BLK, BLK),
        task_left[0, 0, 0],
        task_right[0, 0, 0],
        colloc_block.reshape(-1),
        live.reshape(-1),
        factors.reshape(-1, BLK),
        anchor,
        nr, nc,
    )
    vmem = pl.BlockSpec(memory_space=pltpu.VMEM)
    dma = pltpu.SemaphoreType.DMA
    brick, low, high, sides = place(corner, own, below, above)
    low, high, sides = pl.pallas_call(
        exchange_kernel,
        out_shape=(*(jax.ShapeDtypeStruct((BZ, 16, 128), BF16),) * 2, jax.ShapeDtypeStruct((BXY, 128), F32)),
        in_specs=[vmem, vmem, vmem],
        out_specs=(vmem, vmem, vmem),
        scratch_shapes=[
            pltpu.VMEM((BZ, 16, 128), BF16),
            pltpu.VMEM((BZ, 16, 128), BF16),
            pltpu.VMEM((2, ROWS, 128), BF16),
            dma((8,)),
            dma((8,)),
        ],
        compiler_params=pltpu.CompilerParams(collective_id=1, has_side_effects=True, vmem_limit_bytes=8 * 1024 * 1024),
        name="rim_exchange",
    )(low, high, sides)
    density, charge = finish(brick, low, high, sides, density)
    return (density[None, None], charge)


def solution(mesh):
    placed = tuple(P("row", "col", "depth", *(None,) * n) for n in (4, 4, 3, 3, 2, 1, 6, 3))
    return jax.shard_map(
        local,
        mesh=mesh,
        in_specs=placed,
        out_specs=(P("row", "col", "depth", None, None), P("depth", "row", "col")),
        check_vma=False,
    )
```

```python
import functools

import jax
import jax.numpy as jnp
from jax import lax
from jax.experimental import pallas as pl
from jax.experimental.pallas import tpu as pltpu
from jax.sharding import PartitionSpec as P

BLK = 128
NA = 2
NB = 4
NC = 16
CUBE = 8
HALO = 4
BZ = 16
BXY = 256
CELLS = CUBE * CUBE * CUBE
SCALE = 0.0625
F32 = jnp.float32
BF16 = jnp.bfloat16
MESH = pl.DeviceIdType.MESH
NT = (((1,), (1,)), ((), ()))


def product_kernel(
    x_hbm, y_hbm, left_hbm, right_hbm, block_ref, live_ref, factor_hbm, anchor_ref,
    density_ref, own_ref, below_ref, above_ref, near_ref,
    x_ref, y_ref, left_ref, right_ref, factor_ref, near_anchor_ref,
    xg, yg, kmat, rhs, total, part_out, part_in, b0, b1, pairs, cubes, first_in, second_out,
    own_in, below_in, above_in,
    xr_send, xr_recv, xl_send, xl_recv, yr_send, yr_recv, yl_send, yl_recv, ys_send, ys_recv,
    part_send, part_recv, first_send, first_recv, second_send, second_recv, anchor_send, anchor_recv, load_sem,
):
    nr, nc, nd = lax.axis_size("row"), lax.axis_size("col"), lax.axis_size("depth")
    chips = nr // 2
    r, c, d = lax.axis_index("row"), lax.axis_index("col"), lax.axis_index("depth")
    core = lax.rem(r, 2)
    chip = r // 2
    sibling = r + 1 - 2 * core

    def up(i, j, n):
        return lax.rem(i + j, n)

    def send(src, dst, s, t, row, col, depth):
        copy = pltpu.make_async_remote_copy(
            src_ref=src, dst_ref=dst, send_sem=s, recv_sem=t, device_id=(row, col, depth), device_id_type=MESH
        )
        copy.start()
        return copy

    barrier = pltpu.get_barrier_semaphore()
    greeted = 0
    for j in range(1, nr):
        pl.semaphore_signal(barrier, inc=1, device_id=(up(r, j, nr), c, d), device_id_type=MESH)
        greeted += 1
    for j in range(nc):
        for k in (0, 1, nd - 1):
            if j or k:
                pl.semaphore_signal(barrier, inc=1, device_id=(r, up(c, j, nc), up(d, k, nd)), device_id_type=MESH)
                greeted += 1
    for k in range(2, nd - 1):
        pl.semaphore_signal(barrier, inc=1, device_id=(r, c, up(d, k, nd)), device_id_type=MESH)
        greeted += 1
    loads = [pltpu.make_async_copy(a, b, load_sem.at[i]) for i, (a, b) in enumerate(((x_hbm, x_ref), (y_hbm, y_ref), (left_hbm, left_ref), (right_hbm, right_ref), (factor_hbm, factor_ref)))]
    for load in loads:
        load.start()
    loads[0].wait()
    loads[1].wait()
    pl.semaphore_wait(barrier, greeted)

    copies = []
    right, left = up(c, 1, nc), up(c, nc - 1, nc)
    chip_r, chip_l = up(chip, 1, chips) * 2 + core, up(chip, chips - 1, chips) * 2 + core
    half = nc // 2

    def x_step(h):
        rows_r = pl.ds(0, 256) if h < half else pl.ds(0, 128)
        rows_l = pl.ds(0, 256) if h < half else pl.ds(128, 128)
        src_r, src_l = up(c, nc - (h - 1), nc), up(c, h - 1, nc)
        copies.append(
            send((x_ref if h == 1 else xg.at[src_r]).at[rows_r], xg.at[src_r, rows_r], xr_send.at[h - 1], xr_recv.at[h - 1], r, right, d)
        )
        copies.append(
            send((x_ref if h == 1 else xg.at[src_l]).at[rows_l], xg.at[src_l, rows_l], xl_send.at[h - 1], xl_recv.at[h - 1], r, left, d)
        )

    def x_wait(h):
        rows_r = pl.ds(0, 256) if h < half else pl.ds(0, 128)
        rows_l = pl.ds(0, 256) if h < half else pl.ds(128, 128)
        src_r, src_l = up(c, nc - h, nc), up(c, h, nc)
        pltpu.make_async_copy(xg.at[src_r, rows_r], xg.at[src_r, rows_r], xr_recv.at[h - 1]).wait()
        pltpu.make_async_copy(xg.at[src_l, rows_l], xg.at[src_l, rows_l], xl_recv.at[h - 1]).wait()

    def y_wait(slot, rows, sem):
        pltpu.make_async_copy(yg.at[slot, rows], yg.at[slot, rows], sem).wait()

    def y_share(q):
        slot = up(r, 2 * q, nr)
        copies.append(send(y_ref if q == 0 else yg.at[slot], yg.at[slot], ys_send.at[q], ys_recv.at[q], sibling, c, d))

    whole, lower, upper = pl.ds(0, 512), pl.ds(0, 256), pl.ds(256, 256)
    x_step(1)
    y_share(0)
    copies.append(send(y_ref, yg.at[r], yr_send.at[0], yr_recv.at[0], chip_r, c, d))
    copies.append(send(y_ref, yg.at[r], yl_send.at[0], yl_recv.at[0], chip_l, c, d))
    for i, k in enumerate((1, nd - 1)):
        copies.append(send(anchor_ref, near_anchor_ref.at[i], anchor_send.at[i], anchor_recv.at[i], r, c, up(d, k, nd)))

    loads[2].wait()
    loads[3].wait()
    npair = NA * NB
    task = left_ref[...] * NB + right_ref[...]
    counts = jnp.concatenate(
        [jnp.sum(jnp.where(task == p, 1.0, 0.0).astype(F32), axis=1) for p in range(npair)], axis=0
    )
    pick_out = (lax.broadcasted_iota(jnp.int32, (256, NC), 0) // 16 == lax.broadcasted_iota(jnp.int32, (256, NC), 1))
    spread = lax.dot_general(pick_out.astype(F32), counts, NT, preferred_element_type=F32)
    npanel = left_ref.shape[0]
    row64 = lax.broadcasted_iota(jnp.int32, (npair * npanel, npair * 16), 0)
    lane64 = lax.broadcasted_iota(jnp.int32, (npair * npanel, npair * 16), 1)
    same = lax.rem(lax.broadcasted_iota(jnp.int32, (256, 128), 0), 16) == lax.rem(
        lax.broadcasted_iota(jnp.int32, (256, 128), 1), 16
    )
    for k in range(npanel):
        pick_in = (row64 == (lane64 // 16) * npanel + k).astype(BF16)
        m = jnp.dot(spread.astype(BF16), pick_in, preferred_element_type=F32)
        m = jnp.where(same, m, 0.0).astype(BF16)
        kmat[k, :, 0:128] = m
        kmat[k, :, 128:256] = m

    pairs[...] = jnp.zeros_like(pairs)

    def basis(lo, hi):
        @pl.loop(lo, hi)
        def _(t):
            for w in range(2):
                k = t * 2 + w
                f = factor_ref[pl.ds(pl.multiple_of(k * 48, 16), 48), :].astype(F32)
                for e, out in ((0, b0), (1, b1)):
                    f0, f1, f2 = (f[24 * e + 8 * i : 24 * e + 8 * i + 8] for i in range(3))
                    for a in range(CUBE):
                        g = f0[a : a + 1] * f1
                        for b in range(0, CUBE, 2):
                            two = jnp.concatenate([g[b : b + 1] * f2, g[b + 1 : b + 2] * f2], axis=0)
                            out[t, a * 64 + b * 8 : a * 64 + b * 8 + 16, w * 128 : w * 128 + 128] = two.astype(BF16)

    def stage_panel(delta):
        for b in range(NB):
            xs = x_ref if delta == 0 else xg.at[up(c, delta, nc)]
            ys = y_ref if delta == 0 else yg.at[up(r, delta, nr)]
            p = jnp.dot(xs[...], ys[b * 128 : b * 128 + 128, :], preferred_element_type=F32)
            high = p.astype(BF16)
            low = (p - high.astype(F32)).astype(BF16)
            for a in range(NA):
                at = (a * NB + b) * 16
                for ch in range(8):
                    rows = slice(a * 128 + ch * 16, a * 128 + ch * 16 + 16)
                    rhs[at : at + 16, ch * 128 : ch * 128 + 128] = high[rows]
                    rhs[128 + at : 128 + at + 16, ch * 128 : ch * 128 + 128] = low[rows]

    def panel(delta):
        stage_panel(delta)
        k = lax.rem(r + c + delta, npanel)
        got = jnp.dot(kmat[k], rhs[...], preferred_element_type=F32)
        if delta == 0:
            total[...] = got
        else:
            total[...] += got

    nslot = factor_ref.shape[0] // 48
    quarter = nslot // 8

    panel(0)
    loads[4].wait()
    x_wait(1)
    x_step(2)
    y_wait(up(r, nr - 2, nr), whole, yr_recv.at[0])
    copies.append(
        send(yg.at[up(r, nr - 2, nr), lower], yg.at[up(r, nr - 2, nr), lower], yr_send.at[1], yr_recv.at[1], chip_r, c, d)
    )
    y_wait(up(r, 2, nr), whole, yl_recv.at[0])
    copies.append(send(yg.at[up(r, 2, nr), upper], yg.at[up(r, 2, nr), upper], yl_send.at[1], yl_recv.at[1], chip_l, c, d))
    y_share(chips - 1)
    y_share(1)
    basis(0, quarter)
    x_wait(2)
    x_step(3)
    y_wait(up(r, 4, nr), lower, yr_recv.at[1])
    y_wait(up(r, 4, nr), upper, yl_recv.at[1])
    y_share(2)
    panel(2)
    panel(nr - 2)
    x_wait(3)
    x_step(4)
    for q in range(chips):
        y_wait(lax.rem(sibling + 2 * q, nr), whole, ys_recv.at[q])
    for delta in (1, nr - 1, 3, nr - 3):
        panel(delta)
    x_wait(4)
    stage_panel(half)
    k = lax.rem(r + c + half, npanel)

    def last(dest):
        rows = pl.ds(pl.multiple_of(dest * 64, 64), 64)
        return total[rows, :] + jnp.dot(kmat[k, rows, :], rhs[...], preferred_element_type=F32)

    for j in (2, 1, 3):
        dest = up(d, j, nd)
        part_out[j - 1] = last(dest).astype(BF16)
        copies.append(send(part_out.at[j - 1], part_in.at[j - 1], part_send.at[j - 1], part_recv.at[j - 1], r, c, dest))
    summed = last(d)
    basis(quarter, 4 * quarter)
    for j in (1, 3, 2):
        pltpu.make_async_copy(part_in.at[j - 1], part_in.at[j - 1], part_recv.at[j - 1]).wait()
        summed = summed + part_in[j - 1].astype(F32)
    density = summed.astype(BF16)
    for o in range(NC // 4):
        for ch in range(8):
            density_ref[o, ch * 16 : ch * 16 + 16, :] = density[o * 16 : o * 16 + 16, ch * 128 : ch * 128 + 128]
    for i in range(4):
        for j in range(4):
            pairs[i * 4 + j, 0:128, 0:128] = density_ref[i]
            pairs[i * 4 + j, 128:256, 128:256] = density_ref[j]

    row16 = lax.broadcasted_iota(jnp.int32, (16, 256), 0)
    side = lax.broadcasted_iota(jnp.int32, (16, 256), 1) // 128
    for j in (2, 1, 3, 0):
        group = up(chip, j, chips)
        base = group * 8

        def two(i, acc):
            t = base + i
            which = block_ref[t * 2] * 4 + block_ref[t * 2 + 1]
            ones = jnp.where(
                row16 == i * 2 + side,
                jnp.where(side == 0, jnp.minimum(live_ref[t * 2], 1), jnp.minimum(live_ref[t * 2 + 1], 1)).astype(F32) * SCALE,
                0.0,
            ).astype(BF16)
            weight = pairs[which]
            new = []
            for q in range(4):
                rows = pl.ds(q * 128, 128)
                v = jnp.dot(b0[t, rows, :], weight, preferred_element_type=F32)
                v = (v * b1[t, rows, :].astype(F32)).astype(BF16)
                new.append(acc[q] + lax.dot_general(ones, v, NT, preferred_element_type=F32))
            return tuple(new)

        acc = lax.fori_loop(0, 8, two, tuple(jnp.zeros((16, 128), F32) for _ in range(4)), unroll=4)
        for q in range(4):
            cubes[j, q] = acc[q]
        for w in range(2):
            owner = group * 2 + w
            if j:
                copies.append(
                    send(cubes.at[j, :, pl.ds(8 * w, 8)], first_in.at[:, pl.ds(pl.multiple_of(r * 8, 8), 8)], first_send.at[2 * j + w], first_recv.at[r], owner, c, d)
                )
    mine = pl.ds(pl.multiple_of(core * 8, 8), 8)
    theirs = pl.ds(pl.multiple_of(8 - core * 8, 8), 8)
    here = pl.ds(pl.multiple_of(r * 8, 8), 8)
    copies.append(send(cubes.at[0, :, theirs], first_in.at[:, here], first_send.at[0], first_recv.at[r], sibling, c, d))
    first_in[:, here, :] = cubes[0, :, mine, :]
    for j in range(1, nr):
        src = up(r, j, nr)
        rows = first_in.at[:, pl.ds(pl.multiple_of(src * 8, 8), 8)]
        pltpu.make_async_copy(rows, rows, first_recv.at[src]).wait()

    for s in range(nc):
        got = [first_in[q, pl.ds(s, 8, stride=8), :] for q in range(4)]
        for h in range(2):
            second_out[s, h] = jnp.concatenate(got[2 * h : 2 * h + 2], axis=0).astype(BF16)
    for j in [*range(1, nc), 0]:
        s = up(c, j, nc)
        copies.append(send(second_out.at[s, 1], below_in.at[c], second_send.at[1, j], second_recv.at[1, c], r, s, up(d, 1, nd)))
        copies.append(send(second_out.at[s, 0], above_in.at[c], second_send.at[2, j], second_recv.at[2, c], r, s, up(d, nd - 1, nd)))
        if j:
            copies.append(send(second_out.at[s], own_in.at[c], second_send.at[0, j], second_recv.at[0, c], r, s, d))
    own_ref[c] = second_out[c]
    for j in range(nc):
        s = up(c, j, nc)
        if j:
            pltpu.make_async_copy(own_in.at[s], own_in.at[s], second_recv.at[0, s]).wait()
            own_ref[s] = own_in[s]
        pltpu.make_async_copy(below_in.at[s], below_in.at[s], second_recv.at[1, s]).wait()
        below_ref[s] = below_in[s]
        pltpu.make_async_copy(above_in.at[s], above_in.at[s], second_recv.at[2, s]).wait()
        above_ref[s] = above_in[s]
    for i in range(2):
        pltpu.make_async_copy(near_anchor_ref.at[i], near_anchor_ref.at[i], anchor_recv.at[i]).wait()
        near_ref[i + 1] = near_anchor_ref[i]
    near_ref[0] = anchor_ref[...]
    for copy in copies:
        copy.wait_send()


def product(x, y, left, right, block, live, factor, anchor, nr, nc):
    vmem = pl.BlockSpec(memory_space=pltpu.VMEM)
    smem = pl.BlockSpec(memory_space=pltpu.SMEM)
    hbm = pl.BlockSpec(memory_space=pl.ANY)
    dma = pltpu.SemaphoreType.DMA
    slots = block.shape[0]
    return pl.pallas_call(
        product_kernel,
        out_shape=(
            pltpu.VMEM((NC // 4, BLK, BLK), BF16),
            pltpu.VMEM((nc, 2, 16, 128), BF16),
            pltpu.VMEM((nc, 16, 128), BF16),
            pltpu.VMEM((nc, 16, 128), BF16),
            pltpu.VMEM((3, *anchor.shape), jnp.int32),
        ),
        in_specs=[hbm, hbm, hbm, hbm, smem, smem, hbm, vmem],
        out_specs=(vmem,) * 5,
        scratch_shapes=[
            pltpu.VMEM(x.shape, BF16),
            pltpu.VMEM(y.shape, BF16),
            pltpu.VMEM(left.shape, jnp.int32),
            pltpu.VMEM(right.shape, jnp.int32),
            pltpu.VMEM(factor.shape, BF16),
            pltpu.VMEM((2, *anchor.shape), jnp.int32),
            pltpu.VMEM((nc, 256, 128), BF16),
            pltpu.VMEM((nr, 512, 128), BF16),
            pltpu.VMEM((8, 256, 256), BF16),
            pltpu.VMEM((256, 1024), BF16),
            pltpu.VMEM((256, 1024), F32),
            pltpu.VMEM((3, 64, 1024), BF16),
            pltpu.VMEM((3, 64, 1024), BF16),
            pltpu.VMEM((slots // 2, CELLS, 256), BF16),
            pltpu.VMEM((slots // 2, CELLS, 256), BF16),
            pltpu.VMEM((16, 256, 256), BF16),
            pltpu.VMEM((4, 4, 16, 128), F32),
            pltpu.VMEM((4, nr * 8, 128), F32),
            pltpu.VMEM((nc, 2, 16, 128), BF16),
            pltpu.VMEM((nc, 2, 16, 128), BF16),
            pltpu.VMEM((nc, 16, 128), BF16),
            pltpu.VMEM((nc, 16, 128), BF16),
            dma((4,)), dma((4,)), dma((4,)), dma((4,)),
            dma((2,)), dma((2,)), dma((2,)), dma((2,)), dma((4,)), dma((4,)),
            dma((3,)), dma((3,)), dma((8,)), dma((8,)), dma((3, 8)), dma((3, 8)), dma((2,)), dma((2,)), dma((5,)),
        ],
        compiler_params=pltpu.CompilerParams(collective_id=0, has_side_effects=True, vmem_limit_bytes=56 * 1024 * 1024),
        name="product_and_cubes",
    )(x, y, left, right, block, live, factor, anchor)


ROWS = BXY + 32


def spread_tiles(anchor_ref, near_ref, own_ref, below_ref, above_ref, tiles):
    row16 = lax.broadcasted_iota(jnp.int32, (16, 128), 0)
    lane16 = lax.broadcasted_iota(jnp.int32, (16, 128), 1)
    lane = lax.broadcasted_iota(jnp.int32, (8, 128), 1)
    here = lax.rem(lane // 8, 8) == lax.broadcasted_iota(jnp.int32, (8, 128), 0)
    src = lax.broadcasted_iota(jnp.int32, (128, 256), 0)
    dst = lax.broadcasted_iota(jnp.int32, (128, 256), 1)
    fold = ((src // 64 == dst // 128) & (lax.rem(src, 8) == lax.rem(dst, 8))).astype(BF16)

    def turn(corner, s):
        y = jnp.zeros((16, 128), jnp.int32)
        for r in range(8):
            y = jnp.where(lax.rem(row16, 8) == r, corner(r * 8 + s) - HALO, y)
        return lane16 - lax.rem(lane16, 8) + lax.rem(lane16 - y + BXY * 2, 8)

    @pl.loop(0, own_ref.shape[0])
    def _(s):
        index = turn(lambda k: anchor_ref[2, 0, k], s)
        parts = [(own_ref[s, 0], index), (own_ref[s, 1], index)]
        parts.append((below_ref[s], turn(lambda k: near_ref[0, 2, 0, k], s)))
        parts.append((above_ref[s], turn(lambda k: near_ref[1, 2, 0, k], s)))
        for i, (got, index) in enumerate(parts):
            got = got.astype(F32)
            got = jnp.concatenate(
                [jnp.take_along_axis(got[j : j + 8], index[j : j + 8], axis=1) for j in (0, 8)], axis=0
            )
            wide = jnp.concatenate([jnp.where(here, got[j : j + 1], 0.0) for j in range(16)], axis=0)
            out = jnp.dot(wide.astype(BF16), fold, preferred_element_type=F32)
            for q in range(2):
                for r in range(8):
                    for w in range(2):
                        tiles[i * 4 + q * 2 + w, r * 8 + s] = out[(q * 8 + r) * 8 : (q * 8 + r) * 8 + 8, w * 128 : w * 128 + 128]


def place_kernel(corner_ref, own_ref, below_ref, above_ref, brick, low_ref, high_ref, sides_ref, ends_ref, tiles, sides):
    anchor_ref, near_ref = corner_ref.at[0], corner_ref.at[pl.ds(1, 2)]
    for h in range(2):

        @pl.loop(0, BZ)
        def _(z):
            brick[h, z + HALO, 8 : 24 + BXY, :] = jnp.zeros((16 + BXY, 128), F32)

    sides[...] = jnp.zeros_like(sides)
    spread_tiles(anchor_ref, near_ref, own_ref, below_ref, above_ref, tiles)
    lane = lax.broadcasted_iota(jnp.int32, (8, 128), 1)

    def add(half, count, shift, k, oz, ox, oy):
        first = jnp.maximum(oy - HALO, 0) // 128
        rows = pl.ds(ox + 16 - HALO, 8)
        planes = pl.ds(oz + shift, count)
        for h in (first, first + 1):
            t = lane + (h * 128 - oy + HALO)
            inside = (t >= 0) & (t < 8)
            brick[h, planes, rows, :] += jnp.where(inside[None], tiles[4 * half : 4 * half + count, k], 0.0)

        @pl.when((oy < HALO) | (oy > BXY - HALO))
        def _():
            for w in range(count):
                z = oz + shift + w - HALO
                start = jnp.where(oy < HALO, z * 4, 64 + z * 4)
                base = start + jnp.where(oy < HALO, oy, oy - (BXY + HALO))
                u = pltpu.roll(tiles[4 * half + w, k], lax.rem(base - oy + HALO + 512, 8), 1)
                t = lane - base
                inside = (t >= 0) & (t < 8) & (lane >= start) & (lane < start + 4) & (z >= 0) & (z < BZ)
                sides[rows, :] += jnp.where(inside, u, 0.0)

    @pl.loop(0, corner_ref.shape[3])
    def _(k):
        add(0, 8, 0, k, anchor_ref[0, 0, k], anchor_ref[1, 0, k], anchor_ref[2, 0, k])

        @pl.when(near_ref[0, 0, 0, k] > BZ - HALO)
        def _():
            add(2, 4, HALO - BZ, k, near_ref[0, 0, 0, k], near_ref[0, 1, 0, k], near_ref[0, 2, 0, k])

        @pl.when(near_ref[1, 0, 0, k] < HALO)
        def _():
            add(3, 4, BZ, k, near_ref[1, 0, 0, k], near_ref[1, 1, 0, k], near_ref[1, 2, 0, k])

    for z in range(BZ):
        low_ref[z] = jnp.concatenate([brick[h, z + HALO, 8:16] for h in range(2)], axis=0).astype(BF16)
        high_ref[z] = jnp.concatenate([brick[h, z + HALO, 16 + BXY : 24 + BXY] for h in range(2)], axis=0).astype(BF16)
    one, two = sides[16 : 16 + BXY // 2, :], sides[16 + BXY // 2 : 16 + BXY, :]
    left = lax.broadcasted_iota(jnp.int32, one.shape, 1) < 64
    sides_ref[0] = jnp.where(left, one, pltpu.roll(two, 64, 1)).astype(BF16)
    sides_ref[1] = jnp.where(left, pltpu.roll(one, 64, 1), two).astype(BF16)
    ends_ref[0] = sides[0:16, :].astype(BF16)
    ends_ref[1] = sides[16 + BXY : 32 + BXY, :].astype(BF16)


def exchange_kernel(low_ref, high_ref, sides_ref, ends_ref, low_out, high_out, sides_out, low_in, high_in, sides_in, ends_in, send_sem, recv_sem):
    nr, nc = lax.axis_size("row"), lax.axis_size("col")
    r, c, d = lax.axis_index("row"), lax.axis_index("col"), lax.axis_index("depth")
    barrier = pltpu.get_barrier_semaphore()
    for i in (nr - 1, 0, 1):
        for j in (nc - 1, 0, 1):
            if i or j:
                to = (lax.rem(r + i, nr), lax.rem(c + j, nc), d)
                pl.semaphore_signal(barrier, inc=1, device_id=to, device_id_type=MESH)
    pl.semaphore_wait(barrier, 8)
    plan = [
        (0, nc - 1, sides_ref.at[0], sides_in.at[0]),
        (0, 1, sides_ref.at[1], sides_in.at[1]),
        (nr - 1, 0, low_ref, low_in),
        (1, 0, high_ref, high_in),
        (nr - 1, nc - 1, ends_ref.at[0], ends_in.at[0]),
        (nr - 1, 1, ends_ref.at[0], ends_in.at[1]),
        (1, nc - 1, ends_ref.at[1], ends_in.at[2]),
        (1, 1, ends_ref.at[1], ends_in.at[3]),
    ]
    copies = []
    for n, (i, j, src, dst) in enumerate(plan):
        copy = pltpu.make_async_remote_copy(
            src_ref=src, dst_ref=dst, send_sem=send_sem.at[n], recv_sem=recv_sem.at[n],
            device_id=(lax.rem(r + i, nr), lax.rem(c + j, nc), d), device_id_type=MESH,
        )
        copy.start()
        copies.append(copy)
    for copy in copies:
        copy.wait()
    low_out[...] = low_in[...]
    high_out[...] = high_in[...]
    right, left = sides_in[0].astype(F32), sides_in[1].astype(F32)
    lower = lax.broadcasted_iota(jnp.int32, right.shape, 1) < 64
    sides_out[0 : BXY // 2, :] = jnp.where(lower, right, pltpu.roll(left, 64, 1))
    sides_out[BXY // 2 : BXY, :] = jnp.where(lower, pltpu.roll(right, 64, 1), left)
    lower = lax.broadcasted_iota(jnp.int32, (16, 128), 1) < 64
    after = jnp.where(lower, ends_in[0].astype(F32), ends_in[1].astype(F32))
    before = jnp.where(lower, ends_in[2].astype(F32), ends_in[3].astype(F32))
    sides_out[0:8, :] += before[0:8]
    sides_out[BXY - 8 : BXY, :] += after[8:16]


def charge_kernel(brick, low_ref, high_ref, sides_ref, density_ref, density_out, charge_ref, full, sems):
    copies = [pltpu.make_async_copy(density_ref, density_out, sems.at[BZ])]
    copies[0].start()
    src = lax.broadcasted_iota(jnp.int32, (128, 256), 0)
    dst = lax.broadcasted_iota(jnp.int32, (128, 256), 1)
    sides = sides_ref[...].astype(BF16)
    at = jnp.where(dst < 4, 64 + dst, jnp.where(dst >= BXY - 4, dst - (BXY - 4), -BXY))
    for z in range(BZ):
        unfold = (src == at + z * 4).astype(BF16)
        out = jnp.dot(sides, unfold, preferred_element_type=F32)
        for h in range(2):
            lanes = slice(h * 128, h * 128 + 128)
            full[z, :, lanes] = out[:, lanes] + brick[h, z + HALO, 16 : 16 + BXY, :]
            full[z, 0:8, lanes] += high_ref[z].astype(F32)[8 * h : 8 * h + 8]
            full[z, BXY - 8 : BXY, lanes] += low_ref[z].astype(F32)[8 * h : 8 * h + 8]
        copies.append(pltpu.make_async_copy(full.at[z], charge_ref.at[z], sems.at[z]))
        copies[-1].start()
    for copy in copies:
        copy.wait()


def place(corner, own, below, above):
    vmem = pl.BlockSpec(memory_space=pltpu.VMEM)
    smem = pl.BlockSpec(memory_space=pltpu.SMEM)
    nk = corner.shape[3]
    faces = (jax.ShapeDtypeStruct((BZ, 16, 128), BF16),) * 2
    return pl.pallas_call(
        place_kernel,
        out_shape=(pltpu.VMEM((3, BZ + 2 * HALO, ROWS, 128), F32), *faces, jax.ShapeDtypeStruct((2, BXY // 2, 128), BF16), jax.ShapeDtypeStruct((2, 16, 128), BF16)),
        in_specs=[smem, vmem, vmem, vmem],
        out_specs=(vmem,) * 5,
        scratch_shapes=[pltpu.VMEM((16, nk, 8, 128), F32), pltpu.VMEM((ROWS, 128), F32)],
        compiler_params=pltpu.CompilerParams(vmem_limit_bytes=32 * 1024 * 1024),
        name="place",
    )(corner, own, below, above)


def finish(brick, low, high, sides, density):
    vmem = pl.BlockSpec(memory_space=pltpu.VMEM)
    hbm = pl.BlockSpec(memory_space=pl.ANY)
    return pl.pallas_call(
        charge_kernel,
        out_shape=(
            jax.ShapeDtypeStruct(density.shape, BF16),
            jax.ShapeDtypeStruct((BZ, BXY, BXY), F32),
        ),
        in_specs=[vmem, vmem, vmem, vmem, vmem],
        out_specs=(hbm, hbm),
        scratch_shapes=[pltpu.VMEM((BZ, BXY, BXY), F32), pltpu.SemaphoreType.DMA((BZ + 1,))],
        compiler_params=pltpu.CompilerParams(vmem_limit_bytes=32 * 1024 * 1024),
        name="charge",
    )(brick, low, high, sides, density)


def local(x_blocks, y_blocks, task_left, task_right, colloc_block, live, factors, cube_anchor):
    nr, nc = lax.axis_size("row"), lax.axis_size("col")
    anchor = cube_anchor[0, 0, 0].transpose(2, 1, 0)
    density, own, below, above, corner = product(
        x_blocks.reshape(NA * BLK, BLK),
        y_blocks.reshape(NB * BLK, BLK),
        task_left[0, 0, 0],
        task_right[0, 0, 0],
        colloc_block.reshape(-1),
        live.reshape(-1),
        factors.reshape(-1, BLK),
        anchor,
        nr, nc,
    )
    vmem = pl.BlockSpec(memory_space=pltpu.VMEM)
    dma = pltpu.SemaphoreType.DMA
    brick, low, high, sides, ends = place(corner, own, below, above)
    low, high, sides = pl.pallas_call(
        exchange_kernel,
        out_shape=(*(jax.ShapeDtypeStruct((BZ, 16, 128), BF16),) * 2, jax.ShapeDtypeStruct((BXY, 128), F32)),
        in_specs=[vmem, vmem, vmem, vmem],
        out_specs=(vmem, vmem, vmem),
        scratch_shapes=[
            pltpu.VMEM((BZ, 16, 128), BF16),
            pltpu.VMEM((BZ, 16, 128), BF16),
            pltpu.VMEM((2, BXY // 2, 128), BF16),
            pltpu.VMEM((4, 16, 128), BF16),
            dma((8,)),
            dma((8,)),
        ],
        compiler_params=pltpu.CompilerParams(collective_id=1, has_side_effects=True, vmem_limit_bytes=8 * 1024 * 1024),
        name="rim_exchange",
    )(low, high, sides, ends)
    density, charge = finish(brick, low, high, sides, density)
    return (density[None, None], charge)


def solution(mesh):
    placed = tuple(P("row", "col", "depth", *(None,) * n) for n in (4, 4, 3, 3, 2, 1, 6, 3))
    return jax.shard_map(
        local,
        mesh=mesh,
        in_specs=placed,
        out_specs=(P("row", "col", "depth", None, None), P("depth", "row", "col")),
        check_vma=False,
    )
```

```python
import functools

import jax
import jax.numpy as jnp
from jax import lax
from jax.experimental import pallas as pl
from jax.experimental.pallas import tpu as pltpu
from jax.sharding import PartitionSpec as P

BLK = 128
NA = 2
NB = 4
NC = 16
CUBE = 8
HALO = 4
BZ = 16
BXY = 256
CELLS = CUBE * CUBE * CUBE
SCALE = 0.0625
F32 = jnp.float32
BF16 = jnp.bfloat16
MESH = pl.DeviceIdType.MESH
NT = (((1,), (1,)), ((), ()))


def product_kernel(
    x_hbm, y_hbm, left_hbm, right_hbm, block_ref, live_ref, factor_hbm, anchor_ref,
    density_ref, own_ref, below_ref, above_ref, near_ref,
    x_ref, y_ref, left_ref, right_ref, factor_ref, near_anchor_ref,
    xg, yg, kmat, rhs, total, part_out, part_in, b0, b1, pairs, cubes, first_in, second_out,
    own_in, below_in, above_in,
    xr_send, xr_recv, xl_send, xl_recv, yr_send, yr_recv, yl_send, yl_recv, ys_send, ys_recv,
    part_send, part_recv, first_send, first_recv, second_send, second_recv, anchor_send, anchor_recv, load_sem,
):
    nr, nc, nd = lax.axis_size("row"), lax.axis_size("col"), lax.axis_size("depth")
    chips = nr // 2
    r, c, d = lax.axis_index("row"), lax.axis_index("col"), lax.axis_index("depth")
    core = lax.rem(r, 2)
    chip = r // 2
    sibling = r + 1 - 2 * core

    def up(i, j, n):
        return lax.rem(i + j, n)

    def send(src, dst, s, t, row, col, depth):
        copy = pltpu.make_async_remote_copy(
            src_ref=src, dst_ref=dst, send_sem=s, recv_sem=t, device_id=(row, col, depth), device_id_type=MESH
        )
        copy.start()
        return copy

    barrier = pltpu.get_barrier_semaphore()
    greeted = 0
    for j in range(1, nr):
        pl.semaphore_signal(barrier, inc=1, device_id=(up(r, j, nr), c, d), device_id_type=MESH)
        greeted += 1
    for j in range(nc):
        for k in (0, 1, nd - 1):
            if j or k:
                pl.semaphore_signal(barrier, inc=1, device_id=(r, up(c, j, nc), up(d, k, nd)), device_id_type=MESH)
                greeted += 1
    for k in range(2, nd - 1):
        pl.semaphore_signal(barrier, inc=1, device_id=(r, c, up(d, k, nd)), device_id_type=MESH)
        greeted += 1
    loads = [pltpu.make_async_copy(a, b, load_sem.at[i]) for i, (a, b) in enumerate(((x_hbm, x_ref), (y_hbm, y_ref), (left_hbm, left_ref), (right_hbm, right_ref), (factor_hbm, factor_ref)))]
    for load in loads:
        load.start()
    loads[0].wait()
    loads[1].wait()
    pl.semaphore_wait(barrier, greeted)

    copies = []
    right, left = up(c, 1, nc), up(c, nc - 1, nc)
    chip_r, chip_l = up(chip, 1, chips) * 2 + core, up(chip, chips - 1, chips) * 2 + core
    half = nc // 2

    def x_step(h):
        rows_r = pl.ds(0, 256) if h < half else pl.ds(0, 128)
        rows_l = pl.ds(0, 256) if h < half else pl.ds(128, 128)
        src_r, src_l = up(c, nc - (h - 1), nc), up(c, h - 1, nc)
        copies.append(
            send((x_ref if h == 1 else xg.at[src_r]).at[rows_r], xg.at[src_r, rows_r], xr_send.at[h - 1], xr_recv.at[h - 1], r, right, d)
        )
        copies.append(
            send((x_ref if h == 1 else xg.at[src_l]).at[rows_l], xg.at[src_l, rows_l], xl_send.at[h - 1], xl_recv.at[h - 1], r, left, d)
        )

    def x_wait(h):
        rows_r = pl.ds(0, 256) if h < half else pl.ds(0, 128)
        rows_l = pl.ds(0, 256) if h < half else pl.ds(128, 128)
        src_r, src_l = up(c, nc - h, nc), up(c, h, nc)
        pltpu.make_async_copy(xg.at[src_r, rows_r], xg.at[src_r, rows_r], xr_recv.at[h - 1]).wait()
        pltpu.make_async_copy(xg.at[src_l, rows_l], xg.at[src_l, rows_l], xl_recv.at[h - 1]).wait()

    def y_wait(slot, rows, sem):
        pltpu.make_async_copy(yg.at[slot, rows], yg.at[slot, rows], sem).wait()

    def y_share(q):
        slot = up(r, 2 * q, nr)
        copies.append(send(y_ref if q == 0 else yg.at[slot], yg.at[slot], ys_send.at[q], ys_recv.at[q], sibling, c, d))

    whole, lower, upper = pl.ds(0, 512), pl.ds(0, 256), pl.ds(256, 256)
    x_step(1)
    y_share(0)
    copies.append(send(y_ref, yg.at[r], yr_send.at[0], yr_recv.at[0], chip_r, c, d))
    copies.append(send(y_ref, yg.at[r], yl_send.at[0], yl_recv.at[0], chip_l, c, d))
    for i, k in enumerate((1, nd - 1)):
        copies.append(send(anchor_ref, near_anchor_ref.at[i], anchor_send.at[i], anchor_recv.at[i], r, c, up(d, k, nd)))

    loads[2].wait()
    loads[3].wait()
    npair = NA * NB
    task = left_ref[...] * NB + right_ref[...]
    counts = jnp.concatenate(
        [jnp.sum(jnp.where(task == p, 1.0, 0.0).astype(F32), axis=1) for p in range(npair)], axis=0
    )
    pick_out = (lax.broadcasted_iota(jnp.int32, (256, NC), 0) // 16 == lax.broadcasted_iota(jnp.int32, (256, NC), 1))
    spread = lax.dot_general(pick_out.astype(F32), counts, NT, preferred_element_type=F32)
    npanel = left_ref.shape[0]
    row64 = lax.broadcasted_iota(jnp.int32, (npair * npanel, npair * 16), 0)
    lane64 = lax.broadcasted_iota(jnp.int32, (npair * npanel, npair * 16), 1)
    same = lax.rem(lax.broadcasted_iota(jnp.int32, (256, 128), 0), 16) == lax.rem(
        lax.broadcasted_iota(jnp.int32, (256, 128), 1), 16
    )
    for k in range(npanel):
        pick_in = (row64 == (lane64 // 16) * npanel + k).astype(BF16)
        m = jnp.dot(spread.astype(BF16), pick_in, preferred_element_type=F32)
        m = jnp.where(same, m, 0.0).astype(BF16)
        kmat[k, :, 0:128] = m
        kmat[k, :, 128:256] = m

    pairs[...] = jnp.zeros_like(pairs)

    def basis(lo, hi):
        @pl.loop(lo, hi)
        def _(t):
            for w in range(2):
                k = t * 2 + w
                f = factor_ref[pl.ds(pl.multiple_of(k * 48, 16), 48), :].astype(F32)
                for e, out in ((0, b0), (1, b1)):
                    f0, f1, f2 = (f[24 * e + 8 * i : 24 * e + 8 * i + 8] for i in range(3))
                    for a in range(CUBE):
                        g = f0[a : a + 1] * f1
                        for b in range(0, CUBE, 2):
                            two = jnp.concatenate([g[b : b + 1] * f2, g[b + 1 : b + 2] * f2], axis=0)
                            out[t, a * 64 + b * 8 : a * 64 + b * 8 + 16, w * 128 : w * 128 + 128] = two.astype(BF16)

    def stage_panel(delta):
        for b in range(NB):
            xs = x_ref if delta == 0 else xg.at[up(c, delta, nc)]
            ys = y_ref if delta == 0 else yg.at[up(r, delta, nr)]
            p = jnp.dot(xs[...], ys[b * 128 : b * 128 + 128, :], preferred_element_type=F32)
            high = p.astype(BF16)
            low = (p - high.astype(F32)).astype(BF16)
            for a in range(NA):
                at = (a * NB + b) * 16
                for ch in range(8):
                    rows = slice(a * 128 + ch * 16, a * 128 + ch * 16 + 16)
                    rhs[at : at + 16, ch * 128 : ch * 128 + 128] = high[rows]
                    rhs[128 + at : 128 + at + 16, ch * 128 : ch * 128 + 128] = low[rows]

    def panel(delta):
        stage_panel(delta)
        k = lax.rem(r + c + delta, npanel)
        got = jnp.dot(kmat[k], rhs[...], preferred_element_type=F32)
        if delta == 0:
            total[...] = got
        else:
            total[...] += got

    nslot = factor_ref.shape[0] // 48
    quarter = nslot // 8

    panel(0)
    loads[4].wait()
    x_wait(1)
    x_step(2)
    y_wait(up(r, nr - 2, nr), whole, yr_recv.at[0])
    copies.append(
        send(yg.at[up(r, nr - 2, nr), lower], yg.at[up(r, nr - 2, nr), lower], yr_send.at[1], yr_recv.at[1], chip_r, c, d)
    )
    y_wait(up(r, 2, nr), whole, yl_recv.at[0])
    copies.append(send(yg.at[up(r, 2, nr), upper], yg.at[up(r, 2, nr), upper], yl_send.at[1], yl_recv.at[1], chip_l, c, d))
    y_share(chips - 1)
    y_share(1)
    basis(0, quarter)
    x_wait(2)
    x_step(3)
    y_wait(up(r, 4, nr), lower, yr_recv.at[1])
    y_wait(up(r, 4, nr), upper, yl_recv.at[1])
    y_share(2)
    panel(2)
    panel(nr - 2)
    x_wait(3)
    x_step(4)
    for q in range(chips):
        y_wait(lax.rem(sibling + 2 * q, nr), whole, ys_recv.at[q])
    for delta in (1, nr - 1, 3, nr - 3):
        panel(delta)
    x_wait(4)
    stage_panel(half)
    k = lax.rem(r + c + half, npanel)

    def last(dest):
        rows = pl.ds(pl.multiple_of(dest * 64, 64), 64)
        return total[rows, :] + jnp.dot(kmat[k, rows, :], rhs[...], preferred_element_type=F32)

    for j in (2, 1, 3):
        dest = up(d, j, nd)
        part_out[j - 1] = last(dest).astype(BF16)
        copies.append(send(part_out.at[j - 1], part_in.at[j - 1], part_send.at[j - 1], part_recv.at[j - 1], r, c, dest))
    summed = last(d)
    basis(quarter, 4 * quarter)
    for j in (1, 3, 2):
        pltpu.make_async_copy(part_in.at[j - 1], part_in.at[j - 1], part_recv.at[j - 1]).wait()
        summed = summed + part_in[j - 1].astype(F32)
    density = summed.astype(BF16)
    for o in range(NC // 4):
        for ch in range(8):
            density_ref[o, ch * 16 : ch * 16 + 16, :] = density[o * 16 : o * 16 + 16, ch * 128 : ch * 128 + 128]
    for i in range(4):
        for j in range(4):
            pairs[i * 4 + j, 0:128, 0:128] = density_ref[i]
            pairs[i * 4 + j, 128:256, 128:256] = density_ref[j]

    row16 = lax.broadcasted_iota(jnp.int32, (16, 256), 0)
    side = lax.broadcasted_iota(jnp.int32, (16, 256), 1) // 128
    for j in (2, 1, 3, 0):
        group = up(chip, j, chips)
        base = group * 8

        def two(i, acc):
            t = base + i
            which = block_ref[t * 2] * 4 + block_ref[t * 2 + 1]
            ones = jnp.where(
                row16 == i * 2 + side,
                jnp.where(side == 0, jnp.minimum(live_ref[t * 2], 1), jnp.minimum(live_ref[t * 2 + 1], 1)).astype(F32) * SCALE,
                0.0,
            ).astype(BF16)
            weight = pairs[which]
            new = []
            for q in range(4):
                rows = pl.ds(q * 128, 128)
                v = jnp.dot(b0[t, rows, :], weight, preferred_element_type=F32)
                v = (v * b1[t, rows, :].astype(F32)).astype(BF16)
                new.append(acc[q] + lax.dot_general(ones, v, NT, preferred_element_type=F32))
            return tuple(new)

        acc = lax.fori_loop(0, 8, two, tuple(jnp.zeros((16, 128), F32) for _ in range(4)), unroll=4)
        for q in range(4):
            cubes[j, q] = acc[q]
        for w in range(2):
            owner = group * 2 + w
            if j:
                copies.append(
                    send(cubes.at[j, :, pl.ds(8 * w, 8)], first_in.at[:, pl.ds(pl.multiple_of(r * 8, 8), 8)], first_send.at[2 * j + w], first_recv.at[r], owner, c, d)
                )
    mine = pl.ds(pl.multiple_of(core * 8, 8), 8)
    theirs = pl.ds(pl.multiple_of(8 - core * 8, 8), 8)
    here = pl.ds(pl.multiple_of(r * 8, 8), 8)
    copies.append(send(cubes.at[0, :, theirs], first_in.at[:, here], first_send.at[0], first_recv.at[r], sibling, c, d))
    first_in[:, here, :] = cubes[0, :, mine, :]
    for j in range(1, nr):
        src = up(r, j, nr)
        rows = first_in.at[:, pl.ds(pl.multiple_of(src * 8, 8), 8)]
        pltpu.make_async_copy(rows, rows, first_recv.at[src]).wait()

    for s in range(nc):
        got = [first_in[q, pl.ds(s, 8, stride=8), :] for q in range(4)]
        for h in range(2):
            second_out[s, h] = jnp.concatenate(got[2 * h : 2 * h + 2], axis=0).astype(BF16)
    for j in [*range(1, nc), 0]:
        s = up(c, j, nc)
        copies.append(send(second_out.at[s, 1], below_in.at[c], second_send.at[1, j], second_recv.at[1, c], r, s, up(d, 1, nd)))
        copies.append(send(second_out.at[s, 0], above_in.at[c], second_send.at[2, j], second_recv.at[2, c], r, s, up(d, nd - 1, nd)))
        if j:
            copies.append(send(second_out.at[s], own_in.at[c], second_send.at[0, j], second_recv.at[0, c], r, s, d))
    own_ref[c] = second_out[c]
    for j in range(nc):
        s = up(c, j, nc)
        if j:
            pltpu.make_async_copy(own_in.at[s], own_in.at[s], second_recv.at[0, s]).wait()
            own_ref[s] = own_in[s]
        pltpu.make_async_copy(below_in.at[s], below_in.at[s], second_recv.at[1, s]).wait()
        below_ref[s] = below_in[s]
        pltpu.make_async_copy(above_in.at[s], above_in.at[s], second_recv.at[2, s]).wait()
        above_ref[s] = above_in[s]
    for i in range(2):
        pltpu.make_async_copy(near_anchor_ref.at[i], near_anchor_ref.at[i], anchor_recv.at[i]).wait()
        near_ref[i + 1] = near_anchor_ref[i]
    near_ref[0] = anchor_ref[...]
    for copy in copies:
        copy.wait_send()


def product(x, y, left, right, block, live, factor, anchor, nr, nc):
    vmem = pl.BlockSpec(memory_space=pltpu.VMEM)
    smem = pl.BlockSpec(memory_space=pltpu.SMEM)
    hbm = pl.BlockSpec(memory_space=pl.ANY)
    dma = pltpu.SemaphoreType.DMA
    slots = block.shape[0]
    return pl.pallas_call(
        product_kernel,
        out_shape=(
            pltpu.VMEM((NC // 4, BLK, BLK), BF16),
            pltpu.VMEM((nc, 2, 16, 128), BF16),
            pltpu.VMEM((nc, 16, 128), BF16),
            pltpu.VMEM((nc, 16, 128), BF16),
            pltpu.VMEM((3, *anchor.shape), jnp.int32),
        ),
        in_specs=[hbm, hbm, hbm, hbm, smem, smem, hbm, vmem],
        out_specs=(vmem,) * 5,
        scratch_shapes=[
            pltpu.VMEM(x.shape, BF16),
            pltpu.VMEM(y.shape, BF16),
            pltpu.VMEM(left.shape, jnp.int32),
            pltpu.VMEM(right.shape, jnp.int32),
            pltpu.VMEM(factor.shape, BF16),
            pltpu.VMEM((2, *anchor.shape), jnp.int32),
            pltpu.VMEM((nc, 256, 128), BF16),
            pltpu.VMEM((nr, 512, 128), BF16),
            pltpu.VMEM((8, 256, 256), BF16),
            pltpu.VMEM((256, 1024), BF16),
            pltpu.VMEM((256, 1024), F32),
            pltpu.VMEM((3, 64, 1024), BF16),
            pltpu.VMEM((3, 64, 1024), BF16),
            pltpu.VMEM((slots // 2, CELLS, 256), BF16),
            pltpu.VMEM((slots // 2, CELLS, 256), BF16),
            pltpu.VMEM((16, 256, 256), BF16),
            pltpu.VMEM((4, 4, 16, 128), F32),
            pltpu.VMEM((4, nr * 8, 128), F32),
            pltpu.VMEM((nc, 2, 16, 128), BF16),
            pltpu.VMEM((nc, 2, 16, 128), BF16),
            pltpu.VMEM((nc, 16, 128), BF16),
            pltpu.VMEM((nc, 16, 128), BF16),
            dma((4,)), dma((4,)), dma((4,)), dma((4,)),
            dma((2,)), dma((2,)), dma((2,)), dma((2,)), dma((4,)), dma((4,)),
            dma((3,)), dma((3,)), dma((8,)), dma((8,)), dma((3, 8)), dma((3, 8)), dma((2,)), dma((2,)), dma((5,)),
        ],
        compiler_params=pltpu.CompilerParams(collective_id=0, has_side_effects=True, vmem_limit_bytes=56 * 1024 * 1024),
        name="product_and_cubes",
    )(x, y, left, right, block, live, factor, anchor)


ROWS = BXY + 32


def spread_tiles(anchor_ref, near_ref, own_ref, below_ref, above_ref, tiles):
    row16 = lax.broadcasted_iota(jnp.int32, (16, 128), 0)
    lane16 = lax.broadcasted_iota(jnp.int32, (16, 128), 1)
    lane = lax.broadcasted_iota(jnp.int32, (8, 128), 1)
    here = lax.rem(lane // 8, 8) == lax.broadcasted_iota(jnp.int32, (8, 128), 0)
    src = lax.broadcasted_iota(jnp.int32, (128, 256), 0)
    dst = lax.broadcasted_iota(jnp.int32, (128, 256), 1)
    fold = ((src // 64 == dst // 128) & (lax.rem(src, 8) == lax.rem(dst, 8))).astype(BF16)

    def turn(corner, s):
        y = jnp.zeros((16, 128), jnp.int32)
        for r in range(8):
            y = jnp.where(lax.rem(row16, 8) == r, corner(r * 8 + s) - HALO, y)
        return lane16 - lax.rem(lane16, 8) + lax.rem(lane16 - y + BXY * 2, 8)

    @pl.loop(0, own_ref.shape[0], unroll=8)
    def _(s):
        index = turn(lambda k: anchor_ref[2, 0, k], s)
        parts = [(own_ref[s, 0], index), (own_ref[s, 1], index)]
        parts.append((below_ref[s], turn(lambda k: near_ref[0, 2, 0, k], s)))
        parts.append((above_ref[s], turn(lambda k: near_ref[1, 2, 0, k], s)))
        for i, (got, index) in enumerate(parts):
            got = got.astype(F32)
            got = jnp.concatenate(
                [jnp.take_along_axis(got[j : j + 8], index[j : j + 8], axis=1) for j in (0, 8)], axis=0
            )
            wide = jnp.concatenate([jnp.where(here, got[j : j + 1], 0.0) for j in range(16)], axis=0)
            out = jnp.dot(wide.astype(BF16), fold, preferred_element_type=F32)
            for q in range(2):
                for r in range(8):
                    for w in range(2):
                        tiles[i * 4 + q * 2 + w, r * 8 + s] = out[(q * 8 + r) * 8 : (q * 8 + r) * 8 + 8, w * 128 : w * 128 + 128]


def place_kernel(corner_ref, own_ref, below_ref, above_ref, brick, low_ref, high_ref, sides_ref, ends_ref, tiles, sides):
    for h in range(2):

        @pl.loop(0, BZ)
        def _(z):
            brick[h, z + HALO, 8 : 24 + BXY, :] = jnp.zeros((16 + BXY, 128), F32)

    sides[...] = jnp.zeros_like(sides)
    spread_tiles(corner_ref.at[0], corner_ref.at[pl.ds(1, 2)], own_ref, below_ref, above_ref, tiles)
    lane = lax.broadcasted_iota(jnp.int32, (8, 128), 1)

    def add(half, count, start, k, ox, oy):
        first = jnp.maximum(oy - HALO, 0) // 128
        rows = pl.ds(ox + 16 - HALO, 8)
        planes = pl.ds(start, count)
        for h in (first, first + 1):
            t = lane + (h * 128 - oy + HALO)
            inside = (t >= 0) & (t < 8)
            brick[h, planes, rows, :] += jnp.where(inside[None], tiles[4 * half : 4 * half + count, k], 0.0)

    def add_rim(half, count, shift, k, oz, ox, oy):
        for w in range(count):
            z = oz + shift + w - HALO
            start = jnp.where(oy < HALO, z * 4, 64 + z * 4)
            base = start + jnp.where(oy < HALO, oy, oy - (BXY + HALO))
            u = pltpu.roll(tiles[4 * half + w, k], lax.rem(base - oy + HALO + 512, 8), 1)
            t = lane - base
            inside = (t >= 0) & (t < 8) & (lane >= start) & (lane < start + 4) & (z >= 0) & (z < BZ)
            sides[pl.ds(ox + 16 - HALO, 8), :] += jnp.where(inside, u, 0.0)

    def corner(i, k):
        return corner_ref[i, 0, 0, k], corner_ref[i, 1, 0, k], corner_ref[i, 2, 0, k]

    def is_rim(oy):
        return (oy < HALO) | (oy > BXY - HALO)

    nk = corner_ref.shape[3]

    @pl.loop(0, nk, unroll=4)
    def _(k):
        z, x, y = corner(0, k)
        add(0, 8, z, k, x, y)
        z, x, y = corner(1, k)
        add(2, 4, jnp.where(z > BZ - HALO, z + HALO - BZ, BZ + HALO), k, x, y)
        z, x, y = corner(2, k)
        add(3, 4, jnp.where(z < HALO, z + BZ, BZ + HALO), k, x, y)

    @pl.loop(0, nk)
    def _(k):
        y0, y1, y2 = corner_ref[0, 2, 0, k], corner_ref[1, 2, 0, k], corner_ref[2, 2, 0, k]

        @pl.when(is_rim(y0) | is_rim(y1) | is_rim(y2))
        def _():
            @pl.when(is_rim(y0))
            def _():
                add_rim(0, 8, 0, k, *corner(0, k))

            @pl.when(is_rim(y1))
            def _():
                add_rim(2, 4, HALO - BZ, k, *corner(1, k))

            @pl.when(is_rim(y2))
            def _():
                add_rim(3, 4, BZ, k, *corner(2, k))

    for z in range(BZ):
        low_ref[z] = jnp.concatenate([brick[h, z + HALO, 8:16] for h in range(2)], axis=0).astype(BF16)
        high_ref[z] = jnp.concatenate([brick[h, z + HALO, 16 + BXY : 24 + BXY] for h in range(2)], axis=0).astype(BF16)
    one, two = sides[16 : 16 + BXY // 2, :], sides[16 + BXY // 2 : 16 + BXY, :]
    left = lax.broadcasted_iota(jnp.int32, one.shape, 1) < 64
    sides_ref[0] = jnp.where(left, one, pltpu.roll(two, 64, 1)).astype(BF16)
    sides_ref[1] = jnp.where(left, pltpu.roll(one, 64, 1), two).astype(BF16)
    ends_ref[0] = sides[0:16, :].astype(BF16)
    ends_ref[1] = sides[16 + BXY : 32 + BXY, :].astype(BF16)


def exchange_kernel(low_ref, high_ref, sides_ref, ends_ref, low_out, high_out, sides_out, low_in, high_in, sides_in, ends_in, send_sem, recv_sem):
    nr, nc = lax.axis_size("row"), lax.axis_size("col")
    r, c, d = lax.axis_index("row"), lax.axis_index("col"), lax.axis_index("depth")
    barrier = pltpu.get_barrier_semaphore()
    for i in (nr - 1, 0, 1):
        for j in (nc - 1, 0, 1):
            if i or j:
                to = (lax.rem(r + i, nr), lax.rem(c + j, nc), d)
                pl.semaphore_signal(barrier, inc=1, device_id=to, device_id_type=MESH)
    pl.semaphore_wait(barrier, 8)
    plan = [
        (0, nc - 1, sides_ref.at[0], sides_in.at[0]),
        (0, 1, sides_ref.at[1], sides_in.at[1]),
        (nr - 1, 0, low_ref, low_in),
        (1, 0, high_ref, high_in),
        (nr - 1, nc - 1, ends_ref.at[0], ends_in.at[0]),
        (nr - 1, 1, ends_ref.at[0], ends_in.at[1]),
        (1, nc - 1, ends_ref.at[1], ends_in.at[2]),
        (1, 1, ends_ref.at[1], ends_in.at[3]),
    ]
    copies = []
    for n, (i, j, src, dst) in enumerate(plan):
        copy = pltpu.make_async_remote_copy(
            src_ref=src, dst_ref=dst, send_sem=send_sem.at[n], recv_sem=recv_sem.at[n],
            device_id=(lax.rem(r + i, nr), lax.rem(c + j, nc), d), device_id_type=MESH,
        )
        copy.start()
        copies.append(copy)
    for copy in copies:
        copy.wait()
    low_out[...] = low_in[...]
    high_out[...] = high_in[...]
    right, left = sides_in[0].astype(F32), sides_in[1].astype(F32)
    lower = lax.broadcasted_iota(jnp.int32, right.shape, 1) < 64
    sides_out[0 : BXY // 2, :] = jnp.where(lower, right, pltpu.roll(left, 64, 1))
    sides_out[BXY // 2 : BXY, :] = jnp.where(lower, pltpu.roll(right, 64, 1), left)
    lower = lax.broadcasted_iota(jnp.int32, (16, 128), 1) < 64
    after = jnp.where(lower, ends_in[0].astype(F32), ends_in[1].astype(F32))
    before = jnp.where(lower, ends_in[2].astype(F32), ends_in[3].astype(F32))
    sides_out[0:8, :] += before[0:8]
    sides_out[BXY - 8 : BXY, :] += after[8:16]


def charge_kernel(brick, low_ref, high_ref, sides_ref, density_ref, density_out, charge_ref, full, sems):
    copies = [pltpu.make_async_copy(density_ref, density_out, sems.at[BZ])]
    copies[0].start()
    src = lax.broadcasted_iota(jnp.int32, (128, 256), 0)
    dst = lax.broadcasted_iota(jnp.int32, (128, 256), 1)
    sides = sides_ref[...].astype(BF16)
    at = jnp.where(dst < 4, 64 + dst, jnp.where(dst >= BXY - 4, dst - (BXY - 4), -BXY))
    for z in range(BZ):
        unfold = (src == at + z * 4).astype(BF16)
        out = jnp.dot(sides, unfold, preferred_element_type=F32)
        for h in range(2):
            lanes = slice(h * 128, h * 128 + 128)
            full[z, :, lanes] = out[:, lanes] + brick[h, z + HALO, 16 : 16 + BXY, :]
            full[z, 0:8, lanes] += high_ref[z].astype(F32)[8 * h : 8 * h + 8]
            full[z, BXY - 8 : BXY, lanes] += low_ref[z].astype(F32)[8 * h : 8 * h + 8]
        copies.append(pltpu.make_async_copy(full.at[z], charge_ref.at[z], sems.at[z]))
        copies[-1].start()
    for copy in copies:
        copy.wait()


def place(corner, own, below, above):
    vmem = pl.BlockSpec(memory_space=pltpu.VMEM)
    smem = pl.BlockSpec(memory_space=pltpu.SMEM)
    nk = corner.shape[3]
    faces = (jax.ShapeDtypeStruct((BZ, 16, 128), BF16),) * 2
    return pl.pallas_call(
        place_kernel,
        out_shape=(pltpu.VMEM((3, BZ + 2 * HALO, ROWS, 128), F32), *faces, jax.ShapeDtypeStruct((2, BXY // 2, 128), BF16), jax.ShapeDtypeStruct((2, 16, 128), BF16)),
        in_specs=[smem, vmem, vmem, vmem],
        out_specs=(vmem,) * 5,
        scratch_shapes=[pltpu.VMEM((16, nk, 8, 128), F32), pltpu.VMEM((ROWS, 128), F32)],
        compiler_params=pltpu.CompilerParams(vmem_limit_bytes=32 * 1024 * 1024),
        name="place",
    )(corner, own, below, above)


def finish(brick, low, high, sides, density):
    vmem = pl.BlockSpec(memory_space=pltpu.VMEM)
    hbm = pl.BlockSpec(memory_space=pl.ANY)
    return pl.pallas_call(
        charge_kernel,
        out_shape=(
            jax.ShapeDtypeStruct(density.shape, BF16),
            jax.ShapeDtypeStruct((BZ, BXY, BXY), F32),
        ),
        in_specs=[vmem, vmem, vmem, vmem, vmem],
        out_specs=(hbm, hbm),
        scratch_shapes=[pltpu.VMEM((BZ, BXY, BXY), F32), pltpu.SemaphoreType.DMA((BZ + 1,))],
        compiler_params=pltpu.CompilerParams(vmem_limit_bytes=32 * 1024 * 1024),
        name="charge",
    )(brick, low, high, sides, density)


def local(x_blocks, y_blocks, task_left, task_right, colloc_block, live, factors, cube_anchor):
    nr, nc = lax.axis_size("row"), lax.axis_size("col")
    anchor = cube_anchor[0, 0, 0].transpose(2, 1, 0)
    density, own, below, above, corner = product(
        x_blocks.reshape(NA * BLK, BLK),
        y_blocks.reshape(NB * BLK, BLK),
        task_left[0, 0, 0],
        task_right[0, 0, 0],
        colloc_block.reshape(-1),
        live.reshape(-1),
        factors.reshape(-1, BLK),
        anchor,
        nr, nc,
    )
    vmem = pl.BlockSpec(memory_space=pltpu.VMEM)
    dma = pltpu.SemaphoreType.DMA
    brick, low, high, sides, ends = place(corner, own, below, above)
    low, high, sides = pl.pallas_call(
        exchange_kernel,
        out_shape=(*(jax.ShapeDtypeStruct((BZ, 16, 128), BF16),) * 2, jax.ShapeDtypeStruct((BXY, 128), F32)),
        in_specs=[vmem, vmem, vmem, vmem],
        out_specs=(vmem, vmem, vmem),
        scratch_shapes=[
            pltpu.VMEM((BZ, 16, 128), BF16),
            pltpu.VMEM((BZ, 16, 128), BF16),
            pltpu.VMEM((2, BXY // 2, 128), BF16),
            pltpu.VMEM((4, 16, 128), BF16),
            dma((8,)),
            dma((8,)),
        ],
        compiler_params=pltpu.CompilerParams(collective_id=1, has_side_effects=True, vmem_limit_bytes=8 * 1024 * 1024),
        name="rim_exchange",
    )(low, high, sides, ends)
    density, charge = finish(brick, low, high, sides, density)
    return (density[None, None], charge)


def solution(mesh):
    placed = tuple(P("row", "col", "depth", *(None,) * n) for n in (4, 4, 3, 3, 2, 1, 6, 3))
    return jax.shard_map(
        local,
        mesh=mesh,
        in_specs=placed,
        out_specs=(P("row", "col", "depth", None, None), P("depth", "row", "col")),
        check_vma=False,
    )
```

```python
import functools

import jax
import jax.numpy as jnp
from jax import lax
from jax.experimental import pallas as pl
from jax.experimental.pallas import tpu as pltpu
from jax.sharding import PartitionSpec as P

BLK = 128
NA = 2
NB = 4
NC = 16
CUBE = 8
HALO = 4
BZ = 16
BXY = 256
CELLS = CUBE * CUBE * CUBE
SCALE = 0.0625
F32 = jnp.float32
BF16 = jnp.bfloat16
MESH = pl.DeviceIdType.MESH
NT = (((1,), (1,)), ((), ()))


def product_kernel(
    x_hbm, y_hbm, left_hbm, right_hbm, block_ref, live_ref, factor_hbm, anchor_ref,
    density_ref, own_ref, below_ref, above_ref, near_ref,
    x_ref, y_ref, left_ref, right_ref, factor_ref, near_anchor_ref,
    xg, yg, kmat, rhs, total, part_out, part_in, b0, b1, pairs, cubes, first_in, second_out,
    own_in, below_in, above_in,
    xr_send, xr_recv, xl_send, xl_recv, yr_send, yr_recv, yl_send, yl_recv, ys_send, ys_recv,
    part_send, part_recv, first_send, first_recv, second_send, second_recv, anchor_send, anchor_recv, load_sem,
):
    nr, nc, nd = lax.axis_size("row"), lax.axis_size("col"), lax.axis_size("depth")
    chips = nr // 2
    r, c, d = lax.axis_index("row"), lax.axis_index("col"), lax.axis_index("depth")
    core = lax.rem(r, 2)
    chip = r // 2
    sibling = r + 1 - 2 * core

    def up(i, j, n):
        return lax.rem(i + j, n)

    def send(src, dst, s, t, row, col, depth):
        copy = pltpu.make_async_remote_copy(
            src_ref=src, dst_ref=dst, send_sem=s, recv_sem=t, device_id=(row, col, depth), device_id_type=MESH
        )
        copy.start()
        return copy

    barrier = pltpu.get_barrier_semaphore()
    greeted = 0
    for j in range(1, nr):
        pl.semaphore_signal(barrier, inc=1, device_id=(up(r, j, nr), c, d), device_id_type=MESH)
        greeted += 1
    for j in range(nc):
        for k in (0, 1, nd - 1):
            if j or k:
                pl.semaphore_signal(barrier, inc=1, device_id=(r, up(c, j, nc), up(d, k, nd)), device_id_type=MESH)
                greeted += 1
    for k in range(2, nd - 1):
        pl.semaphore_signal(barrier, inc=1, device_id=(r, c, up(d, k, nd)), device_id_type=MESH)
        greeted += 1
    loads = [pltpu.make_async_copy(a, b, load_sem.at[i]) for i, (a, b) in enumerate(((x_hbm, x_ref), (y_hbm, y_ref), (left_hbm, left_ref), (right_hbm, right_ref), (factor_hbm, factor_ref)))]
    for load in loads:
        load.start()
    loads[0].wait()
    loads[1].wait()
    pl.semaphore_wait(barrier, greeted)

    copies = []
    chip_r, chip_l = up(chip, 1, chips) * 2 + core, up(chip, chips - 1, chips) * 2 + core
    half = nc // 2

    def x_step(h):
        hop = min(h, 2)
        rows_r = pl.ds(0, 256) if h < half else pl.ds(0, 128)
        rows_l = pl.ds(0, 256) if h < half else pl.ds(128, 128)
        src_r, src_l = up(c, nc - (h - hop), nc), up(c, h - hop, nc)
        copies.append(
            send((x_ref if h == hop else xg.at[src_r]).at[rows_r], xg.at[src_r, rows_r], xr_send.at[h - 1], xr_recv.at[h - 1], r, up(c, hop, nc), d)
        )
        copies.append(
            send((x_ref if h == hop else xg.at[src_l]).at[rows_l], xg.at[src_l, rows_l], xl_send.at[h - 1], xl_recv.at[h - 1], r, up(c, nc - hop, nc), d)
        )

    def x_wait(h):
        rows_r = pl.ds(0, 256) if h < half else pl.ds(0, 128)
        rows_l = pl.ds(0, 256) if h < half else pl.ds(128, 128)
        src_r, src_l = up(c, nc - h, nc), up(c, h, nc)
        pltpu.make_async_copy(xg.at[src_r, rows_r], xg.at[src_r, rows_r], xr_recv.at[h - 1]).wait()
        pltpu.make_async_copy(xg.at[src_l, rows_l], xg.at[src_l, rows_l], xl_recv.at[h - 1]).wait()

    def y_wait(slot, rows, sem):
        pltpu.make_async_copy(yg.at[slot, rows], yg.at[slot, rows], sem).wait()

    def y_share(q):
        slot = up(r, 2 * q, nr)
        copies.append(send(y_ref if q == 0 else yg.at[slot], yg.at[slot], ys_send.at[q], ys_recv.at[q], sibling, c, d))

    whole = pl.ds(0, 512)
    x_step(1)
    copies.append(send(y_ref, yg.at[r], yr_send.at[0], yr_recv.at[0], chip_r, c, d))
    copies.append(send(y_ref, yg.at[r], yl_send.at[0], yl_recv.at[0], chip_l, c, d))
    x_step(2)
    copies.append(send(y_ref, yg.at[r], yr_send.at[1], yr_recv.at[1], up(r, 4, nr), c, d))
    y_share(0)
    for i, k in enumerate((1, nd - 1)):
        copies.append(send(anchor_ref, near_anchor_ref.at[i], anchor_send.at[i], anchor_recv.at[i], r, c, up(d, k, nd)))

    loads[2].wait()
    loads[3].wait()
    npair = NA * NB
    task = left_ref[...] * NB + right_ref[...]
    counts = jnp.concatenate(
        [jnp.sum(jnp.where(task == p, 1.0, 0.0).astype(F32), axis=1) for p in range(npair)], axis=0
    )
    pick_out = (lax.broadcasted_iota(jnp.int32, (256, NC), 0) // 16 == lax.broadcasted_iota(jnp.int32, (256, NC), 1))
    spread = lax.dot_general(pick_out.astype(F32), counts, NT, preferred_element_type=F32)
    npanel = left_ref.shape[0]
    row64 = lax.broadcasted_iota(jnp.int32, (npair * npanel, npair * 16), 0)
    lane64 = lax.broadcasted_iota(jnp.int32, (npair * npanel, npair * 16), 1)
    same = lax.rem(lax.broadcasted_iota(jnp.int32, (256, 128), 0), 16) == lax.rem(
        lax.broadcasted_iota(jnp.int32, (256, 128), 1), 16
    )
    for k in range(npanel):
        pick_in = (row64 == (lane64 // 16) * npanel + k).astype(BF16)
        m = jnp.dot(spread.astype(BF16), pick_in, preferred_element_type=F32)
        m = jnp.where(same, m, 0.0).astype(BF16)
        kmat[k, :, 0:128] = m
        kmat[k, :, 128:256] = m

    pairs[...] = jnp.zeros_like(pairs)

    def basis(lo, hi):
        @pl.loop(lo, hi)
        def _(t):
            for w in range(2):
                k = t * 2 + w
                f = factor_ref[pl.ds(pl.multiple_of(k * 48, 16), 48), :].astype(F32)
                for e, out in ((0, b0), (1, b1)):
                    f0, f1, f2 = (f[24 * e + 8 * i : 24 * e + 8 * i + 8] for i in range(3))
                    for a in range(CUBE):
                        g = f0[a : a + 1] * f1
                        for b in range(0, CUBE, 2):
                            two = jnp.concatenate([g[b : b + 1] * f2, g[b + 1 : b + 2] * f2], axis=0)
                            out[t, a * 64 + b * 8 : a * 64 + b * 8 + 16, w * 128 : w * 128 + 128] = two.astype(BF16)

    def stage_panel(delta):
        for b in range(NB):
            xs = x_ref if delta == 0 else xg.at[up(c, delta, nc)]
            ys = y_ref if delta == 0 else yg.at[up(r, delta, nr)]
            p = jnp.dot(xs[...], ys[b * 128 : b * 128 + 128, :], preferred_element_type=F32)
            high = p.astype(BF16)
            low = (p - high.astype(F32)).astype(BF16)
            for a in range(NA):
                at = (a * NB + b) * 16
                for ch in range(8):
                    rows = slice(a * 128 + ch * 16, a * 128 + ch * 16 + 16)
                    rhs[at : at + 16, ch * 128 : ch * 128 + 128] = high[rows]
                    rhs[128 + at : 128 + at + 16, ch * 128 : ch * 128 + 128] = low[rows]

    def panel(delta):
        stage_panel(delta)
        k = lax.rem(r + c + delta, npanel)
        got = jnp.dot(kmat[k], rhs[...], preferred_element_type=F32)
        if delta == 0:
            total[...] = got
        else:
            total[...] += got

    nslot = factor_ref.shape[0] // 48
    quarter = nslot // 8

    panel(0)
    loads[4].wait()
    x_wait(1)
    x_step(3)
    y_wait(up(r, nr - 2, nr), whole, yr_recv.at[0])
    y_wait(up(r, 2, nr), whole, yl_recv.at[0])
    y_share(chips - 1)
    y_share(1)
    basis(0, quarter)
    x_wait(2)
    x_step(4)
    y_wait(up(r, 4, nr), whole, yr_recv.at[1])
    y_share(2)
    panel(2)
    panel(nr - 2)
    x_wait(3)
    for q in range(chips):
        y_wait(lax.rem(sibling + 2 * q, nr), whole, ys_recv.at[q])
    for delta in (1, nr - 1, 3, nr - 3):
        panel(delta)
    x_wait(4)
    stage_panel(half)
    k = lax.rem(r + c + half, npanel)

    def last(dest):
        rows = pl.ds(pl.multiple_of(dest * 64, 64), 64)
        return total[rows, :] + jnp.dot(kmat[k, rows, :], rhs[...], preferred_element_type=F32)

    for j in (2, 1, 3):
        dest = up(d, j, nd)
        part_out[j - 1] = last(dest).astype(BF16)
        copies.append(send(part_out.at[j - 1], part_in.at[j - 1], part_send.at[j - 1], part_recv.at[j - 1], r, c, dest))
    summed = last(d)
    basis(quarter, 4 * quarter)
    for j in (1, 3, 2):
        pltpu.make_async_copy(part_in.at[j - 1], part_in.at[j - 1], part_recv.at[j - 1]).wait()
        summed = summed + part_in[j - 1].astype(F32)
    density = summed.astype(BF16)
    for o in range(NC // 4):
        for ch in range(8):
            density_ref[o, ch * 16 : ch * 16 + 16, :] = density[o * 16 : o * 16 + 16, ch * 128 : ch * 128 + 128]
    for i in range(4):
        for j in range(4):
            pairs[i * 4 + j, 0:128, 0:128] = density_ref[i]
            pairs[i * 4 + j, 128:256, 128:256] = density_ref[j]

    row16 = lax.broadcasted_iota(jnp.int32, (16, 256), 0)
    side = lax.broadcasted_iota(jnp.int32, (16, 256), 1) // 128
    for j in (2, 1, 3, 0):
        group = up(chip, j, chips)
        base = group * 8

        def two(i, acc):
            t = base + i
            which = block_ref[t * 2] * 4 + block_ref[t * 2 + 1]
            ones = jnp.where(
                row16 == i * 2 + side,
                jnp.where(side == 0, jnp.minimum(live_ref[t * 2], 1), jnp.minimum(live_ref[t * 2 + 1], 1)).astype(F32) * SCALE,
                0.0,
            ).astype(BF16)
            weight = pairs[which]
            new = []
            for q in range(4):
                rows = pl.ds(q * 128, 128)
                v = jnp.dot(b0[t, rows, :], weight, preferred_element_type=F32)
                v = (v * b1[t, rows, :].astype(F32)).astype(BF16)
                new.append(acc[q] + lax.dot_general(ones, v, NT, preferred_element_type=F32))
            return tuple(new)

        acc = lax.fori_loop(0, 8, two, tuple(jnp.zeros((16, 128), F32) for _ in range(4)), unroll=4)
        for q in range(4):
            cubes[j, q] = acc[q]
        for w in range(2):
            owner = group * 2 + w
            if j:
                copies.append(
                    send(cubes.at[j, :, pl.ds(8 * w, 8)], first_in.at[:, pl.ds(pl.multiple_of(r * 8, 8), 8)], first_send.at[2 * j + w], first_recv.at[r], owner, c, d)
                )
    mine = pl.ds(pl.multiple_of(core * 8, 8), 8)
    theirs = pl.ds(pl.multiple_of(8 - core * 8, 8), 8)
    here = pl.ds(pl.multiple_of(r * 8, 8), 8)
    copies.append(send(cubes.at[0, :, theirs], first_in.at[:, here], first_send.at[0], first_recv.at[r], sibling, c, d))
    first_in[:, here, :] = cubes[0, :, mine, :]
    for j in range(1, nr):
        src = up(r, j, nr)
        rows = first_in.at[:, pl.ds(pl.multiple_of(src * 8, 8), 8)]
        pltpu.make_async_copy(rows, rows, first_recv.at[src]).wait()

    for s in range(nc):
        got = [first_in[q, pl.ds(s, 8, stride=8), :] for q in range(4)]
        for h in range(2):
            second_out[s, h] = jnp.concatenate(got[2 * h : 2 * h + 2], axis=0).astype(BF16)
    for j in [*range(1, nc), 0]:
        s = up(c, j, nc)
        copies.append(send(second_out.at[s, 1], below_in.at[c], second_send.at[1, j], second_recv.at[1, c], r, s, up(d, 1, nd)))
        copies.append(send(second_out.at[s, 0], above_in.at[c], second_send.at[2, j], second_recv.at[2, c], r, s, up(d, nd - 1, nd)))
        if j:
            copies.append(send(second_out.at[s], own_in.at[c], second_send.at[0, j], second_recv.at[0, c], r, s, d))
    own_ref[c] = second_out[c]
    for j in range(nc):
        s = up(c, j, nc)
        if j:
            pltpu.make_async_copy(own_in.at[s], own_in.at[s], second_recv.at[0, s]).wait()
            own_ref[s] = own_in[s]
        pltpu.make_async_copy(below_in.at[s], below_in.at[s], second_recv.at[1, s]).wait()
        below_ref[s] = below_in[s]
        pltpu.make_async_copy(above_in.at[s], above_in.at[s], second_recv.at[2, s]).wait()
        above_ref[s] = above_in[s]
    for i in range(2):
        pltpu.make_async_copy(near_anchor_ref.at[i], near_anchor_ref.at[i], anchor_recv.at[i]).wait()
        near_ref[i + 1] = near_anchor_ref[i]
    near_ref[0] = anchor_ref[...]
    for copy in copies:
        copy.wait_send()


def product(x, y, left, right, block, live, factor, anchor, nr, nc):
    vmem = pl.BlockSpec(memory_space=pltpu.VMEM)
    smem = pl.BlockSpec(memory_space=pltpu.SMEM)
    hbm = pl.BlockSpec(memory_space=pl.ANY)
    dma = pltpu.SemaphoreType.DMA
    slots = block.shape[0]
    return pl.pallas_call(
        product_kernel,
        out_shape=(
            pltpu.VMEM((NC // 4, BLK, BLK), BF16),
            pltpu.VMEM((nc, 2, 16, 128), BF16),
            pltpu.VMEM((nc, 16, 128), BF16),
            pltpu.VMEM((nc, 16, 128), BF16),
            pltpu.VMEM((3, *anchor.shape), jnp.int32),
        ),
        in_specs=[hbm, hbm, hbm, hbm, smem, smem, hbm, vmem],
        out_specs=(vmem,) * 5,
        scratch_shapes=[
            pltpu.VMEM(x.shape, BF16),
            pltpu.VMEM(y.shape, BF16),
            pltpu.VMEM(left.shape, jnp.int32),
            pltpu.VMEM(right.shape, jnp.int32),
            pltpu.VMEM(factor.shape, BF16),
            pltpu.VMEM((2, *anchor.shape), jnp.int32),
            pltpu.VMEM((nc, 256, 128), BF16),
            pltpu.VMEM((nr, 512, 128), BF16),
            pltpu.VMEM((8, 256, 256), BF16),
            pltpu.VMEM((256, 1024), BF16),
            pltpu.VMEM((256, 1024), F32),
            pltpu.VMEM((3, 64, 1024), BF16),
            pltpu.VMEM((3, 64, 1024), BF16),
            pltpu.VMEM((slots // 2, CELLS, 256), BF16),
            pltpu.VMEM((slots // 2, CELLS, 256), BF16),
            pltpu.VMEM((16, 256, 256), BF16),
            pltpu.VMEM((4, 4, 16, 128), F32),
            pltpu.VMEM((4, nr * 8, 128), F32),
            pltpu.VMEM((nc, 2, 16, 128), BF16),
            pltpu.VMEM((nc, 2, 16, 128), BF16),
            pltpu.VMEM((nc, 16, 128), BF16),
            pltpu.VMEM((nc, 16, 128), BF16),
            dma((4,)), dma((4,)), dma((4,)), dma((4,)),
            dma((2,)), dma((2,)), dma((1,)), dma((1,)), dma((4,)), dma((4,)),
            dma((3,)), dma((3,)), dma((8,)), dma((8,)), dma((3, 8)), dma((3, 8)), dma((2,)), dma((2,)), dma((5,)),
        ],
        compiler_params=pltpu.CompilerParams(collective_id=0, has_side_effects=True, vmem_limit_bytes=56 * 1024 * 1024),
        name="product_and_cubes",
    )(x, y, left, right, block, live, factor, anchor)


ROWS = BXY + 32


def spread_tiles(anchor_ref, near_ref, own_ref, below_ref, above_ref, tiles):
    row16 = lax.broadcasted_iota(jnp.int32, (16, 128), 0)
    lane16 = lax.broadcasted_iota(jnp.int32, (16, 128), 1)
    lane = lax.broadcasted_iota(jnp.int32, (8, 128), 1)
    here = lax.rem(lane // 8, 8) == lax.broadcasted_iota(jnp.int32, (8, 128), 0)
    src = lax.broadcasted_iota(jnp.int32, (128, 256), 0)
    dst = lax.broadcasted_iota(jnp.int32, (128, 256), 1)
    fold = ((src // 64 == dst // 128) & (lax.rem(src, 8) == lax.rem(dst, 8))).astype(BF16)

    def turn(corner, s):
        y = jnp.zeros((16, 128), jnp.int32)
        for r in range(8):
            y = jnp.where(lax.rem(row16, 8) == r, corner(r * 8 + s) - HALO, y)
        return lane16 - lax.rem(lane16, 8) + lax.rem(lane16 - y + BXY * 2, 8)

    @pl.loop(0, own_ref.shape[0], unroll=8)
    def _(s):
        index = turn(lambda k: anchor_ref[2, 0, k], s)
        parts = [(own_ref[s, 0], index), (own_ref[s, 1], index)]
        parts.append((below_ref[s], turn(lambda k: near_ref[0, 2, 0, k], s)))
        parts.append((above_ref[s], turn(lambda k: near_ref[1, 2, 0, k], s)))
        for i, (got, index) in enumerate(parts):
            got = got.astype(F32)
            got = jnp.concatenate(
                [jnp.take_along_axis(got[j : j + 8], index[j : j + 8], axis=1) for j in (0, 8)], axis=0
            )
            wide = jnp.concatenate([jnp.where(here, got[j : j + 1], 0.0) for j in range(16)], axis=0)
            out = jnp.dot(wide.astype(BF16), fold, preferred_element_type=F32)
            for q in range(2):
                for r in range(8):
                    for w in range(2):
                        tiles[i * 4 + q * 2 + w, r * 8 + s] = out[(q * 8 + r) * 8 : (q * 8 + r) * 8 + 8, w * 128 : w * 128 + 128]


def place_kernel(corner_ref, own_ref, below_ref, above_ref, brick, low_ref, high_ref, sides_ref, ends_ref, tiles, sides):
    for h in range(2):

        @pl.loop(0, BZ)
        def _(z):
            brick[h, z + HALO, 8 : 24 + BXY, :] = jnp.zeros((16 + BXY, 128), F32)

    sides[...] = jnp.zeros_like(sides)
    spread_tiles(corner_ref.at[0], corner_ref.at[pl.ds(1, 2)], own_ref, below_ref, above_ref, tiles)
    lane = lax.broadcasted_iota(jnp.int32, (8, 128), 1)

    def add(half, count, start, k, ox, oy):
        first = jnp.maximum(oy - HALO, 0) // 128
        rows = pl.ds(ox + 16 - HALO, 8)
        planes = pl.ds(start, count)
        for h in (first, first + 1):
            t = lane + (h * 128 - oy + HALO)
            inside = (t >= 0) & (t < 8)
            brick[h, planes, rows, :] += jnp.where(inside[None], tiles[4 * half : 4 * half + count, k], 0.0)

    def add_rim(half, count, shift, k, oz, ox, oy):
        for w in range(count):
            z = oz + shift + w - HALO
            start = jnp.where(oy < HALO, z * 4, 64 + z * 4)
            base = start + jnp.where(oy < HALO, oy, oy - (BXY + HALO))
            u = pltpu.roll(tiles[4 * half + w, k], lax.rem(base - oy + HALO + 512, 8), 1)
            t = lane - base
            inside = (t >= 0) & (t < 8) & (lane >= start) & (lane < start + 4) & (z >= 0) & (z < BZ)
            sides[pl.ds(ox + 16 - HALO, 8), :] += jnp.where(inside, u, 0.0)

    def corner(i, k):
        return corner_ref[i, 0, 0, k], corner_ref[i, 1, 0, k], corner_ref[i, 2, 0, k]

    def is_rim(oy):
        return (oy < HALO) | (oy > BXY - HALO)

    nk = corner_ref.shape[3]

    @pl.loop(0, nk, unroll=4)
    def _(k):
        z, x, y = corner(0, k)
        add(0, 8, z, k, x, y)
        z, x, y = corner(1, k)
        add(2, 4, jnp.where(z > BZ - HALO, z + HALO - BZ, BZ + HALO), k, x, y)
        z, x, y = corner(2, k)
        add(3, 4, jnp.where(z < HALO, z + BZ, BZ + HALO), k, x, y)

    @pl.loop(0, nk)
    def _(k):
        y0, y1, y2 = corner_ref[0, 2, 0, k], corner_ref[1, 2, 0, k], corner_ref[2, 2, 0, k]

        @pl.when(is_rim(y0) | is_rim(y1) | is_rim(y2))
        def _():
            @pl.when(is_rim(y0))
            def _():
                add_rim(0, 8, 0, k, *corner(0, k))

            @pl.when(is_rim(y1))
            def _():
                add_rim(2, 4, HALO - BZ, k, *corner(1, k))

            @pl.when(is_rim(y2))
            def _():
                add_rim(3, 4, BZ, k, *corner(2, k))

    for z in range(BZ):
        low_ref[z] = jnp.concatenate([brick[h, z + HALO, 8:16] for h in range(2)], axis=0).astype(BF16)
        high_ref[z] = jnp.concatenate([brick[h, z + HALO, 16 + BXY : 24 + BXY] for h in range(2)], axis=0).astype(BF16)
    one, two = sides[16 : 16 + BXY // 2, :], sides[16 + BXY // 2 : 16 + BXY, :]
    left = lax.broadcasted_iota(jnp.int32, one.shape, 1) < 64
    sides_ref[0] = jnp.where(left, one, pltpu.roll(two, 64, 1)).astype(BF16)
    sides_ref[1] = jnp.where(left, pltpu.roll(one, 64, 1), two).astype(BF16)
    ends_ref[0] = sides[0:16, :].astype(BF16)
    ends_ref[1] = sides[16 + BXY : 32 + BXY, :].astype(BF16)


def exchange_kernel(low_ref, high_ref, sides_ref, ends_ref, low_out, high_out, sides_out, low_in, high_in, sides_in, ends_in, send_sem, recv_sem):
    nr, nc = lax.axis_size("row"), lax.axis_size("col")
    r, c, d = lax.axis_index("row"), lax.axis_index("col"), lax.axis_index("depth")
    barrier = pltpu.get_barrier_semaphore()
    for i in (nr - 1, 0, 1):
        for j in (nc - 1, 0, 1):
            if i or j:
                to = (lax.rem(r + i, nr), lax.rem(c + j, nc), d)
                pl.semaphore_signal(barrier, inc=1, device_id=to, device_id_type=MESH)
    pl.semaphore_wait(barrier, 8)
    plan = [
        (0, nc - 1, sides_ref.at[0], sides_in.at[0]),
        (0, 1, sides_ref.at[1], sides_in.at[1]),
        (nr - 1, 0, low_ref, low_in),
        (1, 0, high_ref, high_in),
        (nr - 1, nc - 1, ends_ref.at[0], ends_in.at[0]),
        (nr - 1, 1, ends_ref.at[0], ends_in.at[1]),
        (1, nc - 1, ends_ref.at[1], ends_in.at[2]),
        (1, 1, ends_ref.at[1], ends_in.at[3]),
    ]
    copies = []
    for n, (i, j, src, dst) in enumerate(plan):
        copy = pltpu.make_async_remote_copy(
            src_ref=src, dst_ref=dst, send_sem=send_sem.at[n], recv_sem=recv_sem.at[n],
            device_id=(lax.rem(r + i, nr), lax.rem(c + j, nc), d), device_id_type=MESH,
        )
        copy.start()
        copies.append(copy)
    for copy in copies:
        copy.wait()
    low_out[...] = low_in[...]
    high_out[...] = high_in[...]
    right, left = sides_in[0].astype(F32), sides_in[1].astype(F32)
    lower = lax.broadcasted_iota(jnp.int32, right.shape, 1) < 64
    sides_out[0 : BXY // 2, :] = jnp.where(lower, right, pltpu.roll(left, 64, 1))
    sides_out[BXY // 2 : BXY, :] = jnp.where(lower, pltpu.roll(right, 64, 1), left)
    lower = lax.broadcasted_iota(jnp.int32, (16, 128), 1) < 64
    after = jnp.where(lower, ends_in[0].astype(F32), ends_in[1].astype(F32))
    before = jnp.where(lower, ends_in[2].astype(F32), ends_in[3].astype(F32))
    sides_out[0:8, :] += before[0:8]
    sides_out[BXY - 8 : BXY, :] += after[8:16]


def charge_kernel(brick, low_ref, high_ref, sides_ref, density_ref, density_out, charge_ref, full, sems):
    copies = [pltpu.make_async_copy(density_ref, density_out, sems.at[BZ])]
    copies[0].start()
    src = lax.broadcasted_iota(jnp.int32, (128, 256), 0)
    dst = lax.broadcasted_iota(jnp.int32, (128, 256), 1)
    sides = sides_ref[...].astype(BF16)
    at = jnp.where(dst < 4, 64 + dst, jnp.where(dst >= BXY - 4, dst - (BXY - 4), -BXY))
    for z in range(BZ):
        unfold = (src == at + z * 4).astype(BF16)
        out = jnp.dot(sides, unfold, preferred_element_type=F32)
        for h in range(2):
            lanes = slice(h * 128, h * 128 + 128)
            full[z, :, lanes] = out[:, lanes] + brick[h, z + HALO, 16 : 16 + BXY, :]
            full[z, 0:8, lanes] += high_ref[z].astype(F32)[8 * h : 8 * h + 8]
            full[z, BXY - 8 : BXY, lanes] += low_ref[z].astype(F32)[8 * h : 8 * h + 8]
        copies.append(pltpu.make_async_copy(full.at[z], charge_ref.at[z], sems.at[z]))
        copies[-1].start()
    for copy in copies:
        copy.wait()


def place(corner, own, below, above):
    vmem = pl.BlockSpec(memory_space=pltpu.VMEM)
    smem = pl.BlockSpec(memory_space=pltpu.SMEM)
    nk = corner.shape[3]
    faces = (jax.ShapeDtypeStruct((BZ, 16, 128), BF16),) * 2
    return pl.pallas_call(
        place_kernel,
        out_shape=(pltpu.VMEM((3, BZ + 2 * HALO, ROWS, 128), F32), *faces, jax.ShapeDtypeStruct((2, BXY // 2, 128), BF16), jax.ShapeDtypeStruct((2, 16, 128), BF16)),
        in_specs=[smem, vmem, vmem, vmem],
        out_specs=(vmem,) * 5,
        scratch_shapes=[pltpu.VMEM((16, nk, 8, 128), F32), pltpu.VMEM((ROWS, 128), F32)],
        compiler_params=pltpu.CompilerParams(vmem_limit_bytes=32 * 1024 * 1024),
        name="place",
    )(corner, own, below, above)


def finish(brick, low, high, sides, density):
    vmem = pl.BlockSpec(memory_space=pltpu.VMEM)
    hbm = pl.BlockSpec(memory_space=pl.ANY)
    return pl.pallas_call(
        charge_kernel,
        out_shape=(
            jax.ShapeDtypeStruct(density.shape, BF16),
            jax.ShapeDtypeStruct((BZ, BXY, BXY), F32),
        ),
        in_specs=[vmem, vmem, vmem, vmem, vmem],
        out_specs=(hbm, hbm),
        scratch_shapes=[pltpu.VMEM((BZ, BXY, BXY), F32), pltpu.SemaphoreType.DMA((BZ + 1,))],
        compiler_params=pltpu.CompilerParams(vmem_limit_bytes=32 * 1024 * 1024),
        name="charge",
    )(brick, low, high, sides, density)


def local(x_blocks, y_blocks, task_left, task_right, colloc_block, live, factors, cube_anchor):
    nr, nc = lax.axis_size("row"), lax.axis_size("col")
    anchor = cube_anchor[0, 0, 0].transpose(2, 1, 0)
    density, own, below, above, corner = product(
        x_blocks.reshape(NA * BLK, BLK),
        y_blocks.reshape(NB * BLK, BLK),
        task_left[0, 0, 0],
        task_right[0, 0, 0],
        colloc_block.reshape(-1),
        live.reshape(-1),
        factors.reshape(-1, BLK),
        anchor,
        nr, nc,
    )
    vmem = pl.BlockSpec(memory_space=pltpu.VMEM)
    dma = pltpu.SemaphoreType.DMA
    brick, low, high, sides, ends = place(corner, own, below, above)
    low, high, sides = pl.pallas_call(
        exchange_kernel,
        out_shape=(*(jax.ShapeDtypeStruct((BZ, 16, 128), BF16),) * 2, jax.ShapeDtypeStruct((BXY, 128), F32)),
        in_specs=[vmem, vmem, vmem, vmem],
        out_specs=(vmem, vmem, vmem),
        scratch_shapes=[
            pltpu.VMEM((BZ, 16, 128), BF16),
            pltpu.VMEM((BZ, 16, 128), BF16),
            pltpu.VMEM((2, BXY // 2, 128), BF16),
            pltpu.VMEM((4, 16, 128), BF16),
            dma((8,)),
            dma((8,)),
        ],
        compiler_params=pltpu.CompilerParams(collective_id=1, has_side_effects=True, vmem_limit_bytes=8 * 1024 * 1024),
        name="rim_exchange",
    )(low, high, sides, ends)
    density, charge = finish(brick, low, high, sides, density)
    return (density[None, None], charge)


def solution(mesh):
    placed = tuple(P("row", "col", "depth", *(None,) * n) for n in (4, 4, 3, 3, 2, 1, 6, 3))
    return jax.shard_map(
        local,
        mesh=mesh,
        in_specs=placed,
        out_specs=(P("row", "col", "depth", None, None), P("depth", "row", "col")),
        check_vma=False,
    )
```

```python
import functools

import jax
import jax.numpy as jnp
from jax import lax
from jax.experimental import pallas as pl
from jax.experimental.pallas import tpu as pltpu
from jax.sharding import PartitionSpec as P

BLK = 128
NA = 2
NB = 4
NC = 16
CUBE = 8
HALO = 4
BZ = 16
BXY = 256
CELLS = CUBE * CUBE * CUBE
SCALE = 0.0625
F32 = jnp.float32
BF16 = jnp.bfloat16
MESH = pl.DeviceIdType.MESH
NT = (((1,), (1,)), ((), ()))


def product_kernel(
    x_hbm, y_hbm, left_hbm, right_hbm, block_ref, live_ref, factor_hbm, anchor_ref,
    density_ref, own_ref, below_ref, above_ref, near_ref,
    x_ref, y_ref, left_ref, right_ref, factor_ref, near_anchor_ref,
    xg, yg, kmat, rhs, total, part_out, part_in, b0, b1, pairs, cubes, first_in, second_out,
    own_in, below_in, above_in,
    xr_send, xr_recv, xl_send, xl_recv, yr_send, yr_recv, yl_send, yl_recv, ys_send, ys_recv,
    part_send, part_recv, first_send, first_recv, second_send, second_recv, anchor_send, anchor_recv, load_sem,
):
    nr, nc, nd = lax.axis_size("row"), lax.axis_size("col"), lax.axis_size("depth")
    chips = nr // 2
    r, c, d = lax.axis_index("row"), lax.axis_index("col"), lax.axis_index("depth")
    core = lax.rem(r, 2)
    chip = r // 2
    sibling = r + 1 - 2 * core

    def up(i, j, n):
        return lax.rem(i + j, n)

    def send(src, dst, s, t, row, col, depth):
        copy = pltpu.make_async_remote_copy(
            src_ref=src, dst_ref=dst, send_sem=s, recv_sem=t, device_id=(row, col, depth), device_id_type=MESH
        )
        copy.start()
        return copy

    barrier = pltpu.get_barrier_semaphore()
    greeted = 0
    for j in range(1, nr):
        pl.semaphore_signal(barrier, inc=1, device_id=(up(r, j, nr), c, d), device_id_type=MESH)
        greeted += 1
    for j in range(nc):
        for k in (0, 1, nd - 1):
            if j or k:
                pl.semaphore_signal(barrier, inc=1, device_id=(r, up(c, j, nc), up(d, k, nd)), device_id_type=MESH)
                greeted += 1
    for k in range(2, nd - 1):
        pl.semaphore_signal(barrier, inc=1, device_id=(r, c, up(d, k, nd)), device_id_type=MESH)
        greeted += 1
    loads = [pltpu.make_async_copy(a, b, load_sem.at[i]) for i, (a, b) in enumerate(((x_hbm, x_ref), (y_hbm, y_ref), (left_hbm, left_ref), (right_hbm, right_ref), (factor_hbm, factor_ref)))]
    for load in loads:
        load.start()
    loads[0].wait()
    loads[1].wait()
    pl.semaphore_wait(barrier, greeted)

    copies = []
    chip_r, chip_l = up(chip, 1, chips) * 2 + core, up(chip, chips - 1, chips) * 2 + core
    half = nc // 2

    def x_step(h):
        hop = min(h, 2)
        rows_r = pl.ds(0, 256) if h < half else pl.ds(0, 128)
        rows_l = pl.ds(0, 256) if h < half else pl.ds(128, 128)
        src_r, src_l = up(c, nc - (h - hop), nc), up(c, h - hop, nc)
        copies.append(
            send((x_ref if h == hop else xg.at[src_r]).at[rows_r], xg.at[src_r, rows_r], xr_send.at[h - 1], xr_recv.at[h - 1], r, up(c, hop, nc), d)
        )
        copies.append(
            send((x_ref if h == hop else xg.at[src_l]).at[rows_l], xg.at[src_l, rows_l], xl_send.at[h - 1], xl_recv.at[h - 1], r, up(c, nc - hop, nc), d)
        )

    def x_wait(h):
        rows_r = pl.ds(0, 256) if h < half else pl.ds(0, 128)
        rows_l = pl.ds(0, 256) if h < half else pl.ds(128, 128)
        src_r, src_l = up(c, nc - h, nc), up(c, h, nc)
        pltpu.make_async_copy(xg.at[src_r, rows_r], xg.at[src_r, rows_r], xr_recv.at[h - 1]).wait()
        pltpu.make_async_copy(xg.at[src_l, rows_l], xg.at[src_l, rows_l], xl_recv.at[h - 1]).wait()

    def y_wait(slot, rows, sem):
        pltpu.make_async_copy(yg.at[slot, rows], yg.at[slot, rows], sem).wait()

    def y_share(q):
        slot = up(r, 2 * q, nr)
        copies.append(send(y_ref if q == 0 else yg.at[slot], yg.at[slot], ys_send.at[q], ys_recv.at[q], sibling, c, d))

    whole = pl.ds(0, 512)
    x_step(1)
    copies.append(send(y_ref, yg.at[r], yr_send.at[0], yr_recv.at[0], chip_r, c, d))
    copies.append(send(y_ref, yg.at[r], yl_send.at[0], yl_recv.at[0], chip_l, c, d))
    x_step(2)
    copies.append(send(y_ref, yg.at[r], yr_send.at[1], yr_recv.at[1], up(r, 4, nr), c, d))
    y_share(0)
    for i, k in enumerate((1, nd - 1)):
        copies.append(send(anchor_ref, near_anchor_ref.at[i], anchor_send.at[i], anchor_recv.at[i], r, c, up(d, k, nd)))

    loads[2].wait()
    loads[3].wait()
    npair = NA * NB
    task = left_ref[...] * NB + right_ref[...]
    counts = jnp.concatenate(
        [jnp.sum(jnp.where(task == p, 1.0, 0.0).astype(F32), axis=1) for p in range(npair)], axis=0
    )
    pick_out = (lax.broadcasted_iota(jnp.int32, (256, NC), 0) // 16 == lax.broadcasted_iota(jnp.int32, (256, NC), 1))
    spread = lax.dot_general(pick_out.astype(F32), counts, NT, preferred_element_type=F32)
    npanel = left_ref.shape[0]
    row64 = lax.broadcasted_iota(jnp.int32, (npair * npanel, npair * 16), 0)
    lane64 = lax.broadcasted_iota(jnp.int32, (npair * npanel, npair * 16), 1)
    same = lax.rem(lax.broadcasted_iota(jnp.int32, (256, 128), 0), 16) == lax.rem(
        lax.broadcasted_iota(jnp.int32, (256, 128), 1), 16
    )
    for k in range(npanel):
        pick_in = (row64 == (lane64 // 16) * npanel + k).astype(BF16)
        m = jnp.dot(spread.astype(BF16), pick_in, preferred_element_type=F32)
        m = jnp.where(same, m, 0.0).astype(BF16)
        kmat[k, :, 0:128] = m
        kmat[k, :, 128:256] = m

    pairs[...] = jnp.zeros_like(pairs)

    def basis(lo, hi):
        @pl.loop(lo, hi)
        def _(t):
            for w in range(2):
                k = t * 2 + w
                f = factor_ref[pl.ds(pl.multiple_of(k * 48, 16), 48), :].astype(F32)
                for e, out in ((0, b0), (1, b1)):
                    f0, f1, f2 = (f[24 * e + 8 * i : 24 * e + 8 * i + 8] for i in range(3))
                    for a in range(CUBE):
                        g = f0[a : a + 1] * f1
                        for b in range(0, CUBE, 2):
                            two = jnp.concatenate([g[b : b + 1] * f2, g[b + 1 : b + 2] * f2], axis=0)
                            out[t, a * 64 + b * 8 : a * 64 + b * 8 + 16, w * 128 : w * 128 + 128] = two.astype(BF16)

    def stage_panel(delta):
        for b in range(NB):
            xs = x_ref if delta == 0 else xg.at[up(c, delta, nc)]
            ys = y_ref if delta == 0 else yg.at[up(r, delta, nr)]
            p = jnp.dot(xs[...], ys[b * 128 : b * 128 + 128, :], preferred_element_type=F32)
            high = p.astype(BF16)
            low = (p - high.astype(F32)).astype(BF16)
            for a in range(NA):
                at = (a * NB + b) * 16
                for ch in range(8):
                    rows = slice(a * 128 + ch * 16, a * 128 + ch * 16 + 16)
                    rhs[at : at + 16, ch * 128 : ch * 128 + 128] = high[rows]
                    rhs[128 + at : 128 + at + 16, ch * 128 : ch * 128 + 128] = low[rows]

    def panel(delta):
        stage_panel(delta)
        k = lax.rem(r + c + delta, npanel)
        got = jnp.dot(kmat[k], rhs[...], preferred_element_type=F32)
        if delta == 0:
            total[...] = got
        else:
            total[...] += got

    nslot = factor_ref.shape[0] // 48
    quarter = nslot // 8

    panel(0)
    loads[4].wait()
    x_wait(1)
    x_step(3)
    y_wait(up(r, nr - 2, nr), whole, yr_recv.at[0])
    y_wait(up(r, 2, nr), whole, yl_recv.at[0])
    y_share(chips - 1)
    y_share(1)
    basis(0, quarter)
    x_wait(2)
    x_step(4)
    y_wait(up(r, 4, nr), whole, yr_recv.at[1])
    y_share(2)
    panel(2)
    panel(nr - 2)
    for q in (0, 1, chips - 1):
        y_wait(lax.rem(sibling + 2 * q, nr), whole, ys_recv.at[q])
    panel(1)
    panel(nr - 1)
    x_wait(3)
    y_wait(lax.rem(sibling + 4, nr), whole, ys_recv.at[2])
    panel(3)
    panel(nr - 3)
    x_wait(4)
    stage_panel(half)
    k = lax.rem(r + c + half, npanel)

    def last(dest):
        rows = pl.ds(pl.multiple_of(dest * 64, 64), 64)
        return total[rows, :] + jnp.dot(kmat[k, rows, :], rhs[...], preferred_element_type=F32)

    for j in (2, 1, 3):
        dest = up(d, j, nd)
        part_out[j - 1] = last(dest).astype(BF16)
        copies.append(send(part_out.at[j - 1], part_in.at[j - 1], part_send.at[j - 1], part_recv.at[j - 1], r, c, dest))
    summed = last(d)
    basis(quarter, 4 * quarter)
    for j in (1, 3, 2):
        pltpu.make_async_copy(part_in.at[j - 1], part_in.at[j - 1], part_recv.at[j - 1]).wait()
        summed = summed + part_in[j - 1].astype(F32)
    density = summed.astype(BF16)
    for o in range(NC // 4):
        for ch in range(8):
            density_ref[o, ch * 16 : ch * 16 + 16, :] = density[o * 16 : o * 16 + 16, ch * 128 : ch * 128 + 128]
    for i in range(4):
        for j in range(4):
            pairs[i * 4 + j, 0:128, 0:128] = density_ref[i]
            pairs[i * 4 + j, 128:256, 128:256] = density_ref[j]

    row16 = lax.broadcasted_iota(jnp.int32, (16, 256), 0)
    side = lax.broadcasted_iota(jnp.int32, (16, 256), 1) // 128
    for j in (2, 1, 3, 0):
        group = up(chip, j, chips)
        base = group * 8

        def two(i, acc):
            t = base + i
            which = block_ref[t * 2] * 4 + block_ref[t * 2 + 1]
            ones = jnp.where(
                row16 == i * 2 + side,
                jnp.where(side == 0, jnp.minimum(live_ref[t * 2], 1), jnp.minimum(live_ref[t * 2 + 1], 1)).astype(F32) * SCALE,
                0.0,
            ).astype(BF16)
            weight = pairs[which]
            new = []
            for q in range(4):
                rows = pl.ds(q * 128, 128)
                v = jnp.dot(b0[t, rows, :], weight, preferred_element_type=F32)
                v = (v * b1[t, rows, :].astype(F32)).astype(BF16)
                new.append(acc[q] + lax.dot_general(ones, v, NT, preferred_element_type=F32))
            return tuple(new)

        acc = lax.fori_loop(0, 8, two, tuple(jnp.zeros((16, 128), F32) for _ in range(4)), unroll=4)
        for q in range(4):
            cubes[j, q] = acc[q]
        for w in range(2):
            owner = group * 2 + w
            if j:
                copies.append(
                    send(cubes.at[j, :, pl.ds(8 * w, 8)], first_in.at[:, pl.ds(pl.multiple_of(r * 8, 8), 8)], first_send.at[2 * j + w], first_recv.at[r], owner, c, d)
                )
    mine = pl.ds(pl.multiple_of(core * 8, 8), 8)
    theirs = pl.ds(pl.multiple_of(8 - core * 8, 8), 8)
    here = pl.ds(pl.multiple_of(r * 8, 8), 8)
    copies.append(send(cubes.at[0, :, theirs], first_in.at[:, here], first_send.at[0], first_recv.at[r], sibling, c, d))
    first_in[:, here, :] = cubes[0, :, mine, :]
    for j in range(1, nr):
        src = up(r, j, nr)
        rows = first_in.at[:, pl.ds(pl.multiple_of(src * 8, 8), 8)]
        pltpu.make_async_copy(rows, rows, first_recv.at[src]).wait()

    for s in range(nc):
        got = [first_in[q, pl.ds(s, 8, stride=8), :] for q in range(4)]
        for h in range(2):
            second_out[s, h] = jnp.concatenate(got[2 * h : 2 * h + 2], axis=0).astype(BF16)
    for j in (4, 3, 5, 2, 6, 1, 7, 0):
        s = up(c, j, nc)
        copies.append(send(second_out.at[s, 1], below_in.at[c], second_send.at[1, j], second_recv.at[1, c], r, s, up(d, 1, nd)))
        copies.append(send(second_out.at[s, 0], above_in.at[c], second_send.at[2, j], second_recv.at[2, c], r, s, up(d, nd - 1, nd)))
        if j:
            copies.append(send(second_out.at[s], own_in.at[c], second_send.at[0, j], second_recv.at[0, c], r, s, d))
    own_ref[c] = second_out[c]
    for j in range(nc):
        s = up(c, j, nc)
        if j:
            pltpu.make_async_copy(own_in.at[s], own_in.at[s], second_recv.at[0, s]).wait()
            own_ref[s] = own_in[s]
        pltpu.make_async_copy(below_in.at[s], below_in.at[s], second_recv.at[1, s]).wait()
        below_ref[s] = below_in[s]
        pltpu.make_async_copy(above_in.at[s], above_in.at[s], second_recv.at[2, s]).wait()
        above_ref[s] = above_in[s]
    for i in range(2):
        pltpu.make_async_copy(near_anchor_ref.at[i], near_anchor_ref.at[i], anchor_recv.at[i]).wait()
        near_ref[i + 1] = near_anchor_ref[i]
    near_ref[0] = anchor_ref[...]
    for copy in copies:
        copy.wait_send()


def product(x, y, left, right, block, live, factor, anchor, nr, nc):
    vmem = pl.BlockSpec(memory_space=pltpu.VMEM)
    smem = pl.BlockSpec(memory_space=pltpu.SMEM)
    hbm = pl.BlockSpec(memory_space=pl.ANY)
    dma = pltpu.SemaphoreType.DMA
    slots = block.shape[0]
    return pl.pallas_call(
        product_kernel,
        out_shape=(
            pltpu.VMEM((NC // 4, BLK, BLK), BF16),
            pltpu.VMEM((nc, 2, 16, 128), BF16),
            pltpu.VMEM((nc, 16, 128), BF16),
            pltpu.VMEM((nc, 16, 128), BF16),
            pltpu.VMEM((3, *anchor.shape), jnp.int32),
        ),
        in_specs=[hbm, hbm, hbm, hbm, smem, smem, hbm, vmem],
        out_specs=(vmem,) * 5,
        scratch_shapes=[
            pltpu.VMEM(x.shape, BF16),
            pltpu.VMEM(y.shape, BF16),
            pltpu.VMEM(left.shape, jnp.int32),
            pltpu.VMEM(right.shape, jnp.int32),
            pltpu.VMEM(factor.shape, BF16),
            pltpu.VMEM((2, *anchor.shape), jnp.int32),
            pltpu.VMEM((nc, 256, 128), BF16),
            pltpu.VMEM((nr, 512, 128), BF16),
            pltpu.VMEM((8, 256, 256), BF16),
            pltpu.VMEM((256, 1024), BF16),
            pltpu.VMEM((256, 1024), F32),
            pltpu.VMEM((3, 64, 1024), BF16),
            pltpu.VMEM((3, 64, 1024), BF16),
            pltpu.VMEM((slots // 2, CELLS, 256), BF16),
            pltpu.VMEM((slots // 2, CELLS, 256), BF16),
            pltpu.VMEM((16, 256, 256), BF16),
            pltpu.VMEM((4, 4, 16, 128), F32),
            pltpu.VMEM((4, nr * 8, 128), F32),
            pltpu.VMEM((nc, 2, 16, 128), BF16),
            pltpu.VMEM((nc, 2, 16, 128), BF16),
            pltpu.VMEM((nc, 16, 128), BF16),
            pltpu.VMEM((nc, 16, 128), BF16),
            dma((4,)), dma((4,)), dma((4,)), dma((4,)),
            dma((2,)), dma((2,)), dma((1,)), dma((1,)), dma((4,)), dma((4,)),
            dma((3,)), dma((3,)), dma((8,)), dma((8,)), dma((3, 8)), dma((3, 8)), dma((2,)), dma((2,)), dma((5,)),
        ],
        compiler_params=pltpu.CompilerParams(collective_id=0, has_side_effects=True, vmem_limit_bytes=56 * 1024 * 1024),
        name="product_and_cubes",
    )(x, y, left, right, block, live, factor, anchor)


ROWS = BXY + 32


def spread_tiles(anchor_ref, near_ref, own_ref, below_ref, above_ref, tiles):
    row16 = lax.broadcasted_iota(jnp.int32, (16, 128), 0)
    lane16 = lax.broadcasted_iota(jnp.int32, (16, 128), 1)
    lane = lax.broadcasted_iota(jnp.int32, (8, 128), 1)
    here = lax.rem(lane // 8, 8) == lax.broadcasted_iota(jnp.int32, (8, 128), 0)
    src = lax.broadcasted_iota(jnp.int32, (128, 256), 0)
    dst = lax.broadcasted_iota(jnp.int32, (128, 256), 1)
    fold = ((src // 64 == dst // 128) & (lax.rem(src, 8) == lax.rem(dst, 8))).astype(BF16)

    def turn(corner, s):
        y = jnp.zeros((16, 128), jnp.int32)
        for r in range(8):
            y = jnp.where(lax.rem(row16, 8) == r, corner(r * 8 + s) - HALO, y)
        return lane16 - lax.rem(lane16, 8) + lax.rem(lane16 - y + BXY * 2, 8)

    @pl.loop(0, own_ref.shape[0], unroll=8)
    def _(s):
        index = turn(lambda k: anchor_ref[2, 0, k], s)
        parts = [(own_ref[s, 0], index), (own_ref[s, 1], index)]
        parts.append((below_ref[s], turn(lambda k: near_ref[0, 2, 0, k], s)))
        parts.append((above_ref[s], turn(lambda k: near_ref[1, 2, 0, k], s)))
        for i, (got, index) in enumerate(parts):
            got = got.astype(F32)
            got = jnp.concatenate(
                [jnp.take_along_axis(got[j : j + 8], index[j : j + 8], axis=1) for j in (0, 8)], axis=0
            )
            wide = jnp.concatenate([jnp.where(here, got[j : j + 1], 0.0) for j in range(16)], axis=0)
            out = jnp.dot(wide.astype(BF16), fold, preferred_element_type=F32)
            for q in range(2):
                for r in range(8):
                    for w in range(2):
                        tiles[i * 4 + q * 2 + w, r * 8 + s] = out[(q * 8 + r) * 8 : (q * 8 + r) * 8 + 8, w * 128 : w * 128 + 128]


def place_kernel(corner_ref, own_ref, below_ref, above_ref, brick, low_ref, high_ref, sides_ref, ends_ref, tiles, sides):
    for h in range(2):

        @pl.loop(0, BZ)
        def _(z):
            brick[h, z + HALO, 8 : 24 + BXY, :] = jnp.zeros((16 + BXY, 128), F32)

    sides[...] = jnp.zeros_like(sides)
    spread_tiles(corner_ref.at[0], corner_ref.at[pl.ds(1, 2)], own_ref, below_ref, above_ref, tiles)
    lane = lax.broadcasted_iota(jnp.int32, (8, 128), 1)

    def add(half, count, start, k, ox, oy):
        first = jnp.maximum(oy - HALO, 0) // 128
        rows = pl.ds(ox + 16 - HALO, 8)
        planes = pl.ds(start, count)
        for h in (first, first + 1):
            t = lane + (h * 128 - oy + HALO)
            inside = (t >= 0) & (t < 8)
            brick[h, planes, rows, :] += jnp.where(inside[None], tiles[4 * half : 4 * half + count, k], 0.0)

    def add_rim(half, count, shift, k, oz, ox, oy):
        for w in range(count):
            z = oz + shift + w - HALO
            start = jnp.where(oy < HALO, z * 4, 64 + z * 4)
            base = start + jnp.where(oy < HALO, oy, oy - (BXY + HALO))
            u = pltpu.roll(tiles[4 * half + w, k], lax.rem(base - oy + HALO + 512, 8), 1)
            t = lane - base
            inside = (t >= 0) & (t < 8) & (lane >= start) & (lane < start + 4) & (z >= 0) & (z < BZ)
            sides[pl.ds(ox + 16 - HALO, 8), :] += jnp.where(inside, u, 0.0)

    def corner(i, k):
        return corner_ref[i, 0, 0, k], corner_ref[i, 1, 0, k], corner_ref[i, 2, 0, k]

    def is_rim(oy):
        return (oy < HALO) | (oy > BXY - HALO)

    nk = corner_ref.shape[3]

    @pl.loop(0, nk, unroll=4)
    def _(k):
        z, x, y = corner(0, k)
        add(0, 8, z, k, x, y)
        z, x, y = corner(1, k)
        add(2, 4, jnp.where(z > BZ - HALO, z + HALO - BZ, BZ + HALO), k, x, y)
        z, x, y = corner(2, k)
        add(3, 4, jnp.where(z < HALO, z + BZ, BZ + HALO), k, x, y)

    @pl.loop(0, nk)
    def _(k):
        y0, y1, y2 = corner_ref[0, 2, 0, k], corner_ref[1, 2, 0, k], corner_ref[2, 2, 0, k]

        @pl.when(is_rim(y0) | is_rim(y1) | is_rim(y2))
        def _():
            @pl.when(is_rim(y0))
            def _():
                add_rim(0, 8, 0, k, *corner(0, k))

            @pl.when(is_rim(y1))
            def _():
                add_rim(2, 4, HALO - BZ, k, *corner(1, k))

            @pl.when(is_rim(y2))
            def _():
                add_rim(3, 4, BZ, k, *corner(2, k))

    for z in range(BZ):
        low_ref[z] = jnp.concatenate([brick[h, z + HALO, 8:16] for h in range(2)], axis=0).astype(BF16)
        high_ref[z] = jnp.concatenate([brick[h, z + HALO, 16 + BXY : 24 + BXY] for h in range(2)], axis=0).astype(BF16)
    one, two = sides[16 : 16 + BXY // 2, :], sides[16 + BXY // 2 : 16 + BXY, :]
    left = lax.broadcasted_iota(jnp.int32, one.shape, 1) < 64
    sides_ref[0] = jnp.where(left, one, pltpu.roll(two, 64, 1)).astype(BF16)
    sides_ref[1] = jnp.where(left, pltpu.roll(one, 64, 1), two).astype(BF16)
    ends_ref[0] = sides[0:16, :].astype(BF16)
    ends_ref[1] = sides[16 + BXY : 32 + BXY, :].astype(BF16)


def exchange_kernel(low_ref, high_ref, sides_ref, ends_ref, low_out, high_out, sides_out, low_in, high_in, sides_in, ends_in, send_sem, recv_sem):
    nr, nc = lax.axis_size("row"), lax.axis_size("col")
    r, c, d = lax.axis_index("row"), lax.axis_index("col"), lax.axis_index("depth")
    barrier = pltpu.get_barrier_semaphore()
    for i in (nr - 1, 0, 1):
        for j in (nc - 1, 0, 1):
            if i or j:
                to = (lax.rem(r + i, nr), lax.rem(c + j, nc), d)
                pl.semaphore_signal(barrier, inc=1, device_id=to, device_id_type=MESH)
    pl.semaphore_wait(barrier, 8)
    plan = [
        (0, nc - 1, sides_ref.at[0], sides_in.at[0]),
        (0, 1, sides_ref.at[1], sides_in.at[1]),
        (nr - 1, 0, low_ref, low_in),
        (1, 0, high_ref, high_in),
        (nr - 1, nc - 1, ends_ref.at[0], ends_in.at[0]),
        (nr - 1, 1, ends_ref.at[0], ends_in.at[1]),
        (1, nc - 1, ends_ref.at[1], ends_in.at[2]),
        (1, 1, ends_ref.at[1], ends_in.at[3]),
    ]
    copies = []
    for n, (i, j, src, dst) in enumerate(plan):
        copy = pltpu.make_async_remote_copy(
            src_ref=src, dst_ref=dst, send_sem=send_sem.at[n], recv_sem=recv_sem.at[n],
            device_id=(lax.rem(r + i, nr), lax.rem(c + j, nc), d), device_id_type=MESH,
        )
        copy.start()
        copies.append(copy)
    for copy in copies:
        copy.wait()
    low_out[...] = low_in[...]
    high_out[...] = high_in[...]
    right, left = sides_in[0].astype(F32), sides_in[1].astype(F32)
    lower = lax.broadcasted_iota(jnp.int32, right.shape, 1) < 64
    sides_out[0 : BXY // 2, :] = jnp.where(lower, right, pltpu.roll(left, 64, 1))
    sides_out[BXY // 2 : BXY, :] = jnp.where(lower, pltpu.roll(right, 64, 1), left)
    lower = lax.broadcasted_iota(jnp.int32, (16, 128), 1) < 64
    after = jnp.where(lower, ends_in[0].astype(F32), ends_in[1].astype(F32))
    before = jnp.where(lower, ends_in[2].astype(F32), ends_in[3].astype(F32))
    sides_out[0:8, :] += before[0:8]
    sides_out[BXY - 8 : BXY, :] += after[8:16]


def charge_kernel(brick, low_ref, high_ref, sides_ref, density_ref, density_out, charge_ref, full, sems):
    copies = [pltpu.make_async_copy(density_ref, density_out, sems.at[BZ])]
    copies[0].start()
    src = lax.broadcasted_iota(jnp.int32, (128, 256), 0)
    dst = lax.broadcasted_iota(jnp.int32, (128, 256), 1)
    sides = sides_ref[...].astype(BF16)
    at = jnp.where(dst < 4, 64 + dst, jnp.where(dst >= BXY - 4, dst - (BXY - 4), -BXY))
    for z in range(BZ):
        unfold = (src == at + z * 4).astype(BF16)
        out = jnp.dot(sides, unfold, preferred_element_type=F32)
        for h in range(2):
            lanes = slice(h * 128, h * 128 + 128)
            full[z, :, lanes] = out[:, lanes] + brick[h, z + HALO, 16 : 16 + BXY, :]
            full[z, 0:8, lanes] += high_ref[z].astype(F32)[8 * h : 8 * h + 8]
            full[z, BXY - 8 : BXY, lanes] += low_ref[z].astype(F32)[8 * h : 8 * h + 8]
        copies.append(pltpu.make_async_copy(full.at[z], charge_ref.at[z], sems.at[z]))
        copies[-1].start()
    for copy in copies:
        copy.wait()


def place(corner, own, below, above):
    vmem = pl.BlockSpec(memory_space=pltpu.VMEM)
    smem = pl.BlockSpec(memory_space=pltpu.SMEM)
    nk = corner.shape[3]
    faces = (jax.ShapeDtypeStruct((BZ, 16, 128), BF16),) * 2
    return pl.pallas_call(
        place_kernel,
        out_shape=(pltpu.VMEM((3, BZ + 2 * HALO, ROWS, 128), F32), *faces, jax.ShapeDtypeStruct((2, BXY // 2, 128), BF16), jax.ShapeDtypeStruct((2, 16, 128), BF16)),
        in_specs=[smem, vmem, vmem, vmem],
        out_specs=(vmem,) * 5,
        scratch_shapes=[pltpu.VMEM((16, nk, 8, 128), F32), pltpu.VMEM((ROWS, 128), F32)],
        compiler_params=pltpu.CompilerParams(vmem_limit_bytes=32 * 1024 * 1024),
        name="place",
    )(corner, own, below, above)


def finish(brick, low, high, sides, density):
    vmem = pl.BlockSpec(memory_space=pltpu.VMEM)
    hbm = pl.BlockSpec(memory_space=pl.ANY)
    return pl.pallas_call(
        charge_kernel,
        out_shape=(
            jax.ShapeDtypeStruct(density.shape, BF16),
            jax.ShapeDtypeStruct((BZ, BXY, BXY), F32),
        ),
        in_specs=[vmem, vmem, vmem, vmem, vmem],
        out_specs=(hbm, hbm),
        scratch_shapes=[pltpu.VMEM((BZ, BXY, BXY), F32), pltpu.SemaphoreType.DMA((BZ + 1,))],
        compiler_params=pltpu.CompilerParams(vmem_limit_bytes=32 * 1024 * 1024),
        name="charge",
    )(brick, low, high, sides, density)


def local(x_blocks, y_blocks, task_left, task_right, colloc_block, live, factors, cube_anchor):
    nr, nc = lax.axis_size("row"), lax.axis_size("col")
    anchor = cube_anchor[0, 0, 0].transpose(2, 1, 0)
    density, own, below, above, corner = product(
        x_blocks.reshape(NA * BLK, BLK),
        y_blocks.reshape(NB * BLK, BLK),
        task_left[0, 0, 0],
        task_right[0, 0, 0],
        colloc_block.reshape(-1),
        live.reshape(-1),
        factors.reshape(-1, BLK),
        anchor,
        nr, nc,
    )
    vmem = pl.BlockSpec(memory_space=pltpu.VMEM)
    dma = pltpu.SemaphoreType.DMA
    brick, low, high, sides, ends = place(corner, own, below, above)
    low, high, sides = pl.pallas_call(
        exchange_kernel,
        out_shape=(*(jax.ShapeDtypeStruct((BZ, 16, 128), BF16),) * 2, jax.ShapeDtypeStruct((BXY, 128), F32)),
        in_specs=[vmem, vmem, vmem, vmem],
        out_specs=(vmem, vmem, vmem),
        scratch_shapes=[
            pltpu.VMEM((BZ, 16, 128), BF16),
            pltpu.VMEM((BZ, 16, 128), BF16),
            pltpu.VMEM((2, BXY // 2, 128), BF16),
            pltpu.VMEM((4, 16, 128), BF16),
            dma((8,)),
            dma((8,)),
        ],
        compiler_params=pltpu.CompilerParams(collective_id=1, has_side_effects=True, vmem_limit_bytes=8 * 1024 * 1024),
        name="rim_exchange",
    )(low, high, sides, ends)
    density, charge = finish(brick, low, high, sides, density)
    return (density[None, None], charge)


def solution(mesh):
    placed = tuple(P("row", "col", "depth", *(None,) * n) for n in (4, 4, 3, 3, 2, 1, 6, 3))
    return jax.shard_map(
        local,
        mesh=mesh,
        in_specs=placed,
        out_specs=(P("row", "col", "depth", None, None), P("depth", "row", "col")),
        check_vma=False,
    )
```
